32 devices in a mesh: grp: 2 (over y), atoms: 4 (over z), feat: 2 (over x), rep: 2 (over core).
Axes of the slice: x: 2, y: 2, z: 4, core: 2. Of those that a mesh axis runs over, the one named last changes fastest.
Arguments:
- atom_coords: bfloat16 [4, 2048, 3, 3072], P(('grp', 'rep'), None, None, 'atoms'), parts along dimension 0, may hold values from -9 to 9
- atom_pairs: int32 [2, 1024], P(None, 'feat'), may hold values from 0 to 3071, as said below
- traj_ids: int32 [4, 2048], P(('grp', 'rep')), parts along dimension 0, may hold values from 0 to 7, never falling along the last dimension, each value on 1 to 512 neighbouring positions
Outputs:
- corr_inst: float32 [2048, 1024], P(('grp', 'atoms', 'rep'), 'feat'), parts along dimension 0
- corr_lag: float32 [2048, 1024], P(('grp', 'atoms', 'rep'), 'feat'), parts along dimension 0
- projections: float32 [4, 2048, 1024], P(('grp', 'rep'), 'atoms', 'feat'), parts along dimension 0
The draws below stay inside these ranges and needn't reach their ends.
There are 2 independent parts, one for each index of `grp`. The reference program is written for one: setup_inputs(seed, part) draws one part's arguments, and reference() takes and returns one part's arrays. A program takes and returns all parts, laid end to end along the dimension named above; an argument that names none is the same for every part. Nothing has to cross between parts.
Inputs may be any that keep to these rules, and one draw needn't show every extreme that they name: `atom_pairs`: the two atoms of a feature differ. `traj_ids`: trajectory numbers never fall along a replica stream; some trajectory holds exactly 512 frames.
All inputs are finite; a program needn't handle non-finite values.
Results may differ from the reference program's by a relative error of at most 0.0003.
Values may be sent and summed in bfloat16 or wider, within the bound.
No kernel may reach another device: no remote copies, remote signals or barrier semaphores. Data moves between devices by JAX's collectives and lax.ppermute only.
A program may use at most 128 MiB of HBM per device.

```python
import math
import jax
import jax.numpy as jnp
import numpy as np
from jax import lax

ATOMS = 3072
FEATS = 1024
LAG = 10
TRAJS = 8
REPLICAS = 2
FRAMES = 2048


def draw_atom_coords(key, part):
    keys = jax.random.split(key, 10)
    base = jax.random.uniform(keys[0], (1, 1, 3, ATOMS), jnp.float32, -5.0, 5.0)
    times = jnp.arange(FRAMES, dtype=jnp.float32).reshape(1, FRAMES, 1, 1)
    envelope = 0.5 + times / FRAMES
    periods = jnp.exp(jax.random.uniform(keys[1], (3,), jnp.float32, math.log(40.0), math.log(400.0)))
    amplitudes = jax.random.uniform(keys[2], (3, 1, 1, 3, ATOMS), jnp.float32, 0.05, 0.35)
    phases = jax.random.uniform(keys[3], (3, REPLICAS, 1, 3, ATOMS), jnp.float32, -math.pi, math.pi)
    motion = jnp.zeros((REPLICAS, FRAMES, 3, ATOMS), jnp.float32)
    for mode in range(3):
        motion = motion + amplitudes[mode] * jnp.sin(2.0 * math.pi * times / periods[mode] + phases[mode])
    own_periods = jnp.exp(jax.random.uniform(keys[7], (1, 1, 3, ATOMS), jnp.float32, math.log(40.0), math.log(400.0)))
    own_amps = jnp.exp(jax.random.uniform(keys[8], (1, 1, 3, ATOMS), jnp.float32, math.log(0.3), math.log(0.8)))
    own_phases = jax.random.uniform(keys[9], (REPLICAS, 1, 3, ATOMS), jnp.float32, -math.pi, math.pi)
    own_motion = own_amps * jnp.sin(2.0 * math.pi * times / own_periods + own_phases)
    spread = jnp.exp(jax.random.uniform(keys[4], (1, 1, 1, ATOMS), jnp.float32, math.log(0.05), math.log(0.3)))
    noise = jax.random.truncated_normal(keys[6], -3.0, 3.0, (REPLICAS, FRAMES, 3, ATOMS), jnp.float32) * spread
    return (base + envelope * motion + own_motion + noise).astype(jnp.bfloat16)


def draw_atom_pairs(key, part):
    keys = jax.random.split(key, 2)
    first = jax.random.randint(keys[0], (FEATS,), 0, ATOMS, jnp.int32)
    first = first.at[0].set(ATOMS - 1).at[1].set(0)
    offset = jax.random.randint(keys[1], (FEATS,), 1, ATOMS, jnp.int32)
    second = (first + offset) % ATOMS
    return jnp.stack([first, second]).astype(jnp.int32)


def split_up(amount, total, most, skew):
    weights = [(1 << 20) // math.isqrt(rank ** skew) + 1 for rank in range(2, amount + 1)]
    surplus, counts = total - most - (amount - 1), [1] * (amount - 1)
    while surplus > 0:
        movable = [i for i in range(amount - 1) if counts[i] < most]
        whole, budget = sum([weights[i] for i in movable]), surplus
        for i in movable:
            extra = min(most - counts[i], max(1, budget * weights[i] // whole), surplus)
            counts[i] = counts[i] + extra
            surplus = surplus - extra
    return np.array([most] + counts)


def ragged(own_key, amount, total, most, skew):
    if amount == 2:
        one = jax.random.randint(own_key, (), max(1, total - most), min(most, total - 1) + 1)
        return jnp.stack([one, total - one])
    tallies = jnp.asarray(split_up(amount, total, most, skew), jnp.int32)
    twos = (amount - 1) // 2
    source_of, taker = tallies[1:1 + 2 * twos:2], tallies[2:2 + 2 * twos:2]
    margin = jnp.minimum(source_of - 1, most - taker)
    shifted = jax.random.randint(jax.random.fold_in(own_key, 1), (twos,), 0, 1 << 20) % (margin + 1)
    tallies = tallies.at[1:1 + 2 * twos:2].set(source_of - shifted).at[2:2 + 2 * twos:2].set(taker + shifted)
    return tallies[jax.random.permutation(jax.random.fold_in(own_key, 2), amount)]


def setup_inputs(seed: int = 0, part: int = 0) -> dict:
    arg_keys = jax.random.split(jax.random.key(seed), 4)
    own_keys = jax.random.split(jax.random.fold_in(arg_keys[3], part), 4)
    return {
        "atom_coords": draw_atom_coords(jax.random.fold_in(jax.random.fold_in(arg_keys[3], part), 71), part),
        "atom_pairs": draw_atom_pairs(jax.random.fold_in(arg_keys[3], 71), part),
        "traj_ids": jax.vmap(lambda own: jnp.searchsorted(jnp.cumsum(ragged(own, TRAJS, FRAMES, FRAMES // 4, 1)), jnp.arange(FRAMES), side="right"))(jax.random.split(own_keys[2], REPLICAS)).reshape((REPLICAS, FRAMES)).astype(jnp.int32),
    }


def featurize(positions, pairs):
    first = jnp.take(positions, pairs[0], axis=2)
    second = jnp.take(positions, pairs[1], axis=2)
    delta = first - second
    return jnp.sqrt(lax.optimization_barrier(jnp.sum(delta * delta, axis=1)) + 0.01)

def cross_moment(left, right):
    return lax.dot_general(left, right, (((0,), (0,)), ((), ())), precision=lax.Precision.HIGHEST, preferred_element_type=jnp.float32)

def reference(atom_coords, atom_pairs, traj_ids):
    padding = jnp.full((LAG,), -1, jnp.int32)
    present_list = []
    future_list = []
    valid_list = []
    for replica in range(REPLICAS):
        positions = atom_coords[replica].astype(jnp.float32)
        current = featurize(positions, atom_pairs)
        future = jnp.concatenate([current[LAG:], jnp.zeros((LAG, FEATS), jnp.float32)], 0)
        ids = jnp.concatenate([traj_ids[replica].astype(jnp.int32), padding])
        valid = (ids[:FRAMES] == ids[LAG:]).astype(jnp.float32)[:, None]
        present_list.append(current)
        future_list.append(future)
        valid_list.append(valid)
    count = jnp.float32(0.0)
    total_now = jnp.zeros((FEATS,), jnp.float32)
    total_next = jnp.zeros((FEATS,), jnp.float32)
    for replica in range(REPLICAS):
        count = count + jnp.sum(valid_list[replica])
        total_now = total_now + lax.optimization_barrier(jnp.sum(valid_list[replica] * present_list[replica], 0))
        total_next = total_next + lax.optimization_barrier(jnp.sum(valid_list[replica] * future_list[replica], 0))
    mean_now = total_now / count
    mean_next = total_next / count
    moment_inst = jnp.zeros((FEATS, FEATS), jnp.float32)
    moment_lag = jnp.zeros((FEATS, FEATS), jnp.float32)
    spread_now = jnp.zeros((FEATS,), jnp.float32)
    spread_next = jnp.zeros((FEATS,), jnp.float32)
    centered_list = []
    for replica in range(REPLICAS):
        centered = present_list[replica] - mean_now
        future_centered = future_list[replica] - mean_next
        valid = valid_list[replica]
        moment_inst = moment_inst + cross_moment(centered, valid * centered)
        moment_lag = moment_lag + cross_moment(centered, valid * future_centered)
        spread_now = spread_now + lax.optimization_barrier(jnp.sum(valid * centered * centered, 0))
        spread_next = spread_next + lax.optimization_barrier(jnp.sum(valid * future_centered * future_centered, 0))
        centered_list.append(centered)
    scale_now = 1.0 / jnp.sqrt(spread_now / count + 1e-05)
    scale_next = 1.0 / jnp.sqrt(spread_next / count + 1e-05)
    corr_inst = moment_inst / count * scale_now[:, None] * scale_now[None, :]
    corr_lag = moment_lag / count * scale_now[:, None] * scale_next[None, :]
    projections = jnp.stack([centered * scale_now for centered in centered_list])
    return (corr_inst, corr_lag, projections)
```

```python
import functools

import jax
import jax.numpy as jnp
from jax import lax
from jax.experimental import pallas as pl
from jax.experimental.pallas import tpu as pltpu
from jax.sharding import PartitionSpec as P

LAG = 10
HALO = 16
CHUNK = 64
VMEM_LIMIT = 48 * 1024 * 1024
F32 = jnp.float32
BF16 = jnp.bfloat16


def rotated(block, axis, shift):
    size = lax.axis_size(axis)
    return lax.ppermute(block, axis, [(i, (i + shift) % size) for i in range(size)])


def passed_down(block, axis):
    return lax.ppermute(block, axis, [(i + 1, i) for i in range(lax.axis_size(axis) - 1)])


def params():
    return pltpu.CompilerParams(vmem_limit_bytes=VMEM_LIMIT)


def pick_kernel(groups, cap, place_ref, *refs):
    del place_ref
    blocks, rank_ref, outs = refs[:groups], refs[groups], refs[groups + 1 :]
    width = blocks[0].shape[2]
    slots = lax.broadcasted_iota(jnp.int32, (width, cap), 1)
    chosen = (rank_ref[...] == slots).astype(F32).astype(BF16)
    half = CHUNK // 2
    for block, out in zip(blocks, outs):
        rows = block[...].reshape(3 * CHUNK, width)
        picked = jnp.dot(rows, chosen, preferred_element_type=F32).astype(BF16)
        picked = picked.reshape(3, CHUNK, cap)
        out[:, :, 0:cap] = picked[:, :half, :]
        out[:, :, cap : 2 * cap] = picked[:, half:, :]


def pick(coords, rank, cap, place, chunk, groups, sides):
    frames = coords.shape[1] // groups
    per_group = frames // CHUNK

    def at(shift):
        def index(step, where):
            there = lax.rem(where[0] + shift, groups)
            return (0, there * per_group + chunk * sides + where[1], 0)

        return index

    width = coords.shape[2]
    shape = jax.ShapeDtypeStruct((3, CHUNK // 2, 2 * cap), BF16)
    return pl.pallas_call(
        functools.partial(pick_kernel, groups, cap),
        grid_spec=pltpu.PrefetchScalarGridSpec(
            num_scalar_prefetch=1,
            grid=(1,),
            in_specs=[pl.BlockSpec((3, CHUNK, width), at(s)) for s in range(groups)]
            + [pl.BlockSpec((width, 1), lambda step, where: (0, 0))],
            out_specs=[
                pl.BlockSpec((3, CHUNK // 2, 2 * cap), lambda step, where: (0, 0, 0))
                for _ in range(groups)
            ],
        ),
        out_shape=[shape] * groups,
        compiler_params=params(),
        name="pick",
    )(place, *([coords] * groups), rank)


def distance_kernel(groups, cap, *refs):
    blocks, signs_ref, out, joined = refs[:groups], refs[groups], refs[groups + 1], refs[groups + 2]
    half = CHUNK // 2
    for s, block in enumerate(blocks):
        for k in range(3):
            joined[k * CHUNK : k * CHUNK + half, s * cap : (s + 1) * cap] = block[k, :, 0:cap]
            joined[k * CHUNK + half : (k + 1) * CHUNK, s * cap : (s + 1) * cap] = block[
                k, :, cap : 2 * cap
            ]
    delta = jnp.dot(joined[...], signs_ref[...], preferred_element_type=F32)
    square = delta * delta
    total = square[:CHUNK] + square[CHUNK : 2 * CHUNK] + square[2 * CHUNK :]
    out[...] = jnp.sqrt(total + 0.01)


def distances(blocks, signs, cap):
    groups = len(blocks)
    return pl.pallas_call(
        functools.partial(distance_kernel, groups, cap),
        out_shape=jax.ShapeDtypeStruct((CHUNK, signs.shape[1]), F32),
        scratch_shapes=[pltpu.VMEM((3 * CHUNK, groups * cap), BF16)],
        compiler_params=params(),
        name="distances",
    )(*blocks, signs)


def split_in_two(value):
    high = value.astype(BF16)
    return high, (value - high.astype(F32)).astype(BF16)


def moment_kernel(chunks, sides, place_ref, *refs):
    pieces = refs[: chunks * sides]
    halo_ref, valid_ref, shift_ref, out, own_out, sums_out, sums_next_out, every, own = refs[
        chunks * sides :
    ]
    frames, feats = every.shape
    cols = own.shape[1]
    side = place_ref[1]
    shift = shift_ref[...]
    for j in range(chunks):
        for s in range(sides):
            there = lax.rem(side + sides - s, sides)
            row = pl.multiple_of((j * sides + there) * CHUNK, CHUNK)
            every[pl.ds(row, CHUNK), :] = pieces[j * sides + s][...] - shift
    for s in range(sides):

        @pl.when(side == s)
        def _():
            own[0:frames, :] = every[:, s * cols : (s + 1) * cols]
            own[frames : frames + HALO, :] = halo_ref[...] - shift[:, s * cols : (s + 1) * cols]

    own_out[...] = own[0:frames, :]
    valid = valid_ref[...]
    now = every[...]
    weighed = valid * now
    sums_out[0:1, :] = jnp.sum(weighed, 0, keepdims=True)
    sums_out[1:2, :] = jnp.sum(weighed * now, 0, keepdims=True)
    later = own[LAG : LAG + frames, :]
    weighed_later = valid * later
    sums_next_out[0:1, :] = jnp.sum(weighed_later, 0, keepdims=True)
    sums_next_out[1:2, :] = jnp.sum(weighed_later * later, 0, keepdims=True)
    left_high, left_low = split_in_two(now)
    left_high, left_low = left_high.T, left_low.T
    for part, right in enumerate((valid * own[0:frames, :], weighed_later)):
        right_high, right_low = split_in_two(right)
        total = jnp.dot(left_high, right_high, preferred_element_type=F32)
        total += jnp.dot(left_high, right_low, preferred_element_type=F32)
        total += jnp.dot(left_low, right_high, preferred_element_type=F32)
        out[:, part * cols : (part + 1) * cols] = total


def moments(pieces, halo, valid, shift, place, chunks, sides):
    frames, feats = chunks * sides * CHUNK, shift.shape[1]
    cols = halo.shape[1]
    vmem = pl.BlockSpec(memory_space=pltpu.VMEM)
    return pl.pallas_call(
        functools.partial(moment_kernel, chunks, sides),
        in_specs=[pl.BlockSpec(memory_space=pltpu.SMEM)] + [vmem] * (len(pieces) + 3),
        out_specs=[vmem] * 4,
        out_shape=[
            jax.ShapeDtypeStruct((feats, 2 * cols), F32),
            jax.ShapeDtypeStruct((frames, cols), F32),
            jax.ShapeDtypeStruct((2, feats), F32),
            jax.ShapeDtypeStruct((2, cols), F32),
        ],
        scratch_shapes=[pltpu.VMEM((frames, feats), F32), pltpu.VMEM((frames + HALO, cols), F32)],
        compiler_params=params(),
        name="moments",
    )(place, *pieces, halo, valid, shift)


def with_cap(cap, coords, rank_all, used_pairs, valid, place):
    groups, sides = lax.axis_size("atoms"), lax.axis_size("feat")
    atom_index, feat_index = place[0], place[1]
    width = coords.shape[2]
    frames = coords.shape[1] // groups
    feats = used_pairs.shape[1]
    cols = feats // sides
    chunks = frames // (sides * CHUNK)
    ring = ("atoms", "rep")

    rank = lax.dynamic_index_in_dim(rank_all, atom_index, 0, keepdims=False)[:, None]
    picked = [pick(coords, rank, cap, place, j, groups, sides) for j in range(chunks)]
    arrived = [
        [picked[j][0]] + [rotated(picked[j][s], "atoms", s) for s in range(1, groups)]
        for j in range(chunks)
    ]

    atoms = lax.broadcasted_iota(jnp.int32, (groups, 1, width), 0) * width
    atoms = atoms + lax.broadcasted_iota(jnp.int32, (groups, 1, width), 2)
    slots = lax.broadcasted_iota(jnp.int32, (groups, cap, width), 1)
    listed = jnp.max(jnp.where(rank_all[:, None, :] == slots, atoms, -1), axis=2)
    order = lax.rem(atom_index + groups - jnp.arange(groups, dtype=jnp.int32), groups)
    listed = jnp.take(listed, order, axis=0).reshape(groups * cap, 1)
    signs = (listed == used_pairs[0:1]).astype(BF16) - (listed == used_pairs[1:2]).astype(BF16)

    every, pieces = [], []
    for j in range(chunks):
        block = distances(arrived[j], signs, cap)
        every.append(block)
        pieces += [block] + [rotated(block, "feat", s) for s in range(1, sides)]

    first_valid = lax.dynamic_slice_in_dim(valid, feat_index * CHUNK, CHUNK, 0)
    early = jnp.concatenate(
        [
            jnp.sum(first_valid * every[0], 0, keepdims=True),
            jnp.full((1, feats), jnp.sum(first_valid), F32),
        ],
        0,
    )
    early = lax.psum(early, ("atoms", "feat", "rep"))
    shift = early[0:1] / jnp.maximum(early[1:2], 1.0)

    opening = sum_or_pick(pieces[:sides], feat_index)[:HALO]
    opening = lax.dynamic_slice_in_dim(opening, feat_index * cols, cols, 1)
    halo = passed_down(opening, "atoms")

    local, own, sums, sums_next = moments(pieces, halo, valid, shift, place, chunks, sides)
    mine = lax.psum_scatter(local, ring, scatter_dimension=0, tiled=True)
    count, sums, sums_next = lax.psum((jnp.sum(valid), sums, sums_next), ring)

    mean, mean_next = sums[0] / count, sums_next[0] / count
    spread = sums[1] - count * mean * mean
    spread_next = sums_next[1] - count * mean_next * mean_next
    scale = 1.0 / jnp.sqrt(spread / count + 1e-05)
    scale_next = 1.0 / jnp.sqrt(spread_next / count + 1e-05)
    row_count = feats // lax.axis_size(ring)
    row_start = lax.axis_index(ring) * row_count
    mean_rows = lax.dynamic_slice_in_dim(mean, row_start, row_count)[:, None]
    scale_rows = lax.dynamic_slice_in_dim(scale, row_start, row_count)[:, None]
    mean_cols = lax.dynamic_slice_in_dim(mean, feat_index * cols, cols)[None]
    scale_cols = lax.dynamic_slice_in_dim(scale, feat_index * cols, cols)[None]
    corr_inst = (mine[:, :cols] / count - mean_rows * mean_cols) * scale_rows * scale_cols
    corr_lag = (mine[:, cols:] / count - mean_rows * mean_next[None]) * scale_rows * scale_next
    projections = ((own - mean_cols) * scale_cols)[None]
    return corr_inst, corr_lag, projections


def sum_or_pick(blocks, side):
    sides = len(blocks)
    out = blocks[0]
    for s in range(1, sides):
        out = jnp.where(lax.rem(side + sides - s, sides) == 0, blocks[s], out)
    return out


def shards(atom_coords, atom_pairs, traj_ids):
    groups, sides = lax.axis_size("atoms"), lax.axis_size("feat")
    atom_index, feat_index = lax.axis_index("atoms"), lax.axis_index("feat")
    place = jnp.stack([atom_index, feat_index]).astype(jnp.int32)
    width = atom_coords.shape[3]
    frames = atom_coords.shape[1] // groups
    coords = jnp.transpose(atom_coords[0], (1, 0, 2))

    cols = atom_pairs.shape[1]
    used_pairs = jnp.zeros((2, cols * sides), jnp.int32)
    for s in range(sides):
        there = lax.rem(feat_index + sides - s, sides)
        block = atom_pairs if s == 0 else rotated(atom_pairs, "feat", s)
        used_pairs = lax.dynamic_update_slice_in_dim(used_pairs, block, there * cols, 1)

    atoms = jnp.arange(groups * width, dtype=jnp.int32)
    used = jnp.any(used_pairs.reshape(-1)[:, None] == atoms[None, :], axis=0)
    used = used.reshape(groups, width)
    upto = lax.broadcasted_iota(jnp.int32, (width, width), 0) <= lax.broadcasted_iota(
        jnp.int32, (width, width), 1
    )
    order = jnp.dot(used.astype(BF16), upto.astype(BF16), preferred_element_type=F32)
    order = order.astype(jnp.int32)
    rank_all = jnp.where(used, order - 1, -1)

    ids = jnp.concatenate([traj_ids[0], jnp.full((LAG,), -1, jnp.int32)])
    offset = atom_index * frames
    ids_now = lax.dynamic_slice_in_dim(ids, offset, frames)
    ids_later = lax.dynamic_slice_in_dim(ids, offset + LAG, frames)
    valid = (ids_now == ids_later).astype(F32)[:, None]

    cap = min(width, -(-(width * 9 // 16) // 64) * 64)
    operands = (coords, rank_all, used_pairs, valid, place)
    return lax.cond(
        jnp.max(order) <= cap,
        functools.partial(with_cap, cap),
        functools.partial(with_cap, width),
        *operands,
    )


def solution(mesh):
    placed = (P(("grp", "rep"), None, None, "atoms"), P(None, "feat"), P(("grp", "rep"), None))
    return jax.shard_map(
        shards,
        mesh=mesh,
        in_specs=placed,
        out_specs=(
            P(("grp", "atoms", "rep"), "feat"),
            P(("grp", "atoms", "rep"), "feat"),
            P(("grp", "rep"), "atoms", "feat"),
        ),
        check_vma=False,
    )
```

```python
import functools

import jax
import jax.numpy as jnp
from jax import lax
from jax.experimental import pallas as pl
from jax.experimental.pallas import tpu as pltpu
from jax.sharding import PartitionSpec as P

LAG = 10
HALO = 16
CHUNK = 64
CODE = 32700.0
FINE = 60000.0
MEAN_STEP = 0.001
ROOT_STEP = 0.02
TINY = 1e-30
VMEM_LIMIT = 48 * 1024 * 1024
F32 = jnp.float32
BF16 = jnp.bfloat16
LARGE = pl.CostEstimate(flops=10**11, bytes_accessed=1024, transcendentals=0)
SMALL = pl.CostEstimate(flops=1024, bytes_accessed=1024, transcendentals=0)


def rotated(block, axis, shift):
    size = lax.axis_size(axis)
    return lax.ppermute(block, axis, [(i, (i + shift) % size) for i in range(size)])


def passed_down(block, axis):
    return lax.ppermute(block, axis, [(i + 1, i) for i in range(lax.axis_size(axis) - 1)])


def params():
    return pltpu.CompilerParams(vmem_limit_bytes=VMEM_LIMIT)


def pick_kernel(start, place_ref, coords_ref, rank_ref, after_ref, *refs):
    groups = len(refs) - 2
    outs, rows_ref, sems = refs[:groups], refs[groups], refs[groups + 1]
    size, width = rows_ref.shape[2], rows_ref.shape[3]
    cap = outs[0].shape[2] // 2
    frames = coords_ref.shape[1] // groups
    copies = []
    for s in range(groups):
        there = lax.rem(place_ref[0] + s, groups)
        row = pl.multiple_of(there * frames + start + place_ref[1] * size, CHUNK)
        copies.append(
            pltpu.make_async_copy(
                coords_ref.at[:, pl.ds(row, size), :], rows_ref.at[s], sems.at[s]
            )
        )
    for copy in copies:
        copy.start()
    slots = lax.broadcasted_iota(jnp.int32, (width, cap), 1)
    chosen = (rank_ref[...] == slots).astype(F32).astype(BF16)
    half = size // 2
    for s in range(groups):
        copies[s].wait()
        rows = rows_ref[s].reshape(3 * size, width)
        picked = jnp.dot(rows, chosen, preferred_element_type=F32).astype(BF16)
        picked = picked.reshape(3, size, cap)
        outs[s][:, :, 0:cap] = picked[:, :half, :]
        outs[s][:, :, cap : 2 * cap] = picked[:, half:, :]


def pick(coords, rank, after, cap, place, start, size, groups):
    width = coords.shape[2]
    vmem = pl.BlockSpec(memory_space=pltpu.VMEM)
    return pl.pallas_call(
        functools.partial(pick_kernel, start),
        in_specs=[
            pl.BlockSpec(memory_space=pltpu.SMEM),
            pl.BlockSpec(memory_space=pltpu.HBM),
            vmem,
            pl.BlockSpec(memory_space=pl.ANY),
        ],
        out_specs=[vmem] * groups,
        out_shape=[jax.ShapeDtypeStruct((3, size // 2, 2 * cap), BF16)] * groups,
        scratch_shapes=[
            pltpu.VMEM((groups, 3, size, width), BF16),
            pltpu.SemaphoreType.DMA((groups,)),
        ],
        compiler_params=params(),
        cost_estimate=SMALL,
        name="pick",
    )(place, coords, rank, after)


def distance_kernel(*refs):
    blocks, (signs_ref, after_ref, out, joined) = refs[:-4], refs[-4:]
    half, cap = blocks[0].shape[1], blocks[0].shape[2] // 2
    size = 2 * half
    for s, block in enumerate(blocks):
        columns = slice(s * cap, (s + 1) * cap)
        for k in range(3):
            joined[k * size : k * size + half, columns] = block[k, :, 0:cap]
            joined[k * size + half : (k + 1) * size, columns] = block[k, :, cap : 2 * cap]
    delta = jnp.dot(joined[...], signs_ref[...], preferred_element_type=F32)
    square = delta * delta
    total = square[:size] + square[size : 2 * size] + square[2 * size :]
    out[...] = jnp.sqrt(total + 0.01)


def distances(blocks, signs, after):
    size = 2 * blocks[0].shape[1]
    vmem = pl.BlockSpec(memory_space=pltpu.VMEM)
    return pl.pallas_call(
        distance_kernel,
        in_specs=[vmem] * (len(blocks) + 1) + [pl.BlockSpec(memory_space=pl.ANY)],
        out_specs=vmem,
        out_shape=jax.ShapeDtypeStruct((size, signs.shape[1]), F32),
        scratch_shapes=[pltpu.VMEM((3 * size, signs.shape[0]), BF16)],
        compiler_params=params(),
        cost_estimate=LARGE,
        name="distances",
    )(*blocks, signs, after)


def split_in_two(value):
    high = value.astype(BF16)
    return high, (value - high.astype(F32)).astype(BF16)


def product(left, right):
    left_high, left_low = split_in_two(left)
    right_high, right_low = split_in_two(right)
    left_high, left_low = left_high.T, left_low.T
    total = jnp.dot(left_high, right_high, preferred_element_type=F32)
    total += jnp.dot(left_high, right_low, preferred_element_type=F32)
    return total + jnp.dot(left_low, right_high, preferred_element_type=F32)


def place_pieces(sizes, side, sides, pieces, every, first):
    row = first
    for j, size in enumerate(sizes):
        for s in range(sides):
            there = lax.rem(side + sides - s, sides)
            at = pl.multiple_of(row + there * size, HALO)
            every[pl.ds(at, size), :] = pieces[j * sides + s][...]
        row += sides * size


def own_columns(side, sides, whole, own):
    cols = own.shape[1]
    for s in range(sides):

        @pl.when(side == s)
        def _():
            own[...] = whole[:, s * cols : (s + 1) * cols]


def row_sum(value):
    return jnp.sum(value, 0, keepdims=True)


def early_kernel(sizes, sides, place_ref, *refs):
    pieces = refs[: len(sizes) * sides]
    valid_ref, out, own_out, shift_out, sums_out, tail_out, every, own = refs[len(pieces) :]
    frames = every.shape[0]
    cols = own.shape[1]
    side = place_ref[1]
    place_pieces(sizes, side, sides, pieces, every, 0)
    valid = valid_ref[0:frames, :]
    count = jnp.maximum(jnp.sum(valid), 1.0)
    shift = row_sum(valid * every[...]) / count
    shift_out[...] = shift
    every[...] = every[...] - shift
    tail_out[...] = every[frames - HALO : frames, :]
    own_columns(side, sides, every, own)
    own_out[...] = own[...]
    now = every[...]
    weighed = valid * now
    weighed_later = valid[: frames - LAG] * own[LAG:frames, :]
    sums_out[0:1, :] = row_sum(weighed)
    sums_out[1:2, :] = row_sum(weighed * now)
    sums_out[2:3, 0:cols] = row_sum(weighed_later)
    sums_out[3:4, 0:cols] = row_sum(weighed_later * own[LAG:frames, :])
    weighed_later = jnp.concatenate([weighed_later, jnp.zeros((LAG, cols), F32)], 0)
    out[:, 0:cols] = product(now, valid * own[...])
    out[:, cols : 2 * cols] = product(now, weighed_later)


def early_moments(pieces, valid, place, sizes, sides):
    frames, feats = sides * sum(sizes), pieces[0].shape[1]
    cols = feats // sides
    vmem = pl.BlockSpec(memory_space=pltpu.VMEM)
    return pl.pallas_call(
        functools.partial(early_kernel, sizes, sides),
        in_specs=[pl.BlockSpec(memory_space=pltpu.SMEM)] + [vmem] * (len(pieces) + 1),
        out_specs=[vmem] * 5,
        out_shape=[
            jax.ShapeDtypeStruct((feats, 2 * cols), F32),
            jax.ShapeDtypeStruct((frames, cols), F32),
            jax.ShapeDtypeStruct((1, feats), F32),
            jax.ShapeDtypeStruct((4, feats), F32),
            jax.ShapeDtypeStruct((HALO, feats), F32),
        ],
        scratch_shapes=[pltpu.VMEM((frames, feats), F32), pltpu.VMEM((frames, cols), F32)],
        compiler_params=params(),
        cost_estimate=LARGE,
        name="early_moments",
    )(place, *pieces, valid)


def late_kernel(size, sides, groups, reps, place_ref, *refs):
    pieces = refs[:sides]
    before_ref, shift_ref, sums_ref, tail_ref, halo_ref, valid_ref = refs[sides : sides + 6]
    outs = refs[sides + 6 : sides + 6 + reps]
    own_out, every, own, right, left_high, left_low = refs[sides + 6 + reps :]
    frames, cols = sides * size, own_out.shape[1]
    feats = every.shape[1]
    rows = feats // (groups * reps)
    side = place_ref[1]
    shift = shift_ref[...]
    every[0:HALO, :] = tail_ref[...]
    place_pieces((size,), side, sides, pieces, every, HALO)
    every[HALO : HALO + frames, :] = every[HALO : HALO + frames, :] - shift
    own_columns(side, sides, every, own)
    for s in range(sides):

        @pl.when(side == s)
        def _():
            own[HALO + frames :, :] = halo_ref[...] - shift[:, s * cols : (s + 1) * cols]

    own_out[...] = own[HALO : HALO + frames, :]
    valid_all = valid_ref[...]
    total = jnp.sum(valid_all)
    count = jnp.maximum(total, 1.0)
    valid = valid_all[valid_all.shape[0] - frames :]
    now = every[HALO : HALO + frames, :]
    weighed = valid * now
    sums = sums_ref[0:1, :] + row_sum(weighed)
    squares = sums_ref[1:2, :] + row_sum(weighed * now)
    later = own[HALO : HALO + frames + LAG, :]
    weighed_later = valid_all[valid_all.shape[0] - frames - LAG :] * later
    sums_next = sums_ref[2:3, 0:cols] + row_sum(weighed_later)
    squares_next = sums_ref[3:4, 0:cols] + row_sum(weighed_later * later)
    own_sums = jnp.zeros((1, cols), F32)
    own_shift = jnp.zeros((1, cols), F32)
    for s in range(sides):
        mine = (side == s).astype(F32)
        own_sums += mine * sums[:, s * cols : (s + 1) * cols]
        own_shift += mine * shift[:, s * cols : (s + 1) * cols]
    first = lax.broadcasted_iota(jnp.int32, (HALO, 1), 0) == 0
    every[HALO + frames :, :] = jnp.where(first, sums, 0.0)
    right[0:HALO, :] = jnp.zeros((HALO, 2 * cols), F32)
    right[HALO : HALO + frames, 0:cols] = valid * own[HALO : HALO + frames, :]
    right[HALO - LAG : HALO + frames, cols : 2 * cols] = weighed_later
    right[HALO + frames :, 0:cols] = jnp.where(first, -own_sums / count, 0.0)
    right[HALO + frames :, cols : 2 * cols] = jnp.where(first, -sums_next / count, 0.0)
    high, low = split_in_two(every[...])
    left_high[...] = high.T
    left_low[...] = low.T
    right_high, right_low = split_in_two(right[...])
    for s in reversed(range(reps)):
        rep = lax.rem(place_ref[2] + s, reps)
        out = outs[s]
        for z in range(groups):
            at = pl.ds(pl.multiple_of((z * reps + rep) * rows, rows), rows)
            part = before_ref[at, :]
            part += jnp.dot(left_high[at, :], right_high, preferred_element_type=F32)
            part += jnp.dot(left_high[at, :], right_low, preferred_element_type=F32)
            part += jnp.dot(left_low[at, :], right_high, preferred_element_type=F32)
            out[z * rows : (z + 1) * rows, :] = part
        end = groups * rows
        fold = feats // (2 * cols)
        mean, square = shift + sums / count, squares - sums * sums / count
        for f in range(fold):
            part = slice(2 * cols * f, 2 * cols * (f + 1))
            out[end + f : end + f + 1, :] = mean[:, part]
            out[end + fold + f : end + fold + f + 1, :] = square[:, part]
        end += 2 * fold
        out[end : end + 1, 0:cols] = own_shift + sums_next / count
        out[end : end + 1, cols : 2 * cols] = squares_next - sums_next * sums_next / count
        out[end + 1 : end + 2, :] = jnp.zeros((1, 2 * cols), F32) + total
        spare = out.shape[0] - end - 2
        if spare:
            out[end + 2 :, :] = jnp.zeros((spare, 2 * cols), F32)


def late_moments(pieces, before, shift, sums, tail, halo, valid, place, sides, groups, reps):
    size, feats = pieces[0].shape
    cols = feats // sides
    frames = sides * size
    vmem = pl.BlockSpec(memory_space=pltpu.VMEM)
    outs = pl.pallas_call(
        functools.partial(late_kernel, size, sides, groups, reps),
        in_specs=[pl.BlockSpec(memory_space=pltpu.SMEM)] + [vmem] * (len(pieces) + 6),
        out_specs=[vmem] * (reps + 1),
        out_shape=[jax.ShapeDtypeStruct((feats // reps + 8, 2 * cols), F32)] * reps
        + [jax.ShapeDtypeStruct((frames, cols), F32)],
        scratch_shapes=[
            pltpu.VMEM((frames + 2 * HALO, feats), F32),
            pltpu.VMEM((frames + 2 * HALO, cols), F32),
            pltpu.VMEM((frames + 2 * HALO, 2 * cols), F32),
            pltpu.VMEM((feats, frames + 2 * HALO), BF16),
            pltpu.VMEM((feats, frames + 2 * HALO), BF16),
        ],
        compiler_params=params(),
        cost_estimate=SMALL,
        name="late_moments",
    )(place, *pieces, before, shift, sums, tail, halo, valid)
    return outs[:reps], outs[reps]


def coded(value, step):
    first = jnp.round(value / step)
    second = jnp.round((value - first * step) * (FINE / step))
    return [first, second]


def decoded(first, second, step):
    return first * step + second * (step / FINE)


def rolled(value, first):
    rows, width = value.shape
    wide = jnp.broadcast_to(value, (8, width)) if rows == 1 else value
    return pltpu.roll(wide, lax.rem(width - first, width), 1)[:rows]


def as_column(row):
    return jnp.broadcast_to(row, (8, row.shape[1])).T[:, 0:1]


def share_kernel(groups, feats, place_ref, *refs):
    parts, outs = refs[: -groups - 1], refs[-groups - 1 :]
    reps, width = len(parts), outs[0].shape[1]
    cols = width // 2
    fold = feats // width
    rows = outs[0].shape[0]
    end = groups * rows
    square = jnp.zeros((1, feats), F32)
    square_next = jnp.zeros((1, cols), F32)
    codes = []
    for part in parts:
        own = part[end : end + 8, :]
        mean = [own[f : f + 1] for f in range(fold)]
        squares = [own[fold + f : fold + f + 1] for f in range(fold)]
        final = own[2 * fold : 2 * fold + 1]
        square += jnp.concatenate(squares, 1)
        square_next += final[:, cols:]
        for line in mean:
            codes += coded(line, MEAN_STEP)
        for line in squares:
            codes += coded(jnp.sqrt(jnp.maximum(line, 0.0)), ROOT_STEP)
        codes += coded(final[:, :cols], MEAN_STEP)
        codes[-2:] = [
            jnp.concatenate(pair, 1)
            for pair in zip(codes[-2:], coded(jnp.sqrt(jnp.maximum(final[:, cols:], 0.0)), ROOT_STEP))
        ]
        codes.append(own[2 * fold + 1 : 2 * fold + 2])
    spare = outs[1].shape[0] - rows - len(codes)
    if spare:
        codes.append(jnp.zeros((spare, width), F32))
    codes = jnp.concatenate(codes, 0).astype(jnp.int32).astype(jnp.int16)
    inverse = lax.rsqrt(jnp.maximum(square, TINY))
    inverse_next = lax.rsqrt(jnp.maximum(square_next, TINY))
    inverse_cols = jnp.concatenate(
        [rolled(inverse, place_ref[1] * cols)[:, :cols], inverse_next], 1
    )
    for s in range(groups):
        there = lax.rem(place_ref[0] + s, groups)
        at = pl.ds(pl.multiple_of(there * rows, rows), rows)
        total = parts[0][at, :]
        for part in parts[1:]:
            total += part[at, :]
        if s == 0:
            outs[0][...] = total
            continue
        first = (there * reps + place_ref[2]) * rows
        ratio = total * as_column(rolled(inverse, first)[:, :rows]) * inverse_cols
        root = jnp.sqrt(jnp.minimum(jnp.abs(ratio), 1.001)) * CODE
        root = jnp.where(ratio < 0.0, -root, root)
        outs[s][0:rows, :] = jnp.round(root).astype(jnp.int32).astype(jnp.int16)
        outs[s][rows:, :] = codes
    outs[groups][...] = codes


def share(parts, place, groups, feats):
    width = parts[0].shape[1]
    rows = (parts[0].shape[0] - 8) // groups
    lines = -(-len(parts) * (4 * (feats // width) + 3) // 16) * 16
    vmem = pl.BlockSpec(memory_space=pltpu.VMEM)
    return pl.pallas_call(
        functools.partial(share_kernel, groups, feats),
        in_specs=[pl.BlockSpec(memory_space=pltpu.SMEM)] + [vmem] * len(parts),
        out_specs=[vmem] * (groups + 1),
        out_shape=[jax.ShapeDtypeStruct((rows, width), F32)]
        + [jax.ShapeDtypeStruct((rows + lines, width), jnp.int16)] * (groups - 1)
        + [jax.ShapeDtypeStruct((lines, width), jnp.int16)],
        compiler_params=params(),
        cost_estimate=SMALL,
        name="share",
    )(place, *parts)


def finish_kernel(reps, place_ref, kept_ref, codes_ref, *refs):
    blocks = refs[:-6]
    shift_ref, early_ref, late_ref, inst_out, lag_out, projections_out = refs[-6:]
    rows, cols = inst_out.shape
    feats = shift_ref.shape[1]
    width = 2 * cols
    fold = feats // width
    count = jnp.zeros((1, 1), F32)
    mean = jnp.zeros((1, feats), F32)
    mean_next = jnp.zeros((1, cols), F32)
    stats = []
    for block in (codes_ref,) + tuple(blocks):
        start = 0 if block is codes_ref else rows
        codes = block[start:, :].astype(jnp.int32).astype(F32)
        at = 0
        for r in range(reps):
            lines = [codes[at + i : at + i + 1] for i in range(4 * fold + 3)]
            at += 4 * fold + 3
            pairs = [(lines[2 * i], lines[2 * i + 1]) for i in range(2 * fold + 1)]
            means = [decoded(*pair, MEAN_STEP) for pair in pairs[:fold]]
            roots = [decoded(*pair, ROOT_STEP) for pair in pairs[fold : 2 * fold]]
            one, two = pairs[2 * fold]
            roots_next = decoded(one[:, cols:], two[:, cols:], ROOT_STEP)
            here = [
                jnp.concatenate(means, 1),
                jnp.concatenate([root * root for root in roots], 1),
                decoded(one[:, :cols], two[:, :cols], MEAN_STEP),
                roots_next * roots_next,
                lines[-1][:, 0:1],
            ]
            stats.append(here)
            count += here[4]
            mean += here[4] * here[0]
            mean_next += here[4] * here[2]
    mean, mean_next = mean / count, mean_next / count
    spread = jnp.zeros((1, feats), F32)
    spread_next = jnp.zeros((1, cols), F32)
    away, away_next = [], []
    for here in stats:
        away.append(here[0] - mean)
        away_next.append(here[2] - mean_next)
        spread += here[1] + here[4] * away[-1] * away[-1]
        spread_next += here[3] + here[4] * away_next[-1] * away_next[-1]
    numbers = jnp.concatenate([here[4] for here in stats], 0)
    scale = 1.0 / jnp.sqrt(spread / count + 1e-05)
    scale_next = 1.0 / jnp.sqrt(spread_next / count + 1e-05)
    away = jnp.concatenate(away, 0)

    first_row = (place_ref[0] * reps + place_ref[2]) * rows
    first_col = place_ref[1] * cols
    right = numbers * jnp.concatenate(
        [rolled(away, first_col)[:, :cols], jnp.concatenate(away_next, 0)], 1
    )
    moment = kept_ref[...] + jnp.dot(
        rolled(away, first_row)[:, :rows].T,
        right,
        precision=lax.Precision.HIGHEST,
        preferred_element_type=F32,
    )
    for g, block in enumerate(blocks):
        here = stats[(g + 1) * reps : (g + 2) * reps]
        root = jnp.sqrt(sum(one[1] for one in here))
        root_next = jnp.sqrt(sum(one[3] for one in here))
        root_rows = as_column(rolled(root, first_row)[:, :rows])
        root_cols = jnp.concatenate([rolled(root, first_col)[:, :cols], root_next], 1)
        code = block[0:rows, :].astype(jnp.int32).astype(F32) * (1.0 / CODE)
        moment += code * jnp.abs(code) * root_rows * root_cols
    scale_cols = rolled(scale, first_col)[:, :cols]
    moment = moment / count * as_column(rolled(scale, first_row)[:, :rows])
    inst_out[...] = moment[:, 0:cols] * scale_cols
    lag_out[...] = moment[:, cols : 2 * cols] * scale_next
    offset = rolled(shift_ref[...] - mean, first_col)[:, :cols]
    split = early_ref.shape[0]
    projections_out[0:split, :] = (early_ref[...] + offset) * scale_cols
    projections_out[split:, :] = (late_ref[...] + offset) * scale_cols


def finish(kept, codes, blocks, shift, early, late, place, reps):
    rows = kept.shape[0]
    cols = early.shape[1]
    frames = early.shape[0] + late.shape[0]
    vmem = pl.BlockSpec(memory_space=pltpu.VMEM)
    return pl.pallas_call(
        functools.partial(finish_kernel, reps),
        in_specs=[pl.BlockSpec(memory_space=pltpu.SMEM)] + [vmem] * (len(blocks) + 5),
        out_specs=[vmem] * 3,
        out_shape=[
            jax.ShapeDtypeStruct((rows, cols), F32),
            jax.ShapeDtypeStruct((rows, cols), F32),
            jax.ShapeDtypeStruct((frames, cols), F32),
        ],
        compiler_params=params(),
        cost_estimate=SMALL,
        name="finish",
    )(place, kept, codes, *blocks, shift, early, late)


def chunk_sizes(frames):
    return (frames // 2, frames // 2)


def with_cap(cap, coords, rank_all, used_pairs, valid, place):
    groups, sides = lax.axis_size("atoms"), lax.axis_size("feat")
    atom_index, feat_index = place[0], place[1]
    width = coords.shape[2]
    frames = coords.shape[1] // groups
    feats = used_pairs.shape[1]
    cols = feats // sides
    sizes = chunk_sizes(frames // sides)

    rank = lax.dynamic_index_in_dim(rank_all, atom_index, 0, keepdims=False)[:, None]
    arrived, start, after = [], 0, rank
    for size in sizes:
        picked = pick(coords, rank, after, cap, place, start, size, groups)
        arrived.append([picked[0]] + [rotated(picked[s], "atoms", s) for s in range(1, groups)])
        after = arrived[-1][1]
        start += sides * size

    atoms = lax.broadcasted_iota(jnp.int32, (groups, 1, width), 0) * width
    atoms = atoms + lax.broadcasted_iota(jnp.int32, (groups, 1, width), 2)
    slots = lax.broadcasted_iota(jnp.int32, (groups, cap, width), 1)
    listed = jnp.max(jnp.where(rank_all[:, None, :] == slots, atoms, -1), axis=2)
    order = lax.rem(atom_index + groups - jnp.arange(groups, dtype=jnp.int32), groups)
    listed = jnp.take(listed, order, axis=0).reshape(groups * cap, 1)
    signs = (listed == used_pairs[0:1]).astype(BF16) - (listed == used_pairs[1:2]).astype(BF16)

    pieces, after = [], arrived[-1][0]
    for blocks in arrived:
        block = distances(blocks, signs, after)
        after = block
        pieces.append([block] + [rotated(block, "feat", s) for s in range(1, sides)])

    opening = sum_or_pick(pieces[0], feat_index)[:HALO]
    opening = lax.dynamic_slice_in_dim(opening, feat_index * cols, cols, 1)
    halo = passed_down(opening, "atoms")

    early = [piece for chunk in pieces[:-1] for piece in chunk]
    before, own_early, shift, sums, tail = early_moments(early, valid, place, sizes[:-1], sides)
    reps = lax.axis_size("rep")
    parts, own_late = late_moments(
        pieces[-1], before, shift, sums, tail, halo, valid, place, sides, groups, reps
    )
    parts = [parts[0]] + [rotated(parts[s], "rep", s) for s in range(1, reps)]
    kept, *blocks, codes = share(parts, place, groups, feats)
    blocks = [rotated(block, "atoms", s + 1) for s, block in enumerate(blocks)]
    corr_inst, corr_lag, projections = finish(
        kept, codes, blocks, shift, own_early, own_late, place, reps
    )
    return corr_inst, corr_lag, projections[None]


def sum_or_pick(blocks, side):
    sides = len(blocks)
    out = blocks[0]
    for s in range(1, sides):
        out = jnp.where(lax.rem(side + sides - s, sides) == 0, blocks[s], out)
    return out


def shards(atom_coords, atom_pairs, traj_ids):
    groups, sides = lax.axis_size("atoms"), lax.axis_size("feat")
    atom_index, feat_index = lax.axis_index("atoms"), lax.axis_index("feat")
    place = jnp.stack([atom_index, feat_index, lax.axis_index("rep")]).astype(jnp.int32)
    width = atom_coords.shape[3]
    frames = atom_coords.shape[1] // groups
    coords = jnp.transpose(atom_coords[0], (1, 0, 2))

    cols = atom_pairs.shape[1]
    used_pairs = jnp.zeros((2, cols * sides), jnp.int32)
    for s in range(sides):
        there = lax.rem(feat_index + sides - s, sides)
        block = atom_pairs if s == 0 else rotated(atom_pairs, "feat", s)
        used_pairs = lax.dynamic_update_slice_in_dim(used_pairs, block, there * cols, 1)

    atoms = jnp.arange(groups * width, dtype=jnp.int32)
    used = jnp.any(used_pairs.reshape(-1)[:, None] == atoms[None, :], axis=0)
    used = used.reshape(groups, width)
    upto = lax.broadcasted_iota(jnp.int32, (width, width), 0) <= lax.broadcasted_iota(
        jnp.int32, (width, width), 1
    )
    order = jnp.dot(used.astype(BF16), upto.astype(BF16), preferred_element_type=F32)
    order = order.astype(jnp.int32)
    rank_all = jnp.where(used, order - 1, -1)

    ids = jnp.concatenate([traj_ids[0], jnp.full((LAG,), -1, jnp.int32)])
    offset = atom_index * frames
    ids_now = lax.dynamic_slice_in_dim(ids, offset, frames)
    ids_later = lax.dynamic_slice_in_dim(ids, offset + LAG, frames)
    valid = (ids_now == ids_later).astype(F32)[:, None]

    cap = min(width, -(-(width * 9 // 16) // 64) * 64)
    def again(carry):
        ranks = rank_all + (carry[0] - 1)
        return carry[0] - 1, with_cap(width, coords, ranks, used_pairs, valid, place)

    overflow = (jnp.max(order) > cap).astype(jnp.int32)
    outs = with_cap(cap, coords, rank_all, used_pairs, valid, place)
    return lax.while_loop(lambda carry: carry[0] > 0, again, (overflow, outs))[1]


def solution(mesh):
    placed = (P(("grp", "rep"), None, None, "atoms"), P(None, "feat"), P(("grp", "rep"), None))
    return jax.shard_map(
        shards,
        mesh=mesh,
        in_specs=placed,
        out_specs=(
            P(("grp", "atoms", "rep"), "feat"),
            P(("grp", "atoms", "rep"), "feat"),
            P(("grp", "rep"), "atoms", "feat"),
        ),
        check_vma=False,
    )
```

```python
import functools

import jax
import jax.numpy as jnp
from jax import lax
from jax.experimental import pallas as pl
from jax.experimental.pallas import tpu as pltpu
from jax.sharding import PartitionSpec as P

LAG = 10
HALO = 16
CHUNK = 64
CODE = 32700.0
FINE = 60000.0
MEAN_STEP = 0.001
ROOT_STEP = 0.02
TINY = 1e-30
REACH = 1e-6
VMEM_LIMIT = 48 * 1024 * 1024
F32 = jnp.float32
BF16 = jnp.bfloat16
LARGE = pl.CostEstimate(flops=10**11, bytes_accessed=1024, transcendentals=0)
SMALL = pl.CostEstimate(flops=1024, bytes_accessed=1024, transcendentals=0)


def rotated(block, axis, shift):
    size = lax.axis_size(axis)
    return lax.ppermute(block, axis, [(i, (i + shift) % size) for i in range(size)])


def passed_down(block, axis):
    return lax.ppermute(block, axis, [(i + 1, i) for i in range(lax.axis_size(axis) - 1)])


def params():
    return pltpu.CompilerParams(vmem_limit_bytes=VMEM_LIMIT)


def start_rows(sizes, start, place_ref, coords_ref, rows_refs, sems):
    groups, sides = rows_refs[0].shape[0], lax.axis_size("feat")
    frames = coords_ref.shape[1] // groups
    copies = []
    for j, size in enumerate(sizes):
        for s in range(groups):
            there = lax.rem(place_ref[0] + s, groups)
            row = there * frames + start + place_ref[1] * size
            copies.append(
                pltpu.make_async_copy(
                    coords_ref.at[:, pl.ds(pl.multiple_of(row, HALO), size), :],
                    rows_refs[j].at[s],
                    sems.at[j, s],
                )
            )
        start += sides * size
    for copy in copies:
        copy.start()
    return copies


def pick_rows(rows, chosen, out):
    _, size, width = rows.shape
    cap, half = chosen.shape[1], size // 2
    picked = jnp.dot(
        rows[...].reshape(3 * size, width), chosen, preferred_element_type=F32
    ).astype(BF16)
    picked = picked.reshape(3, size, cap)
    out[:, :, 0:cap] = picked[:, :half, :]
    out[:, :, cap : 2 * cap] = picked[:, half:, :]


def first_pick_kernel(sides, place_ref, coords_ref, ids_ref, *refs):
    pairs, refs = refs[:sides], refs[sides:]
    chosen_ref, ids_out, pairs_out, refs = refs[0], refs[1], refs[2 : 2 + sides], refs[2 + sides :]
    outs, rows_ref, sems = refs[:-2], refs[-2], refs[-1]
    width, cap = chosen_ref.shape
    copies = start_rows((rows_ref.shape[2],), 0, place_ref, coords_ref, [rows_ref], sems)
    ids_out[...] = ids_ref[...]
    for block, copy in zip(pairs, pairs_out):
        copy[...] = block[...]
    rank, _ = ranked(pairs, place_ref[0] * width, width, upto(width))
    lanes = lax.broadcasted_iota(jnp.int32, (width, 128), 1)
    for l in range(0, cap, 128):
        some = min(128, cap - l)
        here = (rank == (lanes + l).astype(F32)).astype(F32).astype(BF16)
        chosen_ref[:, l : l + some] = here[:, :some]
    for s, out in enumerate(outs):
        copies[s].wait()
        pick_rows(rows_ref.at[s], chosen_ref[...], out)


def first_pick(coords, ids, pairs, cap, place, size, groups):
    width = coords.shape[2]
    vmem = pl.BlockSpec(memory_space=pltpu.VMEM)
    outs = pl.pallas_call(
        functools.partial(first_pick_kernel, len(pairs)),
        in_specs=[
            pl.BlockSpec(memory_space=pltpu.SMEM),
            pl.BlockSpec(memory_space=pltpu.HBM),
        ]
        + [vmem] * (len(pairs) + 1),
        out_specs=[vmem] * (2 + len(pairs) + groups),
        out_shape=[
            jax.ShapeDtypeStruct((width, cap), BF16),
            jax.ShapeDtypeStruct(ids.shape, ids.dtype),
        ]
        + [jax.ShapeDtypeStruct(block.shape, block.dtype) for block in pairs]
        + [jax.ShapeDtypeStruct((3, size // 2, 2 * cap), BF16)] * groups,
        scratch_shapes=[
            pltpu.VMEM((groups, 3, size, width), BF16),
            pltpu.SemaphoreType.DMA((1, groups)),
        ],
        compiler_params=params(),
        cost_estimate=SMALL,
        name="first_pick",
    )(place, coords, ids, *pairs)
    sides = len(pairs)
    return outs[0], outs[1], outs[2 : 2 + sides], outs[2 + sides :]


def pick_kernel(start, place_ref, coords_ref, chosen_ref, after_ref, *refs):
    outs, rows_ref, sems = refs[:-2], refs[-2], refs[-1]
    copies = start_rows((rows_ref.shape[2],), start, place_ref, coords_ref, [rows_ref], sems)
    for s, out in enumerate(outs):
        copies[s].wait()
        pick_rows(rows_ref.at[s], chosen_ref[...], out)


def pick(coords, chosen, after, place, start, size, groups):
    width, cap = chosen.shape
    vmem = pl.BlockSpec(memory_space=pltpu.VMEM)
    return pl.pallas_call(
        functools.partial(pick_kernel, start),
        in_specs=[
            pl.BlockSpec(memory_space=pltpu.SMEM),
            pl.BlockSpec(memory_space=pltpu.HBM),
            vmem,
            pl.BlockSpec(memory_space=pl.ANY),
        ],
        out_specs=[vmem] * groups,
        out_shape=[jax.ShapeDtypeStruct((3, size // 2, 2 * cap), BF16)] * groups,
        scratch_shapes=[
            pltpu.VMEM((groups, 3, size, width), BF16),
            pltpu.SemaphoreType.DMA((1, groups)),
        ],
        compiler_params=params(),
        cost_estimate=SMALL,
        name="pick",
    )(place, coords, chosen, after)


def coded(value, step):
    first = jnp.round(value / step)
    second = jnp.round((value - first * step) * (FINE / step))
    return [first, second]


def decoded(first, second, step):
    return first * step + second * (step / FINE)


def decoded_piece(codes, rows):
    size = codes.shape[0] - HALO
    ends = codes[size:, :].astype(jnp.int32).astype(F32)
    middle = decoded(ends[0:1], ends[1:2], MEAN_STEP)
    reach = decoded(ends[2:3], ends[3:4], MEAN_STEP)
    return middle + codes[0:rows, :].astype(jnp.int32).astype(F32) * (reach * (1.0 / CODE))


def distance_kernel(*refs):
    blocks, (signs_ref, after_ref, out, codes_out, joined) = refs[:-5], refs[-5:]
    half, cap = blocks[0].shape[1], blocks[0].shape[2] // 2
    size = 2 * half
    for s, block in enumerate(blocks):
        columns = slice(s * cap, (s + 1) * cap)
        for k in range(3):
            joined[k * size : k * size + half, columns] = block[k, :, 0:cap]
            joined[k * size + half : (k + 1) * size, columns] = block[k, :, cap : 2 * cap]
    delta = jnp.dot(joined[...], signs_ref[...], preferred_element_type=F32)
    square = delta * delta
    total = square[:size] + square[size : 2 * size] + square[2 * size :]
    value = jnp.sqrt(total + 0.01)
    out[...] = value
    least, most = jnp.min(value, 0, keepdims=True), jnp.max(value, 0, keepdims=True)
    ends = coded(0.5 * (most + least), MEAN_STEP) + coded(0.5 * (most - least), MEAN_STEP)
    middle = decoded(ends[0], ends[1], MEAN_STEP)
    reach = decoded(ends[2], ends[3], MEAN_STEP)
    ratio = (value - middle) * (CODE / jnp.maximum(reach, REACH))
    ratio = jnp.round(jnp.clip(ratio, -32767.0, 32767.0))
    codes_out[0:size, :] = ratio.astype(jnp.int32).astype(jnp.int16)
    ends = jnp.concatenate(ends + [jnp.zeros((HALO - 4, out.shape[1]), F32)], 0)
    codes_out[size:, :] = ends.astype(jnp.int32).astype(jnp.int16)


def distances(blocks, signs, after):
    size = 2 * blocks[0].shape[1]
    vmem = pl.BlockSpec(memory_space=pltpu.VMEM)
    return pl.pallas_call(
        distance_kernel,
        in_specs=[vmem] * (len(blocks) + 1) + [pl.BlockSpec(memory_space=pl.ANY)],
        out_specs=[vmem] * 2,
        out_shape=[
            jax.ShapeDtypeStruct((size, signs.shape[1]), F32),
            jax.ShapeDtypeStruct((size + HALO, signs.shape[1]), jnp.int16),
        ],
        scratch_shapes=[pltpu.VMEM((3 * size, signs.shape[0]), BF16)],
        compiler_params=params(),
        cost_estimate=LARGE,
        name="distances",
    )(*blocks, signs, after)


def split_in_two(value):
    high = value.astype(BF16)
    return high, (value - high.astype(F32)).astype(BF16)


def product(left, right):
    left_high, left_low = split_in_two(left)
    right_high, right_low = split_in_two(right)
    left_high, left_low = left_high.T, left_low.T
    total = jnp.dot(left_high, right_high, preferred_element_type=F32)
    total += jnp.dot(left_high, right_low, preferred_element_type=F32)
    return total + jnp.dot(left_low, right_high, preferred_element_type=F32)


def place_pieces(sizes, side, sides, pieces, every, first):
    row = first
    for j, size in enumerate(sizes):
        for s in range(sides):
            there = lax.rem(side + sides - s, sides)
            at = pl.multiple_of(row + there * size, HALO)
            piece = pieces[j * sides + s]
            every[pl.ds(at, size), :] = piece[...] if s == 0 else decoded_piece(piece, size)
        row += sides * size


def own_columns(side, sides, whole, own):
    cols = own.shape[1]
    for s in range(sides):

        @pl.when(side == s)
        def _():
            own[...] = whole[:, s * cols : (s + 1) * cols]


def row_sum(value):
    return jnp.sum(value, 0, keepdims=True)


def early_kernel(sizes, sides, place_ref, *refs):
    pieces = refs[: len(sizes) * sides]
    valid_ref, out, own_out, shift_out, sums_out, tail_out, every, own = refs[len(pieces) :]
    frames = every.shape[0]
    cols = own.shape[1]
    side = place_ref[1]
    place_pieces(sizes, side, sides, pieces, every, 0)
    valid = valid_ref[0:frames, :]
    count = jnp.maximum(jnp.sum(valid), 1.0)
    shift = row_sum(valid * every[...]) / count
    shift_out[...] = shift
    every[...] = every[...] - shift
    tail_out[...] = every[frames - HALO : frames, :]
    own_columns(side, sides, every, own)
    own_out[...] = own[...]
    now = every[...]
    weighed = valid * now
    weighed_later = valid[: frames - LAG] * own[LAG:frames, :]
    sums_out[0:1, :] = row_sum(weighed)
    sums_out[1:2, :] = row_sum(weighed * now)
    sums_out[2:3, 0:cols] = row_sum(weighed_later)
    sums_out[3:4, 0:cols] = row_sum(weighed_later * own[LAG:frames, :])
    weighed_later = jnp.concatenate([weighed_later, jnp.zeros((LAG, cols), F32)], 0)
    out[:, 0:cols] = product(now, valid * own[...])
    out[:, cols : 2 * cols] = product(now, weighed_later)


def early_moments(pieces, valid, place, sizes, sides):
    frames, feats = sides * sum(sizes), pieces[0].shape[1]
    cols = feats // sides
    vmem = pl.BlockSpec(memory_space=pltpu.VMEM)
    return pl.pallas_call(
        functools.partial(early_kernel, sizes, sides),
        in_specs=[pl.BlockSpec(memory_space=pltpu.SMEM)] + [vmem] * (len(pieces) + 1),
        out_specs=[vmem] * 5,
        out_shape=[
            jax.ShapeDtypeStruct((feats, 2 * cols), F32),
            jax.ShapeDtypeStruct((frames, cols), F32),
            jax.ShapeDtypeStruct((1, feats), F32),
            jax.ShapeDtypeStruct((4, feats), F32),
            jax.ShapeDtypeStruct((HALO, feats), F32),
        ],
        scratch_shapes=[pltpu.VMEM((frames, feats), F32), pltpu.VMEM((frames, cols), F32)],
        compiler_params=params(),
        cost_estimate=SMALL,
        name="early_moments",
    )(place, *pieces, valid)


def late_kernel(size, sides, groups, reps, place_ref, *refs):
    pieces = refs[:sides]
    before_ref, shift_ref, sums_ref, tail_ref, halo_ref, valid_ref = refs[sides : sides + 6]
    outs = refs[sides + 6 : sides + 6 + reps]
    own_out, every, own, right, left_high, left_low = refs[sides + 6 + reps :]
    frames, cols = sides * size, own_out.shape[1]
    feats = every.shape[1]
    rows = feats // (groups * reps)
    side = place_ref[1]
    shift = shift_ref[...]
    every[0:HALO, :] = tail_ref[...]
    place_pieces((size,), side, sides, pieces, every, HALO)
    every[HALO : HALO + frames, :] = every[HALO : HALO + frames, :] - shift
    own_columns(side, sides, every, own)
    for s in range(sides):

        @pl.when(side == s)
        def _():
            own[HALO + frames :, :] = halo_ref[...] - shift[:, s * cols : (s + 1) * cols]

    own_out[...] = own[HALO : HALO + frames, :]
    valid_all = valid_ref[...]
    total = jnp.sum(valid_all)
    count = jnp.maximum(total, 1.0)
    valid = valid_all[valid_all.shape[0] - frames :]
    now = every[HALO : HALO + frames, :]
    weighed = valid * now
    sums = sums_ref[0:1, :] + row_sum(weighed)
    squares = sums_ref[1:2, :] + row_sum(weighed * now)
    later = own[HALO : HALO + frames + LAG, :]
    weighed_later = valid_all[valid_all.shape[0] - frames - LAG :] * later
    sums_next = sums_ref[2:3, 0:cols] + row_sum(weighed_later)
    squares_next = sums_ref[3:4, 0:cols] + row_sum(weighed_later * later)
    own_sums = jnp.zeros((1, cols), F32)
    own_shift = jnp.zeros((1, cols), F32)
    for s in range(sides):
        mine = (side == s).astype(F32)
        own_sums += mine * sums[:, s * cols : (s + 1) * cols]
        own_shift += mine * shift[:, s * cols : (s + 1) * cols]
    first = lax.broadcasted_iota(jnp.int32, (HALO, 1), 0) == 0
    every[HALO + frames :, :] = jnp.where(first, sums, 0.0)
    right[0:HALO, :] = jnp.zeros((HALO, 2 * cols), F32)
    right[HALO : HALO + frames, 0:cols] = valid * own[HALO : HALO + frames, :]
    right[HALO - LAG : HALO + frames, cols : 2 * cols] = weighed_later
    right[HALO + frames :, 0:cols] = jnp.where(first, -own_sums / count, 0.0)
    right[HALO + frames :, cols : 2 * cols] = jnp.where(first, -sums_next / count, 0.0)
    high, low = split_in_two(every[...])
    left_high[...] = high.T
    left_low[...] = low.T
    right_high, right_low = split_in_two(right[...])
    for s in reversed(range(reps)):
        rep = lax.rem(place_ref[2] + s, reps)
        out = outs[s]
        for z in range(groups):
            at = pl.ds(pl.multiple_of((z * reps + rep) * rows, rows), rows)
            part = before_ref[at, :]
            part += jnp.dot(left_high[at, :], right_high, preferred_element_type=F32)
            part += jnp.dot(left_high[at, :], right_low, preferred_element_type=F32)
            part += jnp.dot(left_low[at, :], right_high, preferred_element_type=F32)
            out[z * rows : (z + 1) * rows, :] = part
        end = groups * rows
        fold = feats // (2 * cols)
        mean, square = shift + sums / count, squares - sums * sums / count
        for f in range(fold):
            part = slice(2 * cols * f, 2 * cols * (f + 1))
            out[end + f : end + f + 1, :] = mean[:, part]
            out[end + fold + f : end + fold + f + 1, :] = square[:, part]
        end += 2 * fold
        out[end : end + 1, 0:cols] = own_shift + sums_next / count
        out[end : end + 1, cols : 2 * cols] = squares_next - sums_next * sums_next / count
        out[end + 1 : end + 2, :] = jnp.zeros((1, 2 * cols), F32) + total
        spare = out.shape[0] - end - 2
        if spare:
            out[end + 2 :, :] = jnp.zeros((spare, 2 * cols), F32)


def late_moments(pieces, before, shift, sums, tail, halo, valid, place, sides, groups, reps):
    size, feats = pieces[0].shape
    cols = feats // sides
    frames = sides * size
    vmem = pl.BlockSpec(memory_space=pltpu.VMEM)
    outs = pl.pallas_call(
        functools.partial(late_kernel, size, sides, groups, reps),
        in_specs=[pl.BlockSpec(memory_space=pltpu.SMEM)] + [vmem] * (len(pieces) + 6),
        out_specs=[vmem] * (reps + 1),
        out_shape=[jax.ShapeDtypeStruct((feats // reps + 8, 2 * cols), F32)] * reps
        + [jax.ShapeDtypeStruct((frames, cols), F32)],
        scratch_shapes=[
            pltpu.VMEM((frames + 2 * HALO, feats), F32),
            pltpu.VMEM((frames + 2 * HALO, cols), F32),
            pltpu.VMEM((frames + 2 * HALO, 2 * cols), F32),
            pltpu.VMEM((feats, frames + 2 * HALO), BF16),
            pltpu.VMEM((feats, frames + 2 * HALO), BF16),
        ],
        compiler_params=params(),
        cost_estimate=SMALL,
        name="late_moments",
    )(place, *pieces, before, shift, sums, tail, halo, valid)
    return outs[:reps], outs[reps]


def rolled(value, first):
    rows, width = value.shape
    wide = jnp.broadcast_to(value, (8, width)) if rows == 1 else value
    return pltpu.roll(wide, lax.rem(width - first, width), 1)[:rows]


def as_column(row):
    return jnp.broadcast_to(row, (8, row.shape[1])).T[:, 0:1]


def share_kernel(groups, feats, place_ref, *refs):
    parts, outs = refs[: -groups - 1], refs[-groups - 1 :]
    reps, width = len(parts), outs[0].shape[1]
    cols = width // 2
    fold = feats // width
    rows = outs[0].shape[0]
    end = groups * rows
    square = jnp.zeros((1, feats), F32)
    square_next = jnp.zeros((1, cols), F32)
    codes = []
    for part in parts:
        own = part[end : end + 8, :]
        mean = [own[f : f + 1] for f in range(fold)]
        squares = [own[fold + f : fold + f + 1] for f in range(fold)]
        final = own[2 * fold : 2 * fold + 1]
        square += jnp.concatenate(squares, 1)
        square_next += final[:, cols:]
        for line in mean:
            codes += coded(line, MEAN_STEP)
        for line in squares:
            codes += coded(jnp.sqrt(jnp.maximum(line, 0.0)), ROOT_STEP)
        codes += coded(final[:, :cols], MEAN_STEP)
        codes[-2:] = [
            jnp.concatenate(pair, 1)
            for pair in zip(codes[-2:], coded(jnp.sqrt(jnp.maximum(final[:, cols:], 0.0)), ROOT_STEP))
        ]
        codes.append(own[2 * fold + 1 : 2 * fold + 2])
    spare = outs[1].shape[0] - rows - len(codes)
    if spare:
        codes.append(jnp.zeros((spare, width), F32))
    codes = jnp.concatenate(codes, 0).astype(jnp.int32).astype(jnp.int16)
    inverse = lax.rsqrt(jnp.maximum(square, TINY))
    inverse_next = lax.rsqrt(jnp.maximum(square_next, TINY))
    inverse_cols = jnp.concatenate(
        [rolled(inverse, place_ref[1] * cols)[:, :cols], inverse_next], 1
    )
    for s in range(groups):
        there = lax.rem(place_ref[0] + s, groups)
        at = pl.ds(pl.multiple_of(there * rows, rows), rows)
        total = parts[0][at, :]
        for part in parts[1:]:
            total += part[at, :]
        if s == 0:
            outs[0][...] = total
            continue
        first = (there * reps + place_ref[2]) * rows
        ratio = total * as_column(rolled(inverse, first)[:, :rows]) * inverse_cols
        root = jnp.sqrt(jnp.minimum(jnp.abs(ratio), 1.001)) * CODE
        root = jnp.where(ratio < 0.0, -root, root)
        outs[s][0:rows, :] = jnp.round(root).astype(jnp.int32).astype(jnp.int16)
        outs[s][rows:, :] = codes
    outs[groups][...] = codes


def share(parts, place, groups, feats):
    width = parts[0].shape[1]
    rows = (parts[0].shape[0] - 8) // groups
    lines = -(-len(parts) * (4 * (feats // width) + 3) // 16) * 16
    vmem = pl.BlockSpec(memory_space=pltpu.VMEM)
    return pl.pallas_call(
        functools.partial(share_kernel, groups, feats),
        in_specs=[pl.BlockSpec(memory_space=pltpu.SMEM)] + [vmem] * len(parts),
        out_specs=[vmem] * (groups + 1),
        out_shape=[jax.ShapeDtypeStruct((rows, width), F32)]
        + [jax.ShapeDtypeStruct((rows + lines, width), jnp.int16)] * (groups - 1)
        + [jax.ShapeDtypeStruct((lines, width), jnp.int16)],
        compiler_params=params(),
        cost_estimate=SMALL,
        name="share",
    )(place, *parts)


def finish_kernel(reps, place_ref, kept_ref, codes_ref, *refs):
    blocks = refs[:-6]
    shift_ref, early_ref, late_ref, inst_out, lag_out, projections_out = refs[-6:]
    rows, cols = inst_out.shape
    feats = shift_ref.shape[1]
    width = 2 * cols
    fold = feats // width
    count = jnp.zeros((1, 1), F32)
    mean = jnp.zeros((1, feats), F32)
    mean_next = jnp.zeros((1, cols), F32)
    stats = []
    for block in (codes_ref,) + tuple(blocks):
        start = 0 if block is codes_ref else rows
        codes = block[start:, :].astype(jnp.int32).astype(F32)
        at = 0
        for r in range(reps):
            lines = [codes[at + i : at + i + 1] for i in range(4 * fold + 3)]
            at += 4 * fold + 3
            pairs = [(lines[2 * i], lines[2 * i + 1]) for i in range(2 * fold + 1)]
            means = [decoded(*pair, MEAN_STEP) for pair in pairs[:fold]]
            roots = [decoded(*pair, ROOT_STEP) for pair in pairs[fold : 2 * fold]]
            one, two = pairs[2 * fold]
            roots_next = decoded(one[:, cols:], two[:, cols:], ROOT_STEP)
            here = [
                jnp.concatenate(means, 1),
                jnp.concatenate([root * root for root in roots], 1),
                decoded(one[:, :cols], two[:, :cols], MEAN_STEP),
                roots_next * roots_next,
                lines[-1][:, 0:1],
            ]
            stats.append(here)
            count += here[4]
            mean += here[4] * here[0]
            mean_next += here[4] * here[2]
    mean, mean_next = mean / count, mean_next / count
    spread = jnp.zeros((1, feats), F32)
    spread_next = jnp.zeros((1, cols), F32)
    away, away_next = [], []
    for here in stats:
        away.append(here[0] - mean)
        away_next.append(here[2] - mean_next)
        spread += here[1] + here[4] * away[-1] * away[-1]
        spread_next += here[3] + here[4] * away_next[-1] * away_next[-1]
    numbers = jnp.concatenate([here[4] for here in stats], 0)
    scale = 1.0 / jnp.sqrt(spread / count + 1e-05)
    scale_next = 1.0 / jnp.sqrt(spread_next / count + 1e-05)
    away = jnp.concatenate(away, 0)

    first_row = (place_ref[0] * reps + place_ref[2]) * rows
    first_col = place_ref[1] * cols
    right = numbers * jnp.concatenate(
        [rolled(away, first_col)[:, :cols], jnp.concatenate(away_next, 0)], 1
    )
    moment = kept_ref[...] + jnp.dot(
        rolled(away, first_row)[:, :rows].T,
        right,
        precision=lax.Precision.HIGHEST,
        preferred_element_type=F32,
    )
    for g, block in enumerate(blocks):
        here = stats[(g + 1) * reps : (g + 2) * reps]
        root = jnp.sqrt(sum(one[1] for one in here))
        root_next = jnp.sqrt(sum(one[3] for one in here))
        root_rows = as_column(rolled(root, first_row)[:, :rows])
        root_cols = jnp.concatenate([rolled(root, first_col)[:, :cols], root_next], 1)
        code = block[0:rows, :].astype(jnp.int32).astype(F32) * (1.0 / CODE)
        moment += code * jnp.abs(code) * root_rows * root_cols
    scale_cols = rolled(scale, first_col)[:, :cols]
    moment = moment / count * as_column(rolled(scale, first_row)[:, :rows])
    inst_out[...] = moment[:, 0:cols] * scale_cols
    lag_out[...] = moment[:, cols : 2 * cols] * scale_next
    offset = rolled(shift_ref[...] - mean, first_col)[:, :cols]
    split = early_ref.shape[0]
    projections_out[0:split, :] = (early_ref[...] + offset) * scale_cols
    projections_out[split:, :] = (late_ref[...] + offset) * scale_cols


def finish(kept, codes, blocks, shift, early, late, place, reps):
    rows = kept.shape[0]
    cols = early.shape[1]
    frames = early.shape[0] + late.shape[0]
    vmem = pl.BlockSpec(memory_space=pltpu.VMEM)
    return pl.pallas_call(
        functools.partial(finish_kernel, reps),
        in_specs=[pl.BlockSpec(memory_space=pltpu.SMEM)] + [vmem] * (len(blocks) + 5),
        out_specs=[vmem] * 3,
        out_shape=[
            jax.ShapeDtypeStruct((rows, cols), F32),
            jax.ShapeDtypeStruct((rows, cols), F32),
            jax.ShapeDtypeStruct((frames, cols), F32),
        ],
        compiler_params=params(),
        cost_estimate=SMALL,
        name="finish",
    )(place, kept, codes, *blocks, shift, early, late)


def upto(width):
    rows = lax.broadcasted_iota(jnp.int32, (width, width), 0)
    lanes = lax.broadcasted_iota(jnp.int32, (width, width), 1)
    return (lanes <= rows).astype(F32).astype(BF16)


def ranked(pairs, first, width, below):
    atoms = lax.broadcasted_iota(jnp.int32, (width, 128), 0) + first
    hit = jnp.zeros((width, 128), F32)
    for block in pairs:
        for r in range(2):
            for l in range(0, block.shape[1], 128):
                hit = jnp.where(block[r : r + 1, l : l + 128] == atoms, 1.0, hit)
    used = jnp.broadcast_to(jnp.max(hit, axis=1, keepdims=True), (width, 128))
    order = jnp.dot(below, used.astype(BF16), preferred_element_type=F32)
    return jnp.where(used > 0.0, order - 1.0, -1.0), order[width - 1 : width, :]


def signs_kernel(groups, width, cap, place_ref, after_ref, *refs):
    pairs, (signs_out, most_out) = refs[:-2], refs[-2:]
    sides = len(pairs)
    below = upto(width)
    number = lax.broadcasted_iota(jnp.int32, (width, 128), 0) + 1
    high = (number // 8).astype(F32).astype(BF16)
    low = (number % 8).astype(F32).astype(BF16)
    slots = lax.broadcasted_iota(jnp.int32, (cap, width), 0).astype(F32)
    most = jnp.zeros((1, 128), F32)
    for s in range(groups):
        first = lax.rem(place_ref[0] + groups - s, groups) * width
        rank, count = ranked(pairs, first, width, below)
        most = jnp.maximum(most, count)
        chosen = (rank.T[0:1, :] == slots).astype(F32).astype(BF16)
        listed = 8.0 * jnp.dot(chosen, high, preferred_element_type=F32)
        listed += jnp.dot(chosen, low, preferred_element_type=F32)
        listed = listed.astype(jnp.int32) - 1
        listed = jnp.where(listed < 0, -1, listed + first)
        for b, block in enumerate(pairs):
            cols = block.shape[1]
            there = lax.rem(place_ref[1] + sides - b, sides) * cols
            for l in range(0, cols, 128):
                one = (block[0:1, l : l + 128] == listed).astype(F32)
                two = (block[1:2, l : l + 128] == listed).astype(F32)
                at = pl.ds(pl.multiple_of(there + l, 128), 128)
                signs_out[s * cap : (s + 1) * cap, at] = (one - two).astype(BF16)
    most_out[...] = most


def pair_signs(pairs, after, place, groups, width, cap):
    feats = len(pairs) * pairs[0].shape[1]
    vmem = pl.BlockSpec(memory_space=pltpu.VMEM)
    return pl.pallas_call(
        functools.partial(signs_kernel, groups, width, cap),
        in_specs=[pl.BlockSpec(memory_space=pltpu.SMEM), pl.BlockSpec(memory_space=pl.ANY)]
        + [vmem] * len(pairs),
        out_specs=[vmem] * 2,
        out_shape=[
            jax.ShapeDtypeStruct((groups * cap, feats), BF16),
            jax.ShapeDtypeStruct((1, 128), F32),
        ],
        compiler_params=params(),
        cost_estimate=SMALL,
        name="pair_signs",
    )(place, after, *pairs)


def chunk_sizes(frames):
    last = frames // 8 * 3
    return frames - last, last


def with_cap(cap, coords, pairs, traj_ids, place):
    groups, sides = lax.axis_size("atoms"), lax.axis_size("feat")
    atom_index, feat_index = place[0], place[1]
    width = coords.shape[2]
    frames = coords.shape[1] // groups
    cols = pairs[0].shape[1]
    feats = cols * sides
    sizes = chunk_sizes(frames // sides)

    chosen, traj_ids, pairs, picked = first_pick(
        coords, traj_ids, pairs, cap, place, sizes[0], groups
    )
    arrived, start = [], 0
    for j, size in enumerate(sizes):
        if j:
            picked = pick(coords, chosen, arrived[-1][1], place, start, size, groups)
        arrived.append([picked[0]] + [rotated(picked[s], "atoms", s) for s in range(1, groups)])
        start += sides * size

    signs, most_used = pair_signs(pairs, arrived[-1][0], place, groups, width, cap)

    ids = jnp.concatenate([traj_ids[0], jnp.full((LAG,), -1, jnp.int32)])
    offset = atom_index * frames
    ids_now = lax.dynamic_slice_in_dim(ids, offset, frames)
    ids_later = lax.dynamic_slice_in_dim(ids, offset + LAG, frames)
    valid = (ids_now == ids_later).astype(F32)[:, None]

    pieces, after = [], arrived[-1][0]
    for blocks in arrived:
        block, codes = distances(blocks, signs, after)
        after = block
        pieces.append([block] + [rotated(codes, "feat", s) for s in range(1, sides)])

    opening = pieces[0][0][:HALO]
    for s in range(1, sides):
        first = lax.rem(feat_index + sides - s, sides) == 0
        opening = jnp.where(first, decoded_piece(pieces[0][s], HALO), opening)
    opening = lax.dynamic_slice_in_dim(opening, feat_index * cols, cols, 1)
    halo = passed_down(opening, "atoms")

    early = [piece for chunk in pieces[:-1] for piece in chunk]
    before, own_early, shift, sums, tail = early_moments(early, valid, place, sizes[:-1], sides)
    reps = lax.axis_size("rep")
    parts, own_late = late_moments(
        pieces[-1], before, shift, sums, tail, halo, valid, place, sides, groups, reps
    )
    parts = [parts[0]] + [rotated(parts[s], "rep", s) for s in range(1, reps)]
    kept, *blocks, codes = share(parts, place, groups, feats)
    blocks = [rotated(block, "atoms", s + 1) for s, block in enumerate(blocks)]
    corr_inst, corr_lag, projections = finish(
        kept, codes, blocks, shift, own_early, own_late, place, reps
    )
    return (corr_inst, corr_lag, projections[None]), most_used[0, 0]


def shards(atom_coords, atom_pairs, traj_ids):
    place = [lax.axis_index(axis) for axis in ("atoms", "feat", "rep")]
    place = jnp.stack(place).astype(jnp.int32)
    width = atom_coords.shape[3]
    coords = jnp.transpose(atom_coords[0], (1, 0, 2))
    pairs = [atom_pairs] + [rotated(atom_pairs, "feat", s) for s in range(1, lax.axis_size("feat"))]
    cap = min(width, -(-(width * 9 // 16) // 64) * 64)
    outs, most_used = with_cap(cap, coords, pairs, traj_ids, place)

    def again(carry):
        same = [block + (carry[0] - 1) for block in pairs]
        return carry[0] - 1, with_cap(width, coords, same, traj_ids, place)[0]

    overflow = (most_used > cap).astype(jnp.int32)
    return lax.while_loop(lambda carry: carry[0] > 0, again, (overflow, outs))[1]


def solution(mesh):
    placed = (P(("grp", "rep"), None, None, "atoms"), P(None, "feat"), P(("grp", "rep"), None))
    return jax.shard_map(
        shards,
        mesh=mesh,
        in_specs=placed,
        out_specs=(
            P(("grp", "atoms", "rep"), "feat"),
            P(("grp", "atoms", "rep"), "feat"),
            P(("grp", "rep"), "atoms", "feat"),
        ),
        check_vma=False,
    )
```

```python
import functools

import jax
import jax.numpy as jnp
from jax import lax
from jax.experimental import pallas as pl
from jax.experimental.pallas import tpu as pltpu
from jax.sharding import PartitionSpec as P

LAG = 10
HALO = 16
CHUNK = 64
CODE = 32700.0
FINE = 60000.0
MEAN_STEP = 0.001
ROOT_STEP = 0.02
TINY = 1e-30
REACH = 1e-6
VMEM_LIMIT = 32 * 1024 * 1024
F32 = jnp.float32
BF16 = jnp.bfloat16
LARGE = pl.CostEstimate(flops=10**11, bytes_accessed=1024, transcendentals=0)
SMALL = pl.CostEstimate(flops=1024, bytes_accessed=1024, transcendentals=0)


def rotated(block, axis, shift):
    size = lax.axis_size(axis)
    return lax.ppermute(block, axis, [(i, (i + shift) % size) for i in range(size)])


def passed_down(block, axis):
    return lax.ppermute(block, axis, [(i + 1, i) for i in range(lax.axis_size(axis) - 1)])


def params():
    return pltpu.CompilerParams(vmem_limit_bytes=VMEM_LIMIT)


def start_rows(sizes, start, place_ref, coords_ref, rows_refs, sems):
    groups, sides = rows_refs[0].shape[0], lax.axis_size("feat")
    frames = coords_ref.shape[1] // groups
    copies = []
    for j, size in enumerate(sizes):
        for s in range(groups):
            there = lax.rem(place_ref[0] + s, groups)
            row = there * frames + place_ref[1] * (frames // sides) + start
            copies.append(
                pltpu.make_async_copy(
                    coords_ref.at[:, pl.ds(pl.multiple_of(row, HALO), size), :],
                    rows_refs[j].at[s],
                    sems.at[j, s],
                )
            )
        start += size
    for copy in copies:
        copy.start()
    return copies


def packed(cap):
    return -(-3 * cap // 128) * 128


def pick_rows(rows, chosen, out):
    _, size, width = rows.shape
    cap = chosen.shape[1]
    picked = jnp.dot(
        rows[...].reshape(3 * size, width), chosen, preferred_element_type=F32
    ).astype(BF16)
    for k in range(3):
        out[:, k * cap : (k + 1) * cap] = picked[k * size : (k + 1) * size, :]
    if out.shape[1] > 3 * cap:
        out[:, 3 * cap :] = jnp.zeros((size, out.shape[1] - 3 * cap), BF16)


def first_pick_kernel(sides, place_ref, coords_ref, ids_ref, *refs):
    pairs, refs = refs[:sides], refs[sides:]
    chosen_ref, ids_out, pairs_out, refs = refs[0], refs[1], refs[2 : 2 + sides], refs[2 + sides :]
    outs, rows_ref, sems = refs[:-2], refs[-2], refs[-1]
    width, cap = chosen_ref.shape
    copies = start_rows((rows_ref.shape[2],), 0, place_ref, coords_ref, [rows_ref], sems)
    ids_out[...] = ids_ref[...]
    for block, copy in zip(pairs, pairs_out):
        copy[...] = block[...]
    rank, _ = ranked(pairs, place_ref[0] * width, width, upto(width))
    lanes = lax.broadcasted_iota(jnp.int32, (width, 128), 1)
    for l in range(0, cap, 128):
        some = min(128, cap - l)
        here = (rank == (lanes + l).astype(F32)).astype(F32).astype(BF16)
        chosen_ref[:, l : l + some] = here[:, :some]
    for s, out in enumerate(outs):
        copies[s].wait()
        pick_rows(rows_ref.at[s], chosen_ref[...], out)


def first_pick(coords, ids, pairs, cap, place, size, groups):
    width = coords.shape[2]
    vmem = pl.BlockSpec(memory_space=pltpu.VMEM)
    outs = pl.pallas_call(
        functools.partial(first_pick_kernel, len(pairs)),
        in_specs=[
            pl.BlockSpec(memory_space=pltpu.SMEM),
            pl.BlockSpec(memory_space=pltpu.HBM),
        ]
        + [vmem] * (len(pairs) + 1),
        out_specs=[vmem] * (2 + len(pairs) + groups),
        out_shape=[
            jax.ShapeDtypeStruct((width, cap), BF16),
            jax.ShapeDtypeStruct(ids.shape, ids.dtype),
        ]
        + [jax.ShapeDtypeStruct(block.shape, block.dtype) for block in pairs]
        + [jax.ShapeDtypeStruct((size, packed(cap)), BF16)] * groups,
        scratch_shapes=[
            pltpu.VMEM((groups, 3, size, width), BF16),
            pltpu.SemaphoreType.DMA((1, groups)),
        ],
        compiler_params=params(),
        cost_estimate=SMALL,
        name="first_pick",
    )(place, coords, ids, *pairs)
    sides = len(pairs)
    return outs[0], outs[1], outs[2 : 2 + sides], outs[2 + sides :]


def pick_kernel(start, place_ref, coords_ref, chosen_ref, after_ref, *refs):
    outs, rows_ref, sems = refs[:-2], refs[-2], refs[-1]
    copies = start_rows((rows_ref.shape[2],), start, place_ref, coords_ref, [rows_ref], sems)
    for s, out in enumerate(outs):
        copies[s].wait()
        pick_rows(rows_ref.at[s], chosen_ref[...], out)


def pick(coords, chosen, after, place, start, size, groups):
    width, cap = chosen.shape
    vmem = pl.BlockSpec(memory_space=pltpu.VMEM)
    return pl.pallas_call(
        functools.partial(pick_kernel, start),
        in_specs=[
            pl.BlockSpec(memory_space=pltpu.SMEM),
            pl.BlockSpec(memory_space=pltpu.HBM),
            vmem,
            pl.BlockSpec(memory_space=pl.ANY),
        ],
        out_specs=[vmem] * groups,
        out_shape=[jax.ShapeDtypeStruct((size, packed(cap)), BF16)] * groups,
        scratch_shapes=[
            pltpu.VMEM((groups, 3, size, width), BF16),
            pltpu.SemaphoreType.DMA((1, groups)),
        ],
        compiler_params=params(),
        cost_estimate=SMALL,
        name="pick",
    )(place, coords, chosen, after)


def coded(value, step):
    first = jnp.round(value / step)
    second = jnp.round((value - first * step) * (FINE / step))
    return [first, second]


def decoded(first, second, step):
    return first * step + second * (step / FINE)


def decoded_piece(codes, rows):
    size = codes.shape[0] - HALO
    ends = codes[size:, :].astype(jnp.int32).astype(F32)
    middle = decoded(ends[0:1], ends[1:2], MEAN_STEP)
    reach = decoded(ends[2:3], ends[3:4], MEAN_STEP)
    return middle + codes[0:rows, :].astype(jnp.int32).astype(F32) * (reach * (1.0 / CODE))


def distance_kernel(*refs):
    blocks, (signs_ref, after_ref, out, codes_out, joined) = refs[:-5], refs[-5:]
    size = blocks[0].shape[0]
    cap = signs_ref.shape[0] // len(blocks)
    for s, block in enumerate(blocks):
        for k in range(3):
            joined[k * size : (k + 1) * size, s * cap : (s + 1) * cap] = block[
                :, k * cap : (k + 1) * cap
            ]
    delta = jnp.dot(joined[...], signs_ref[...], preferred_element_type=F32)
    square = delta * delta
    total = square[:size] + square[size : 2 * size] + square[2 * size :]
    value = jnp.sqrt(total + 0.01)
    out[...] = value
    least, most = jnp.min(value, 0, keepdims=True), jnp.max(value, 0, keepdims=True)
    ends = coded(0.5 * (most + least), MEAN_STEP) + coded(0.5 * (most - least), MEAN_STEP)
    middle = decoded(ends[0], ends[1], MEAN_STEP)
    reach = decoded(ends[2], ends[3], MEAN_STEP)
    ratio = (value - middle) * (CODE / jnp.maximum(reach, REACH))
    ratio = jnp.round(jnp.clip(ratio, -32767.0, 32767.0))
    codes_out[0:size, :] = ratio.astype(jnp.int32).astype(jnp.int16)
    ends = jnp.concatenate(ends + [jnp.zeros((HALO - 4, out.shape[1]), F32)], 0)
    codes_out[size:, :] = ends.astype(jnp.int32).astype(jnp.int16)


def distances(blocks, signs, after):
    size = blocks[0].shape[0]
    vmem = pl.BlockSpec(memory_space=pltpu.VMEM)
    return pl.pallas_call(
        distance_kernel,
        in_specs=[vmem] * (len(blocks) + 1) + [pl.BlockSpec(memory_space=pl.ANY)],
        out_specs=[vmem] * 2,
        out_shape=[
            jax.ShapeDtypeStruct((size, signs.shape[1]), F32),
            jax.ShapeDtypeStruct((size + HALO, signs.shape[1]), jnp.int16),
        ],
        scratch_shapes=[pltpu.VMEM((3 * size, signs.shape[0]), BF16)],
        compiler_params=params(),
        cost_estimate=LARGE,
        name="distances",
    )(*blocks, signs, after)


def split_in_two(value):
    high = value.astype(BF16)
    return high, (value - high.astype(F32)).astype(BF16)


def product(left, right):
    left_high, left_low = split_in_two(left)
    right_high, right_low = split_in_two(right)
    left_high, left_low = left_high.T, left_low.T
    total = jnp.dot(left_high, right_high, preferred_element_type=F32)
    total += jnp.dot(left_high, right_low, preferred_element_type=F32)
    return total + jnp.dot(left_low, right_high, preferred_element_type=F32)


def row_sum(value):
    return jnp.sum(value, 0, keepdims=True)


def side_columns(side, sides, cols, write):
    for s in range(sides):

        @pl.when(side == s)
        def _():
            write(slice(s * cols, (s + 1) * cols))


def early_kernel(chunks, sides, place_ref, *refs):
    pieces = refs[:chunks]
    valid_ref, out, own_out, shift_out, sums_out, tail_out, every = refs[chunks:]
    frames = every.shape[0]
    cols = own_out.shape[1]
    row = 0
    for piece in pieces:
        every[row : row + piece.shape[0], :] = piece[...]
        row += piece.shape[0]
    side = place_ref[1]
    valid = valid_ref[pl.ds(pl.multiple_of(side * frames, HALO), frames), :]
    count = jnp.maximum(jnp.sum(valid), 1.0)
    shift = row_sum(valid * every[...]) / count
    shift_out[...] = shift
    every[...] = every[...] - shift
    tail_out[...] = every[frames - HALO : frames, :]

    def keep_own(part):
        own_out[...] = every[:, part]

    side_columns(side, sides, cols, keep_own)
    now = every[...]
    own = own_out[...]
    weighed = valid * now
    later = own[LAG:frames, :]
    weighed_later = valid[: frames - LAG] * later
    sums_out[0:1, :] = row_sum(weighed)
    sums_out[1:2, :] = row_sum(weighed * now)
    sums_out[2:3, 0:cols] = row_sum(weighed_later)
    sums_out[3:4, 0:cols] = row_sum(weighed_later * later)
    weighed_later = jnp.concatenate([weighed_later, jnp.zeros((LAG, cols), F32)], 0)
    out[...] = product(now, jnp.concatenate([valid * own, weighed_later], 1))


def early_moments(pieces, valid, place, sides):
    frames, feats = sum(piece.shape[0] for piece in pieces), pieces[0].shape[1]
    cols = feats // sides
    vmem = pl.BlockSpec(memory_space=pltpu.VMEM)
    return pl.pallas_call(
        functools.partial(early_kernel, len(pieces), sides),
        in_specs=[pl.BlockSpec(memory_space=pltpu.SMEM)] + [vmem] * (len(pieces) + 1),
        out_specs=[vmem] * 5,
        out_shape=[
            jax.ShapeDtypeStruct((feats, 2 * cols), F32),
            jax.ShapeDtypeStruct((frames, cols), F32),
            jax.ShapeDtypeStruct((1, feats), F32),
            jax.ShapeDtypeStruct((4, feats), F32),
            jax.ShapeDtypeStruct((HALO, feats), F32),
        ],
        scratch_shapes=[pltpu.VMEM((frames, feats), F32)],
        compiler_params=params(),
        cost_estimate=SMALL,
        name="early_moments",
    )(place, *pieces, valid)


def add_blocks(place_ref, shifts, groups, before_ref, left_refs, right_refs, outs):
    reps = len(outs)
    rows = before_ref.shape[0] // (groups * reps)
    left_high, left_low = left_refs
    right_high, right_low = right_refs[0][...], right_refs[1][...]
    for r in reversed(range(reps)):
        rep = lax.rem(place_ref[2] + r, reps)
        for i, s in enumerate(shifts):
            there = lax.rem(place_ref[0] + s, groups)
            at = pl.ds(pl.multiple_of((there * reps + rep) * rows, rows), rows)
            part = before_ref[at, :]
            part += jnp.dot(left_high[at, :], right_high, preferred_element_type=F32)
            part += jnp.dot(left_high[at, :], right_low, preferred_element_type=F32)
            part += jnp.dot(left_low[at, :], right_high, preferred_element_type=F32)
            outs[r][i * rows : (i + 1) * rows, :] = part


def late_kernel(sizes, sides, groups, reps, shifts, place_ref, *refs):
    chunks = len(sizes)
    codes = refs[: chunks * (sides - 1)]
    refs = refs[chunks * (sides - 1) :]
    before_ref, shift_ref, sums_ref, tail_ref, own_ref, halo_ref, valid_ref = refs[:7]
    outs = refs[7 : 7 + reps]
    own_out, left_high, left_low, right_high, right_low, left, right, own = refs[7 + reps :]
    here, cols = own_ref.shape
    frames, feats = here * sides, shift_ref.shape[1]
    side = place_ref[1]
    shift = shift_ref[...]
    bases = [pl.multiple_of(lax.rem(side + sides - s, sides) * here, HALO) for s in range(sides)]
    left[0:HALO, :] = tail_ref[...]
    row = HALO
    for s in range(1, sides):
        for j, size in enumerate(sizes):
            left[row : row + size, :] = decoded_piece(codes[j * (sides - 1) + s - 1], size) - shift
            row += size
    own[pl.ds(bases[0], here), :] = own_ref[...]

    def keep_own(part):
        own[frames:, :] = halo_ref[...] - shift[:, part]
        for s in range(1, sides):
            rows = slice(HALO + (s - 1) * here, HALO + s * here)
            own[pl.ds(bases[s], here), :] = left[rows, part]

    side_columns(side, sides, cols, keep_own)
    own_out[...] = own[0:frames, :]
    valid_all = valid_ref[...]
    total = jnp.sum(valid_all)
    count = jnp.maximum(total, 1.0)
    sums, squares = sums_ref[0:1, :], sums_ref[1:2, :]
    sums_next, squares_next = sums_ref[2:3, 0:cols], sums_ref[3:4, 0:cols]
    end = bases[0] + here - HALO
    later = own[pl.ds(pl.multiple_of(end, HALO), 2 * HALO), :][LAG : LAG + HALO]
    crossing = lax.broadcasted_iota(jnp.int32, (HALO, 1), 0) >= HALO - LAG
    valid = valid_ref[pl.ds(pl.multiple_of(end, HALO), HALO), :]
    weighed_later = jnp.where(crossing, valid * later, 0.0)
    sums_next += row_sum(weighed_later)
    squares_next += row_sum(weighed_later * later)
    right[0:HALO, 0:cols] = jnp.zeros((HALO, cols), F32)
    right[0:HALO, cols : 2 * cols] = weighed_later
    for s in range(1, sides):
        rows = slice(HALO + (s - 1) * here, HALO + s * here)
        valid = valid_ref[pl.ds(bases[s], here), :]
        weighed = valid * left[rows, :]
        sums += row_sum(weighed)
        squares += row_sum(weighed * left[rows, :])
        around = own[pl.ds(bases[s], here + HALO), :]
        right[rows, 0:cols] = valid * around[0:here]
        later = around[LAG : LAG + here]
        weighed_later = valid * later
        right[rows, cols : 2 * cols] = weighed_later
        sums_next += row_sum(weighed_later)
        squares_next += row_sum(weighed_later * later)
    own_sums = jnp.zeros((1, cols), F32)
    own_shift = jnp.zeros((1, cols), F32)
    for s in range(sides):
        mine = (side == s).astype(F32)
        own_sums += mine * sums[:, s * cols : (s + 1) * cols]
        own_shift += mine * shift[:, s * cols : (s + 1) * cols]
    first = lax.broadcasted_iota(jnp.int32, (HALO, 1), 0) == 0
    last = left.shape[0] - HALO
    left[last:, :] = jnp.where(first, sums, 0.0)
    right[last:, 0:cols] = jnp.where(first, -own_sums / count, 0.0)
    right[last:, cols : 2 * cols] = jnp.where(first, -sums_next / count, 0.0)
    high, low = split_in_two(left[...])
    left_high[...] = high.T
    left_low[...] = low.T
    right_high[...], right_low[...] = split_in_two(right[...])
    add_blocks(
        place_ref, shifts, groups, before_ref, (left_high, left_low), (right_high, right_low), outs
    )
    fold = feats // (2 * cols)
    mean, square = shift + sums / count, squares - sums * sums / count
    for out in outs:
        end = out.shape[0] - 8
        for f in range(fold):
            part = slice(2 * cols * f, 2 * cols * (f + 1))
            out[end + f : end + f + 1, :] = mean[:, part]
            out[end + fold + f : end + fold + f + 1, :] = square[:, part]
        end += 2 * fold
        out[end : end + 1, 0:cols] = own_shift + sums_next / count
        out[end : end + 1, cols : 2 * cols] = squares_next - sums_next * sums_next / count
        out[end + 1 : end + 2, :] = jnp.zeros((1, 2 * cols), F32) + total
        spare = out.shape[0] - end - 2
        if spare:
            out[end + 2 :, :] = jnp.zeros((spare, 2 * cols), F32)


def late_moments(codes, before, shift, sums, tail, own, halo, valid, place, sides, groups, reps, shifts):
    sizes = tuple(chunk[0].shape[0] - HALO for chunk in codes)
    codes = [code for chunk in codes for code in chunk]
    here, cols = own.shape
    feats = shift.shape[1]
    depth = here * (sides - 1) + 2 * HALO
    rows = feats // (groups * reps)
    vmem = pl.BlockSpec(memory_space=pltpu.VMEM)
    outs = pl.pallas_call(
        functools.partial(late_kernel, sizes, sides, groups, reps, shifts),
        in_specs=[pl.BlockSpec(memory_space=pltpu.SMEM)] + [vmem] * (len(codes) + 7),
        out_specs=[vmem] * (reps + 5),
        out_shape=[jax.ShapeDtypeStruct((len(shifts) * rows + 8, 2 * cols), F32)] * reps
        + [
            jax.ShapeDtypeStruct((here * sides, cols), F32),
            jax.ShapeDtypeStruct((feats, depth), BF16),
            jax.ShapeDtypeStruct((feats, depth), BF16),
            jax.ShapeDtypeStruct((depth, 2 * cols), BF16),
            jax.ShapeDtypeStruct((depth, 2 * cols), BF16),
        ],
        scratch_shapes=[
            pltpu.VMEM((depth, feats), F32),
            pltpu.VMEM((depth, 2 * cols), F32),
            pltpu.VMEM((here * sides + HALO, cols), F32),
        ],
        compiler_params=params(),
        cost_estimate=SMALL,
        name="late_moments",
    )(place, *codes, before, shift, sums, tail, own, halo, valid)
    return outs[:reps], outs[reps], outs[reps + 1 :]


def rest_kernel(groups, shifts, place_ref, before_ref, left_high, left_low, right_high, right_low, *outs):
    add_blocks(
        place_ref, shifts, groups, before_ref, (left_high, left_low), (right_high, right_low), outs
    )


def rest_moments(before, factors, place, groups, reps, shifts):
    rows = before.shape[0] // (groups * reps)
    vmem = pl.BlockSpec(memory_space=pltpu.VMEM)
    return pl.pallas_call(
        functools.partial(rest_kernel, groups, shifts),
        in_specs=[pl.BlockSpec(memory_space=pltpu.SMEM)] + [vmem] * 5,
        out_specs=[vmem] * reps,
        out_shape=[jax.ShapeDtypeStruct((len(shifts) * rows, before.shape[1]), F32)] * reps,
        compiler_params=params(),
        cost_estimate=SMALL,
        name="rest_moments",
    )(place, before, *factors)


def rolled(value, first):
    rows, width = value.shape
    wide = jnp.broadcast_to(value, (8, width)) if rows == 1 else value
    return pltpu.roll(wide, lax.rem(width - first, width), 1)[:rows]


def as_column(row):
    return jnp.broadcast_to(row, (8, row.shape[1])).T[:, 0:1]


def code_block(place_ref, groups, reps, s, i, parts, norms, out):
    width = parts[0].shape[1]
    cols = width // 2
    feats = norms.shape[1]
    rows = feats // (groups * reps)
    at = slice(i * rows, (i + 1) * rows)
    total = parts[0][at, :]
    for part in parts[1:]:
        total += part[at, :]
    if s == 0:
        out[...] = total
        return
    there = lax.rem(place_ref[0] + s, groups)
    first = (there * reps + place_ref[2]) * rows
    inverse_cols = jnp.concatenate(
        [rolled(norms[0:1, :], place_ref[1] * cols)[:, :cols], norms[1:2, :cols]], 1
    )
    ratio = total * as_column(rolled(norms[0:1, :], first)[:, :rows]) * inverse_cols
    root = jnp.sqrt(jnp.minimum(jnp.abs(ratio), 1.001)) * CODE
    root = jnp.where(ratio < 0.0, -root, root)
    out[0:rows, :] = jnp.round(root).astype(jnp.int32).astype(jnp.int16)


def first_share_kernel(groups, shifts, place_ref, *refs):
    count = len(shifts)
    parts, outs, codes_out, norms_out = refs[: -count - 2], refs[-count - 2 : -2], refs[-2], refs[-1]
    reps, width = len(parts), parts[0].shape[1]
    cols, feats = width // 2, norms_out.shape[1]
    fold = feats // width
    end = parts[0].shape[0] - 8
    square = jnp.zeros((1, feats), F32)
    square_next = jnp.zeros((1, cols), F32)
    codes = []
    for part in parts:
        own = part[end : end + 8, :]
        squares = [own[fold + f : fold + f + 1] for f in range(fold)]
        final = own[2 * fold : 2 * fold + 1]
        square += jnp.concatenate(squares, 1)
        square_next += final[:, cols:]
        for f in range(fold):
            codes += coded(own[f : f + 1], MEAN_STEP)
        for line in squares:
            codes += coded(jnp.sqrt(jnp.maximum(line, 0.0)), ROOT_STEP)
        pair = coded(final[:, :cols], MEAN_STEP)
        pair_next = coded(jnp.sqrt(jnp.maximum(final[:, cols:], 0.0)), ROOT_STEP)
        codes += [jnp.concatenate(both, 1) for both in zip(pair, pair_next)]
        codes.append(own[2 * fold + 1 : 2 * fold + 2])
    spare = codes_out.shape[0] - len(codes)
    if spare:
        codes.append(jnp.zeros((spare, width), F32))
    codes = jnp.concatenate(codes, 0).astype(jnp.int32).astype(jnp.int16)
    codes_out[...] = codes
    norms_out[...] = jnp.zeros(norms_out.shape, F32)
    norms_out[0:1, :] = lax.rsqrt(jnp.maximum(square, TINY))
    norms_out[1:2, :cols] = lax.rsqrt(jnp.maximum(square_next, TINY))
    for i, (s, out) in enumerate(zip(shifts, outs)):
        code_block(place_ref, groups, reps, s, i, parts, norms_out, out)
        out[out.shape[0] - codes.shape[0] :, :] = codes


def rest_share_kernel(groups, shifts, place_ref, norms_ref, codes_ref, *refs):
    count = len(shifts)
    parts, outs = refs[:-count], refs[-count:]
    for i, (s, out) in enumerate(zip(shifts, outs)):
        code_block(place_ref, groups, len(parts), s, i, parts, norms_ref, out)
        if s:
            out[out.shape[0] - codes_ref.shape[0] :, :] = codes_ref[...]


def first_share(parts, place, groups, shifts, feats):
    width, reps = parts[0].shape[1], len(parts)
    rows = feats // (groups * reps)
    lines = -(-reps * (4 * (feats // width) + 3) // 16) * 16
    vmem = pl.BlockSpec(memory_space=pltpu.VMEM)
    outs = pl.pallas_call(
        functools.partial(first_share_kernel, groups, shifts),
        in_specs=[pl.BlockSpec(memory_space=pltpu.SMEM)] + [vmem] * reps,
        out_specs=[vmem] * (len(shifts) + 2),
        out_shape=[jax.ShapeDtypeStruct((rows + lines, width), jnp.int16)] * len(shifts)
        + [
            jax.ShapeDtypeStruct((lines, width), jnp.int16),
            jax.ShapeDtypeStruct((8, feats), F32),
        ],
        compiler_params=params(),
        cost_estimate=SMALL,
        name="first_share",
    )(place, *parts)
    return outs[:-2], outs[-2], outs[-1]


def rest_share(parts, norms, codes, place, groups, shifts):
    width = parts[0].shape[1]
    rows = parts[0].shape[0] // len(shifts)
    coded_shape = jax.ShapeDtypeStruct((rows + codes.shape[0], width), jnp.int16)
    vmem = pl.BlockSpec(memory_space=pltpu.VMEM)
    return pl.pallas_call(
        functools.partial(rest_share_kernel, groups, shifts),
        in_specs=[pl.BlockSpec(memory_space=pltpu.SMEM)] + [vmem] * (len(parts) + 2),
        out_specs=[vmem] * len(shifts),
        out_shape=[coded_shape if s else jax.ShapeDtypeStruct((rows, width), F32) for s in shifts],
        compiler_params=params(),
        cost_estimate=SMALL,
        name="rest_share",
    )(place, norms, codes, *parts)


def finish_kernel(reps, place_ref, kept_ref, codes_ref, *refs):
    blocks = refs[:-5]
    shift_ref, own_ref, inst_out, lag_out, projections_out = refs[-5:]
    rows, cols = inst_out.shape
    feats = shift_ref.shape[1]
    width = 2 * cols
    fold = feats // width
    count = jnp.zeros((1, 1), F32)
    mean = jnp.zeros((1, feats), F32)
    mean_next = jnp.zeros((1, cols), F32)
    stats = []
    for block in (codes_ref,) + tuple(blocks):
        start = 0 if block is codes_ref else rows
        codes = block[start:, :].astype(jnp.int32).astype(F32)
        at = 0
        for r in range(reps):
            lines = [codes[at + i : at + i + 1] for i in range(4 * fold + 3)]
            at += 4 * fold + 3
            pairs = [(lines[2 * i], lines[2 * i + 1]) for i in range(2 * fold + 1)]
            means = [decoded(*pair, MEAN_STEP) for pair in pairs[:fold]]
            roots = [decoded(*pair, ROOT_STEP) for pair in pairs[fold : 2 * fold]]
            one, two = pairs[2 * fold]
            roots_next = decoded(one[:, cols:], two[:, cols:], ROOT_STEP)
            here = [
                jnp.concatenate(means, 1),
                jnp.concatenate([root * root for root in roots], 1),
                decoded(one[:, :cols], two[:, :cols], MEAN_STEP),
                roots_next * roots_next,
                lines[-1][:, 0:1],
            ]
            stats.append(here)
            count += here[4]
            mean += here[4] * here[0]
            mean_next += here[4] * here[2]
    mean, mean_next = mean / count, mean_next / count
    spread = jnp.zeros((1, feats), F32)
    spread_next = jnp.zeros((1, cols), F32)
    away, away_next = [], []
    for here in stats:
        away.append(here[0] - mean)
        away_next.append(here[2] - mean_next)
        spread += here[1] + here[4] * away[-1] * away[-1]
        spread_next += here[3] + here[4] * away_next[-1] * away_next[-1]
    numbers = jnp.concatenate([here[4] for here in stats], 0)
    scale = 1.0 / jnp.sqrt(spread / count + 1e-05)
    scale_next = 1.0 / jnp.sqrt(spread_next / count + 1e-05)
    away = jnp.concatenate(away, 0)

    first_row = (place_ref[0] * reps + place_ref[2]) * rows
    first_col = place_ref[1] * cols
    right = numbers * jnp.concatenate(
        [rolled(away, first_col)[:, :cols], jnp.concatenate(away_next, 0)], 1
    )
    moment = kept_ref[...] + jnp.dot(
        rolled(away, first_row)[:, :rows].T,
        right,
        precision=lax.Precision.HIGHEST,
        preferred_element_type=F32,
    )
    for g, block in enumerate(blocks):
        here = stats[(g + 1) * reps : (g + 2) * reps]
        root = jnp.sqrt(sum(one[1] for one in here))
        root_next = jnp.sqrt(sum(one[3] for one in here))
        root_rows = as_column(rolled(root, first_row)[:, :rows])
        root_cols = jnp.concatenate([rolled(root, first_col)[:, :cols], root_next], 1)
        code = block[0:rows, :].astype(jnp.int32).astype(F32) * (1.0 / CODE)
        moment += code * jnp.abs(code) * root_rows * root_cols
    scale_cols = rolled(scale, first_col)[:, :cols]
    moment = moment / count * as_column(rolled(scale, first_row)[:, :rows])
    inst_out[...] = moment[:, 0:cols] * scale_cols
    lag_out[...] = moment[:, cols : 2 * cols] * scale_next
    offset = rolled(shift_ref[...] - mean, first_col)[:, :cols]
    projections_out[...] = (own_ref[...] + offset) * scale_cols


def finish(kept, codes, blocks, shift, own, place, reps):
    rows = kept.shape[0]
    frames, cols = own.shape
    vmem = pl.BlockSpec(memory_space=pltpu.VMEM)
    return pl.pallas_call(
        functools.partial(finish_kernel, reps),
        in_specs=[pl.BlockSpec(memory_space=pltpu.SMEM)] + [vmem] * (len(blocks) + 4),
        out_specs=[vmem] * 3,
        out_shape=[
            jax.ShapeDtypeStruct((rows, cols), F32),
            jax.ShapeDtypeStruct((rows, cols), F32),
            jax.ShapeDtypeStruct((frames, cols), F32),
        ],
        compiler_params=params(),
        cost_estimate=SMALL,
        name="finish",
    )(place, kept, codes, *blocks, shift, own)


def upto(width):
    rows = lax.broadcasted_iota(jnp.int32, (width, width), 0)
    lanes = lax.broadcasted_iota(jnp.int32, (width, width), 1)
    return (lanes <= rows).astype(F32).astype(BF16)


def ranked(pairs, first, width, below):
    atoms = lax.broadcasted_iota(jnp.int32, (width, 128), 0) + first
    hit = jnp.zeros((width, 128), F32)
    for block in pairs:
        for r in range(2):
            for l in range(0, block.shape[1], 128):
                hit = jnp.where(block[r : r + 1, l : l + 128] == atoms, 1.0, hit)
    used = jnp.broadcast_to(jnp.max(hit, axis=1, keepdims=True), (width, 128))
    order = jnp.dot(below, used.astype(BF16), preferred_element_type=F32)
    return jnp.where(used > 0.0, order - 1.0, -1.0), order[width - 1 : width, :]


def signs_kernel(groups, width, cap, place_ref, after_ref, *refs):
    pairs, (signs_out, most_out) = refs[:-2], refs[-2:]
    sides = len(pairs)
    below = upto(width)
    number = lax.broadcasted_iota(jnp.int32, (width, 128), 0) + 1
    high = (number // 8).astype(F32).astype(BF16)
    low = (number % 8).astype(F32).astype(BF16)
    slots = lax.broadcasted_iota(jnp.int32, (cap, width), 0).astype(F32)
    most = jnp.zeros((1, 128), F32)
    for s in range(groups):
        first = lax.rem(place_ref[0] + groups - s, groups) * width
        rank, count = ranked(pairs, first, width, below)
        most = jnp.maximum(most, count)
        chosen = (rank.T[0:1, :] == slots).astype(F32).astype(BF16)
        listed = 8.0 * jnp.dot(chosen, high, preferred_element_type=F32)
        listed += jnp.dot(chosen, low, preferred_element_type=F32)
        listed = listed.astype(jnp.int32) - 1
        listed = jnp.where(listed < 0, -1, listed + first)
        for b, block in enumerate(pairs):
            cols = block.shape[1]
            there = lax.rem(place_ref[1] + sides - b, sides) * cols
            for l in range(0, cols, 128):
                one = (block[0:1, l : l + 128] == listed).astype(F32)
                two = (block[1:2, l : l + 128] == listed).astype(F32)
                at = pl.ds(pl.multiple_of(there + l, 128), 128)
                signs_out[s * cap : (s + 1) * cap, at] = (one - two).astype(BF16)
    most_out[...] = most


def pair_signs(pairs, after, place, groups, width, cap):
    feats = len(pairs) * pairs[0].shape[1]
    vmem = pl.BlockSpec(memory_space=pltpu.VMEM)
    return pl.pallas_call(
        functools.partial(signs_kernel, groups, width, cap),
        in_specs=[pl.BlockSpec(memory_space=pltpu.SMEM), pl.BlockSpec(memory_space=pl.ANY)]
        + [vmem] * len(pairs),
        out_specs=[vmem] * 2,
        out_shape=[
            jax.ShapeDtypeStruct((groups * cap, feats), BF16),
            jax.ShapeDtypeStruct((1, 128), F32),
        ],
        compiler_params=params(),
        cost_estimate=LARGE,
        name="pair_signs",
    )(place, after, *pairs)


def chunk_sizes(frames):
    last = frames // 8 * 3
    return frames - last, last


def with_cap(cap, coords, pairs, traj_ids, place):
    groups, sides = lax.axis_size("atoms"), lax.axis_size("feat")
    atom_index, feat_index = place[0], place[1]
    width = coords.shape[2]
    frames = coords.shape[1] // groups
    cols = pairs[0].shape[1]
    feats = cols * sides
    sizes = chunk_sizes(frames // sides)

    chosen, traj_ids, pairs, picked = first_pick(
        coords, traj_ids, pairs, cap, place, sizes[0], groups
    )
    arrived, start = [], 0
    for j, size in enumerate(sizes):
        if j:
            picked = pick(coords, chosen, arrived[-1][1], place, start, size, groups)
        arrived.append([picked[0]] + [rotated(picked[s], "atoms", s) for s in range(1, groups)])
        start += size

    signs, most_used = pair_signs(pairs, arrived[0][0], place, groups, width, cap)

    ids = jnp.concatenate([traj_ids[0], jnp.full((LAG,), -1, jnp.int32)])
    offset = atom_index * frames
    ids_now = lax.dynamic_slice_in_dim(ids, offset, frames)
    ids_later = lax.dynamic_slice_in_dim(ids, offset + LAG, frames)
    valid = (ids_now == ids_later).astype(F32)[:, None]

    own_pieces, codes, after = [], [], arrived[-1][0]
    for j, blocks in enumerate(arrived):
        block, code = distances(blocks, signs, after)
        after = block
        own_pieces.append(block)
        codes.append([rotated(code, "feat", s) for s in range(1, sides)])
        if j == 0:
            opening = passed_down(block[:HALO], "atoms")
    halo = lax.dynamic_slice_in_dim(opening, feat_index * cols, cols, 1)
    for s in range(1, sides):
        there = lax.rem(feat_index + s, sides)
        sent = rotated(lax.dynamic_slice_in_dim(opening, there * cols, cols, 1), "feat", s)
        halo = jnp.where(feat_index == s, sent, halo)

    reps = lax.axis_size("rep")
    shifts = list(range(1, groups)) + [0]
    shifts = tuple(shifts[: groups // 2]), tuple(shifts[groups // 2 :])
    before, own, shift, sums, tail = early_moments(own_pieces, valid, place, sides)
    parts, own, factors = late_moments(
        codes, before, shift, sums, tail, own, halo, valid, place, sides, groups, reps, shifts[0]
    )
    parts = [parts[0]] + [rotated(parts[r], "rep", r) for r in range(1, reps)]
    rest = rest_moments(before, factors, place, groups, reps, shifts[1])
    rest = [rest[0]] + [rotated(rest[r], "rep", r) for r in range(1, reps)]
    blocks, stats, norms = first_share(parts, place, groups, shifts[0], feats)
    blocks = [rotated(block, "atoms", s) for s, block in zip(shifts[0], blocks)]
    *more, kept = rest_share(rest, norms, stats, place, groups, shifts[1])
    blocks += [rotated(block, "atoms", s) for s, block in zip(shifts[1], more)]
    corr_inst, corr_lag, projections = finish(kept, stats, blocks, shift, own, place, reps)
    return (corr_inst, corr_lag, projections[None]), most_used[0, 0]


def shards(atom_coords, atom_pairs, traj_ids):
    place = [lax.axis_index(axis) for axis in ("atoms", "feat", "rep")]
    place = jnp.stack(place).astype(jnp.int32)
    width = atom_coords.shape[3]
    coords = jnp.transpose(atom_coords[0], (1, 0, 2))
    pairs = [atom_pairs] + [rotated(atom_pairs, "feat", s) for s in range(1, lax.axis_size("feat"))]
    cap = min(width, packed(width * 5 // 9) // 3)
    outs, most_used = with_cap(cap, coords, pairs, traj_ids, place)

    def again(carry):
        same = [block + (carry[0] - 1) for block in pairs]
        return carry[0] - 1, with_cap(width, coords, same, traj_ids, place)[0]

    overflow = (most_used > cap).astype(jnp.int32)
    return lax.while_loop(lambda carry: carry[0] > 0, again, (overflow, outs))[1]


def solution(mesh):
    placed = (P(("grp", "rep"), None, None, "atoms"), P(None, "feat"), P(("grp", "rep"), None))
    return jax.shard_map(
        shards,
        mesh=mesh,
        in_specs=placed,
        out_specs=(
            P(("grp", "atoms", "rep"), "feat"),
            P(("grp", "atoms", "rep"), "feat"),
            P(("grp", "rep"), "atoms", "feat"),
        ),
        check_vma=False,
    )
```

```python
import functools

import jax
import jax.numpy as jnp
from jax import lax
from jax.experimental import pallas as pl
from jax.experimental.pallas import tpu as pltpu
from jax.sharding import PartitionSpec as P

LAG = 10
HALO = 16
CHUNK = 64
CODE = 32700.0
FINE = 60000.0
MEAN_STEP = 0.001
ROOT_STEP = 0.02
TINY = 1e-30
REACH = 1e-6
VMEM_LIMIT = 24 * 1024 * 1024
F32 = jnp.float32
BF16 = jnp.bfloat16
LARGE = pl.CostEstimate(flops=10**11, bytes_accessed=1024, transcendentals=0)
SMALL = pl.CostEstimate(flops=1024, bytes_accessed=1024, transcendentals=0)


def rotated(block, axis, shift):
    size = lax.axis_size(axis)
    return lax.ppermute(block, axis, [(i, (i + shift) % size) for i in range(size)])


def shifts_of(axis):
    size = lax.axis_size(axis)
    return sorted(range(1, size), key=lambda s: -min(s, size - s))


def sent_around(blocks):
    moved = {s: rotated(blocks[s], "atoms", s) for s in shifts_of("atoms")}
    return [blocks[0]] + [moved[s] for s in range(1, len(blocks))]


def passed_down(block, axis):
    return lax.ppermute(block, axis, [(i + 1, i) for i in range(lax.axis_size(axis) - 1)])


def params():
    return pltpu.CompilerParams(vmem_limit_bytes=VMEM_LIMIT)


def start_rows(sizes, start, place_ref, coords_ref, rows_refs, sems):
    groups, sides = rows_refs[0].shape[0], lax.axis_size("feat")
    frames = coords_ref.shape[1] // groups
    copies = []
    for j, size in enumerate(sizes):
        for s in range(groups):
            there = lax.rem(place_ref[0] + s, groups)
            row = there * frames + place_ref[1] * (frames // sides) + start
            copies.append(
                pltpu.make_async_copy(
                    coords_ref.at[:, pl.ds(pl.multiple_of(row, HALO), size), :],
                    rows_refs[j].at[s],
                    sems.at[j, s],
                )
            )
        start += size
    for copy in copies:
        copy.start()
    return copies


def packed(cap):
    return -(-3 * cap // 128) * 128


def pick_rows(rows, chosen, out):
    _, size, width = rows.shape
    cap = chosen.shape[1]
    picked = jnp.dot(
        rows[...].reshape(3 * size, width), chosen, preferred_element_type=F32
    ).astype(BF16)
    for k in range(3):
        out[:, k * cap : (k + 1) * cap] = picked[k * size : (k + 1) * size, :]
    if out.shape[1] > 3 * cap:
        out[:, 3 * cap :] = jnp.zeros((size, out.shape[1] - 3 * cap), BF16)


def first_pick_kernel(sides, place_ref, coords_ref, ids_ref, *refs):
    pairs, refs = refs[:sides], refs[sides:]
    chosen_ref, ids_out, pairs_out, refs = refs[0], refs[1], refs[2 : 2 + sides], refs[2 + sides :]
    later_out, outs, rows_ref, sems = refs[0], refs[1:-2], refs[-2], refs[-1]
    width, cap = chosen_ref.shape
    sizes = (rows_ref.shape[2], later_out.shape[2])
    copies = start_rows(sizes, 0, place_ref, coords_ref, [rows_ref, later_out], sems)
    ids_out[...] = ids_ref[...]
    for block, copy in zip(pairs, pairs_out):
        copy[...] = block[...]
    rank, _ = ranked(pairs, place_ref[0] * width, width, upto(width))
    lanes = lax.broadcasted_iota(jnp.int32, (width, 128), 1)
    for l in range(0, cap, 128):
        some = min(128, cap - l)
        here = (rank == (lanes + l).astype(F32)).astype(F32).astype(BF16)
        chosen_ref[:, l : l + some] = here[:, :some]
    for s, out in enumerate(outs):
        copies[s].wait()
        pick_rows(rows_ref.at[s], chosen_ref[...], out)
    for copy in copies[len(outs) :]:
        copy.wait()


def first_pick(coords, ids, pairs, cap, place, sizes, groups):
    width = coords.shape[2]
    size, later = sizes
    vmem = pl.BlockSpec(memory_space=pltpu.VMEM)
    outs = pl.pallas_call(
        functools.partial(first_pick_kernel, len(pairs)),
        in_specs=[
            pl.BlockSpec(memory_space=pltpu.SMEM),
            pl.BlockSpec(memory_space=pltpu.HBM),
        ]
        + [vmem] * (len(pairs) + 1),
        out_specs=[vmem] * (3 + len(pairs) + groups),
        out_shape=[
            jax.ShapeDtypeStruct((width, cap), BF16),
            jax.ShapeDtypeStruct(ids.shape, ids.dtype),
        ]
        + [jax.ShapeDtypeStruct(block.shape, block.dtype) for block in pairs]
        + [jax.ShapeDtypeStruct((groups, 3, later, width), BF16)]
        + [jax.ShapeDtypeStruct((size, packed(cap)), BF16)] * groups,
        scratch_shapes=[
            pltpu.VMEM((groups, 3, size, width), BF16),
            pltpu.SemaphoreType.DMA((2, groups)),
        ],
        compiler_params=params(),
        cost_estimate=SMALL,
        name="first_pick",
    )(place, coords, ids, *pairs)
    last = 2 + len(pairs)
    return outs[0], outs[1], outs[2:last], outs[last], outs[last + 1 :]


def pick_kernel(rows_ref, chosen_ref, after_ref, *outs):
    for s, out in enumerate(outs):
        pick_rows(rows_ref.at[s], chosen_ref[...], out)


def pick(rows, chosen, after):
    groups, _, size, _ = rows.shape
    cap = chosen.shape[1]
    vmem = pl.BlockSpec(memory_space=pltpu.VMEM)
    return pl.pallas_call(
        pick_kernel,
        in_specs=[vmem, vmem, pl.BlockSpec(memory_space=pl.ANY)],
        out_specs=[vmem] * groups,
        out_shape=[jax.ShapeDtypeStruct((size, packed(cap)), BF16)] * groups,
        compiler_params=params(),
        cost_estimate=SMALL,
        name="pick",
    )(rows, chosen, after)


def coded(value, step):
    first = jnp.round(value / step)
    second = jnp.round((value - first * step) * (FINE / step))
    return [first, second]


def decoded(first, second, step):
    return first * step + second * (step / FINE)


def decoded_piece(codes, rows):
    size = codes.shape[0] - HALO
    ends = codes[size:, :].astype(jnp.int32).astype(F32)
    middle = decoded(ends[0:1], ends[1:2], MEAN_STEP)
    reach = decoded(ends[2:3], ends[3:4], MEAN_STEP)
    return middle + codes[0:rows, :].astype(jnp.int32).astype(F32) * (reach * (1.0 / CODE))


def distance_kernel(*refs):
    blocks, (signs_ref, after_ref, out, codes_out, joined) = refs[:-5], refs[-5:]
    size = blocks[0].shape[0]
    cap = signs_ref.shape[0] // len(blocks)
    for s, block in enumerate(blocks):
        for k in range(3):
            joined[k * size : (k + 1) * size, s * cap : (s + 1) * cap] = block[
                :, k * cap : (k + 1) * cap
            ]
    delta = jnp.dot(joined[...], signs_ref[...], preferred_element_type=F32)
    square = delta * delta
    total = square[:size] + square[size : 2 * size] + square[2 * size :]
    value = jnp.sqrt(total + 0.01)
    out[...] = value
    least, most = jnp.min(value, 0, keepdims=True), jnp.max(value, 0, keepdims=True)
    ends = coded(0.5 * (most + least), MEAN_STEP) + coded(0.5 * (most - least), MEAN_STEP)
    middle = decoded(ends[0], ends[1], MEAN_STEP)
    reach = decoded(ends[2], ends[3], MEAN_STEP)
    ratio = (value - middle) * (CODE / jnp.maximum(reach, REACH))
    ratio = jnp.round(jnp.clip(ratio, -32767.0, 32767.0))
    codes_out[0:size, :] = ratio.astype(jnp.int32).astype(jnp.int16)
    ends = jnp.concatenate(ends + [jnp.zeros((HALO - 4, out.shape[1]), F32)], 0)
    codes_out[size:, :] = ends.astype(jnp.int32).astype(jnp.int16)


def distances(blocks, signs, after):
    size = blocks[0].shape[0]
    vmem = pl.BlockSpec(memory_space=pltpu.VMEM)
    return pl.pallas_call(
        distance_kernel,
        in_specs=[vmem] * (len(blocks) + 1) + [pl.BlockSpec(memory_space=pl.ANY)],
        out_specs=[vmem] * 2,
        out_shape=[
            jax.ShapeDtypeStruct((size, signs.shape[1]), F32),
            jax.ShapeDtypeStruct((size + HALO, signs.shape[1]), jnp.int16),
        ],
        scratch_shapes=[pltpu.VMEM((3 * size, signs.shape[0]), BF16)],
        compiler_params=params(),
        cost_estimate=LARGE,
        name="distances",
    )(*blocks, signs, after)


def split_in_two(value):
    high = value.astype(BF16)
    return high, (value - high.astype(F32)).astype(BF16)


def product(left, right):
    left_high, left_low = split_in_two(left)
    right_high, right_low = split_in_two(right)
    left_high, left_low = left_high.T, left_low.T
    total = jnp.dot(left_high, right_high, preferred_element_type=F32)
    total += jnp.dot(left_high, right_low, preferred_element_type=F32)
    return total + jnp.dot(left_low, right_high, preferred_element_type=F32)


def row_sum(value):
    return jnp.sum(value, 0, keepdims=True)


def side_columns(side, sides, cols, write):
    for s in range(sides):

        @pl.when(side == s)
        def _():
            write(slice(s * cols, (s + 1) * cols))


def early_kernel(chunks, sides, place_ref, *refs):
    pieces = refs[:chunks]
    valid_ref, out, own_out, shift_out, sums_out, tail_out, every = refs[chunks:]
    frames = every.shape[0]
    cols = own_out.shape[1]
    row = 0
    for piece in pieces:
        every[row : row + piece.shape[0], :] = piece[...]
        row += piece.shape[0]
    side = place_ref[1]
    valid = valid_ref[pl.ds(pl.multiple_of(side * frames, HALO), frames), :]
    count = jnp.maximum(jnp.sum(valid), 1.0)
    shift = row_sum(valid * every[...]) / count
    shift_out[...] = shift
    every[...] = every[...] - shift
    tail_out[...] = every[frames - HALO : frames, :]

    def keep_own(part):
        own_out[...] = every[:, part]

    side_columns(side, sides, cols, keep_own)
    now = every[...]
    own = own_out[...]
    weighed = valid * now
    later = own[LAG:frames, :]
    weighed_later = valid[: frames - LAG] * later
    sums_out[0:1, :] = row_sum(weighed)
    sums_out[1:2, :] = row_sum(weighed * now)
    sums_out[2:3, 0:cols] = row_sum(weighed_later)
    sums_out[3:4, 0:cols] = row_sum(weighed_later * later)
    weighed_later = jnp.concatenate([weighed_later, jnp.zeros((LAG, cols), F32)], 0)
    out[...] = product(now, jnp.concatenate([valid * own, weighed_later], 1))


def early_moments(pieces, valid, place, sides):
    frames, feats = sum(piece.shape[0] for piece in pieces), pieces[0].shape[1]
    cols = feats // sides
    vmem = pl.BlockSpec(memory_space=pltpu.VMEM)
    return pl.pallas_call(
        functools.partial(early_kernel, len(pieces), sides),
        in_specs=[pl.BlockSpec(memory_space=pltpu.SMEM)] + [vmem] * (len(pieces) + 1),
        out_specs=[vmem] * 5,
        out_shape=[
            jax.ShapeDtypeStruct((feats, 2 * cols), F32),
            jax.ShapeDtypeStruct((frames, cols), F32),
            jax.ShapeDtypeStruct((1, feats), F32),
            jax.ShapeDtypeStruct((4, feats), F32),
            jax.ShapeDtypeStruct((HALO, feats), F32),
        ],
        scratch_shapes=[pltpu.VMEM((frames, feats), F32)],
        compiler_params=params(),
        cost_estimate=SMALL,
        name="early_moments",
    )(place, *pieces, valid)


def add_blocks(place_ref, shifts, groups, before_ref, left_refs, right_refs, outs):
    reps = len(outs)
    rows = before_ref.shape[0] // (groups * reps)
    left_high, left_low = left_refs
    right_high, right_low = right_refs[0][...], right_refs[1][...]
    for r in reversed(range(reps)):
        rep = lax.rem(place_ref[2] + r, reps)
        for i, s in enumerate(shifts):
            there = lax.rem(place_ref[0] + s, groups)
            at = pl.ds(pl.multiple_of((there * reps + rep) * rows, rows), rows)
            part = before_ref[at, :]
            part += jnp.dot(left_high[at, :], right_high, preferred_element_type=F32)
            part += jnp.dot(left_high[at, :], right_low, preferred_element_type=F32)
            part += jnp.dot(left_low[at, :], right_high, preferred_element_type=F32)
            outs[r][i * rows : (i + 1) * rows, :] = part


def late_kernel(sizes, sides, groups, reps, shifts, place_ref, *refs):
    chunks = len(sizes)
    codes = refs[: chunks * (sides - 1)]
    refs = refs[chunks * (sides - 1) :]
    before_ref, shift_ref, sums_ref, tail_ref, own_ref, halo_ref, valid_ref = refs[:7]
    outs = refs[7 : 7 + reps]
    own_out, left_high, left_low, right_high, right_low, left, right, own = refs[7 + reps :]
    here, cols = own_ref.shape
    frames, feats = here * sides, shift_ref.shape[1]
    side = place_ref[1]
    shift = shift_ref[...]
    bases = [pl.multiple_of(lax.rem(side + sides - s, sides) * here, HALO) for s in range(sides)]
    left[0:HALO, :] = tail_ref[...]
    row = HALO
    for s in range(1, sides):
        for j, size in enumerate(sizes):
            left[row : row + size, :] = decoded_piece(codes[j * (sides - 1) + s - 1], size) - shift
            row += size
    own[pl.ds(bases[0], here), :] = own_ref[...]

    def keep_own(part):
        own[frames:, :] = halo_ref[...] - shift[:, part]
        for s in range(1, sides):
            rows = slice(HALO + (s - 1) * here, HALO + s * here)
            own[pl.ds(bases[s], here), :] = left[rows, part]

    side_columns(side, sides, cols, keep_own)
    own_out[...] = own[0:frames, :]
    valid_all = valid_ref[...]
    total = jnp.sum(valid_all)
    count = jnp.maximum(total, 1.0)
    sums, squares = sums_ref[0:1, :], sums_ref[1:2, :]
    sums_next, squares_next = sums_ref[2:3, 0:cols], sums_ref[3:4, 0:cols]
    end = bases[0] + here - HALO
    later = own[pl.ds(pl.multiple_of(end, HALO), 2 * HALO), :][LAG : LAG + HALO]
    crossing = lax.broadcasted_iota(jnp.int32, (HALO, 1), 0) >= HALO - LAG
    valid = valid_ref[pl.ds(pl.multiple_of(end, HALO), HALO), :]
    weighed_later = jnp.where(crossing, valid * later, 0.0)
    sums_next += row_sum(weighed_later)
    squares_next += row_sum(weighed_later * later)
    right[0:HALO, 0:cols] = jnp.zeros((HALO, cols), F32)
    right[0:HALO, cols : 2 * cols] = weighed_later
    for s in range(1, sides):
        rows = slice(HALO + (s - 1) * here, HALO + s * here)
        valid = valid_ref[pl.ds(bases[s], here), :]
        weighed = valid * left[rows, :]
        sums += row_sum(weighed)
        squares += row_sum(weighed * left[rows, :])
        around = own[pl.ds(bases[s], here + HALO), :]
        right[rows, 0:cols] = valid * around[0:here]
        later = around[LAG : LAG + here]
        weighed_later = valid * later
        right[rows, cols : 2 * cols] = weighed_later
        sums_next += row_sum(weighed_later)
        squares_next += row_sum(weighed_later * later)
    own_sums = jnp.zeros((1, cols), F32)
    own_shift = jnp.zeros((1, cols), F32)
    for s in range(sides):
        mine = (side == s).astype(F32)
        own_sums += mine * sums[:, s * cols : (s + 1) * cols]
        own_shift += mine * shift[:, s * cols : (s + 1) * cols]
    first = lax.broadcasted_iota(jnp.int32, (HALO, 1), 0) == 0
    last = left.shape[0] - HALO
    left[last:, :] = jnp.where(first, sums, 0.0)
    right[last:, 0:cols] = jnp.where(first, -own_sums / count, 0.0)
    right[last:, cols : 2 * cols] = jnp.where(first, -sums_next / count, 0.0)
    high, low = split_in_two(left[...])
    left_high[...] = high.T
    left_low[...] = low.T
    right_high[...], right_low[...] = split_in_two(right[...])
    add_blocks(
        place_ref, shifts, groups, before_ref, (left_high, left_low), (right_high, right_low), outs
    )
    fold = feats // (2 * cols)
    mean, square = shift + sums / count, squares - sums * sums / count
    for out in outs:
        end = out.shape[0] - 8
        for f in range(fold):
            part = slice(2 * cols * f, 2 * cols * (f + 1))
            out[end + f : end + f + 1, :] = mean[:, part]
            out[end + fold + f : end + fold + f + 1, :] = square[:, part]
        end += 2 * fold
        out[end : end + 1, 0:cols] = own_shift + sums_next / count
        out[end : end + 1, cols : 2 * cols] = squares_next - sums_next * sums_next / count
        out[end + 1 : end + 2, :] = jnp.zeros((1, 2 * cols), F32) + total
        spare = out.shape[0] - end - 2
        if spare:
            out[end + 2 :, :] = jnp.zeros((spare, 2 * cols), F32)


def late_moments(codes, before, shift, sums, tail, own, halo, valid, place, sides, groups, reps, shifts):
    sizes = tuple(chunk[0].shape[0] - HALO for chunk in codes)
    codes = [code for chunk in codes for code in chunk]
    here, cols = own.shape
    feats = shift.shape[1]
    depth = here * (sides - 1) + 2 * HALO
    rows = feats // (groups * reps)
    vmem = pl.BlockSpec(memory_space=pltpu.VMEM)
    outs = pl.pallas_call(
        functools.partial(late_kernel, sizes, sides, groups, reps, shifts),
        in_specs=[pl.BlockSpec(memory_space=pltpu.SMEM)] + [vmem] * (len(codes) + 7),
        out_specs=[vmem] * (reps + 5),
        out_shape=[jax.ShapeDtypeStruct((len(shifts) * rows + 8, 2 * cols), F32)] * reps
        + [
            jax.ShapeDtypeStruct((here * sides, cols), F32),
            jax.ShapeDtypeStruct((feats, depth), BF16),
            jax.ShapeDtypeStruct((feats, depth), BF16),
            jax.ShapeDtypeStruct((depth, 2 * cols), BF16),
            jax.ShapeDtypeStruct((depth, 2 * cols), BF16),
        ],
        scratch_shapes=[
            pltpu.VMEM((depth, feats), F32),
            pltpu.VMEM((depth, 2 * cols), F32),
            pltpu.VMEM((here * sides + HALO, cols), F32),
        ],
        compiler_params=params(),
        cost_estimate=SMALL,
        name="late_moments",
    )(place, *codes, before, shift, sums, tail, own, halo, valid)
    return outs[:reps], outs[reps], outs[reps + 1 :]


def rest_kernel(groups, shifts, place_ref, before_ref, left_high, left_low, right_high, right_low, *outs):
    add_blocks(
        place_ref, shifts, groups, before_ref, (left_high, left_low), (right_high, right_low), outs
    )


def rest_moments(before, factors, place, groups, reps, shifts):
    rows = before.shape[0] // (groups * reps)
    vmem = pl.BlockSpec(memory_space=pltpu.VMEM)
    return pl.pallas_call(
        functools.partial(rest_kernel, groups, shifts),
        in_specs=[pl.BlockSpec(memory_space=pltpu.SMEM)] + [vmem] * 5,
        out_specs=[vmem] * reps,
        out_shape=[jax.ShapeDtypeStruct((len(shifts) * rows, before.shape[1]), F32)] * reps,
        compiler_params=params(),
        cost_estimate=SMALL,
        name="rest_moments",
    )(place, before, *factors)


def rolled(value, first):
    rows, width = value.shape
    wide = jnp.broadcast_to(value, (8, width)) if rows == 1 else value
    return pltpu.roll(wide, lax.rem(width - first, width), 1)[:rows]


def as_column(row):
    return jnp.broadcast_to(row, (8, row.shape[1])).T[:, 0:1]


def code_block(place_ref, groups, reps, s, i, parts, norms, out):
    width = parts[0].shape[1]
    cols = width // 2
    feats = norms.shape[1]
    rows = feats // (groups * reps)
    at = slice(i * rows, (i + 1) * rows)
    total = parts[0][at, :]
    for part in parts[1:]:
        total += part[at, :]
    if s == 0:
        out[...] = total
        return
    there = lax.rem(place_ref[0] + s, groups)
    first = (there * reps + place_ref[2]) * rows
    inverse_cols = jnp.concatenate(
        [rolled(norms[0:1, :], place_ref[1] * cols)[:, :cols], norms[1:2, :cols]], 1
    )
    ratio = total * as_column(rolled(norms[0:1, :], first)[:, :rows]) * inverse_cols
    root = jnp.sqrt(jnp.minimum(jnp.abs(ratio), 1.001)) * CODE
    root = jnp.where(ratio < 0.0, -root, root)
    out[0:rows, :] = jnp.round(root).astype(jnp.int32).astype(jnp.int16)


def first_share_kernel(groups, shifts, place_ref, *refs):
    count = len(shifts)
    parts, outs, codes_out, norms_out = refs[: -count - 2], refs[-count - 2 : -2], refs[-2], refs[-1]
    reps, width = len(parts), parts[0].shape[1]
    cols, feats = width // 2, norms_out.shape[1]
    fold = feats // width
    end = parts[0].shape[0] - 8
    square = jnp.zeros((1, feats), F32)
    square_next = jnp.zeros((1, cols), F32)
    codes = []
    for part in parts:
        own = part[end : end + 8, :]
        squares = [own[fold + f : fold + f + 1] for f in range(fold)]
        final = own[2 * fold : 2 * fold + 1]
        square += jnp.concatenate(squares, 1)
        square_next += final[:, cols:]
        for f in range(fold):
            codes += coded(own[f : f + 1], MEAN_STEP)
        for line in squares:
            codes += coded(jnp.sqrt(jnp.maximum(line, 0.0)), ROOT_STEP)
        pair = coded(final[:, :cols], MEAN_STEP)
        pair_next = coded(jnp.sqrt(jnp.maximum(final[:, cols:], 0.0)), ROOT_STEP)
        codes += [jnp.concatenate(both, 1) for both in zip(pair, pair_next)]
        codes.append(own[2 * fold + 1 : 2 * fold + 2])
    spare = codes_out.shape[0] - len(codes)
    if spare:
        codes.append(jnp.zeros((spare, width), F32))
    codes = jnp.concatenate(codes, 0).astype(jnp.int32).astype(jnp.int16)
    codes_out[...] = codes
    norms_out[...] = jnp.zeros(norms_out.shape, F32)
    norms_out[0:1, :] = lax.rsqrt(jnp.maximum(square, TINY))
    norms_out[1:2, :cols] = lax.rsqrt(jnp.maximum(square_next, TINY))
    for i, (s, out) in enumerate(zip(shifts, outs)):
        code_block(place_ref, groups, reps, s, i, parts, norms_out, out)
        out[out.shape[0] - codes.shape[0] :, :] = codes


def rest_share_kernel(groups, shifts, place_ref, norms_ref, codes_ref, *refs):
    count = len(shifts)
    parts, outs = refs[:-count], refs[-count:]
    for i, (s, out) in enumerate(zip(shifts, outs)):
        code_block(place_ref, groups, len(parts), s, i, parts, norms_ref, out)
        if s:
            out[out.shape[0] - codes_ref.shape[0] :, :] = codes_ref[...]


def first_share(parts, place, groups, shifts, feats):
    width, reps = parts[0].shape[1], len(parts)
    rows = feats // (groups * reps)
    lines = -(-reps * (4 * (feats // width) + 3) // 16) * 16
    vmem = pl.BlockSpec(memory_space=pltpu.VMEM)
    outs = pl.pallas_call(
        functools.partial(first_share_kernel, groups, shifts),
        in_specs=[pl.BlockSpec(memory_space=pltpu.SMEM)] + [vmem] * reps,
        out_specs=[vmem] * (len(shifts) + 2),
        out_shape=[jax.ShapeDtypeStruct((rows + lines, width), jnp.int16)] * len(shifts)
        + [
            jax.ShapeDtypeStruct((lines, width), jnp.int16),
            jax.ShapeDtypeStruct((8, feats), F32),
        ],
        compiler_params=params(),
        cost_estimate=SMALL,
        name="first_share",
    )(place, *parts)
    return outs[:-2], outs[-2], outs[-1]


def rest_share(parts, norms, codes, place, groups, shifts):
    width = parts[0].shape[1]
    rows = parts[0].shape[0] // len(shifts)
    coded_shape = jax.ShapeDtypeStruct((rows + codes.shape[0], width), jnp.int16)
    vmem = pl.BlockSpec(memory_space=pltpu.VMEM)
    return pl.pallas_call(
        functools.partial(rest_share_kernel, groups, shifts),
        in_specs=[pl.BlockSpec(memory_space=pltpu.SMEM)] + [vmem] * (len(parts) + 2),
        out_specs=[vmem] * len(shifts),
        out_shape=[coded_shape if s else jax.ShapeDtypeStruct((rows, width), F32) for s in shifts],
        compiler_params=params(),
        cost_estimate=SMALL,
        name="rest_share",
    )(place, norms, codes, *parts)


def finish_kernel(reps, place_ref, kept_ref, codes_ref, *refs):
    blocks = refs[:-5]
    shift_ref, own_ref, inst_out, lag_out, projections_out = refs[-5:]
    rows, cols = inst_out.shape
    feats = shift_ref.shape[1]
    width = 2 * cols
    fold = feats // width
    count = jnp.zeros((1, 1), F32)
    mean = jnp.zeros((1, feats), F32)
    mean_next = jnp.zeros((1, cols), F32)
    stats = []
    for block in (codes_ref,) + tuple(blocks):
        start = 0 if block is codes_ref else rows
        codes = block[start:, :].astype(jnp.int32).astype(F32)
        at = 0
        for r in range(reps):
            lines = [codes[at + i : at + i + 1] for i in range(4 * fold + 3)]
            at += 4 * fold + 3
            pairs = [(lines[2 * i], lines[2 * i + 1]) for i in range(2 * fold + 1)]
            means = [decoded(*pair, MEAN_STEP) for pair in pairs[:fold]]
            roots = [decoded(*pair, ROOT_STEP) for pair in pairs[fold : 2 * fold]]
            one, two = pairs[2 * fold]
            roots_next = decoded(one[:, cols:], two[:, cols:], ROOT_STEP)
            here = [
                jnp.concatenate(means, 1),
                jnp.concatenate([root * root for root in roots], 1),
                decoded(one[:, :cols], two[:, :cols], MEAN_STEP),
                roots_next * roots_next,
                lines[-1][:, 0:1],
            ]
            stats.append(here)
            count += here[4]
            mean += here[4] * here[0]
            mean_next += here[4] * here[2]
    mean, mean_next = mean / count, mean_next / count
    spread = jnp.zeros((1, feats), F32)
    spread_next = jnp.zeros((1, cols), F32)
    away, away_next = [], []
    for here in stats:
        away.append(here[0] - mean)
        away_next.append(here[2] - mean_next)
        spread += here[1] + here[4] * away[-1] * away[-1]
        spread_next += here[3] + here[4] * away_next[-1] * away_next[-1]
    numbers = jnp.concatenate([here[4] for here in stats], 0)
    scale = 1.0 / jnp.sqrt(spread / count + 1e-05)
    scale_next = 1.0 / jnp.sqrt(spread_next / count + 1e-05)
    away = jnp.concatenate(away, 0)

    first_row = (place_ref[0] * reps + place_ref[2]) * rows
    first_col = place_ref[1] * cols
    right = numbers * jnp.concatenate(
        [rolled(away, first_col)[:, :cols], jnp.concatenate(away_next, 0)], 1
    )
    moment = kept_ref[...] + jnp.dot(
        rolled(away, first_row)[:, :rows].T,
        right,
        precision=lax.Precision.HIGHEST,
        preferred_element_type=F32,
    )
    for g, block in enumerate(blocks):
        here = stats[(g + 1) * reps : (g + 2) * reps]
        root = jnp.sqrt(sum(one[1] for one in here))
        root_next = jnp.sqrt(sum(one[3] for one in here))
        root_rows = as_column(rolled(root, first_row)[:, :rows])
        root_cols = jnp.concatenate([rolled(root, first_col)[:, :cols], root_next], 1)
        code = block[0:rows, :].astype(jnp.int32).astype(F32) * (1.0 / CODE)
        moment += code * jnp.abs(code) * root_rows * root_cols
    scale_cols = rolled(scale, first_col)[:, :cols]
    moment = moment / count * as_column(rolled(scale, first_row)[:, :rows])
    inst_out[...] = moment[:, 0:cols] * scale_cols
    lag_out[...] = moment[:, cols : 2 * cols] * scale_next
    offset = rolled(shift_ref[...] - mean, first_col)[:, :cols]
    projections_out[...] = (own_ref[...] + offset) * scale_cols


def finish(kept, codes, blocks, shift, own, place, reps):
    rows = kept.shape[0]
    frames, cols = own.shape
    vmem = pl.BlockSpec(memory_space=pltpu.VMEM)
    return pl.pallas_call(
        functools.partial(finish_kernel, reps),
        in_specs=[pl.BlockSpec(memory_space=pltpu.SMEM)] + [vmem] * (len(blocks) + 4),
        out_specs=[vmem] * 3,
        out_shape=[
            jax.ShapeDtypeStruct((rows, cols), F32),
            jax.ShapeDtypeStruct((rows, cols), F32),
            jax.ShapeDtypeStruct((frames, cols), F32),
        ],
        compiler_params=params(),
        cost_estimate=SMALL,
        name="finish",
    )(place, kept, codes, *blocks, shift, own)


def upto(width):
    rows = lax.broadcasted_iota(jnp.int32, (width, width), 0)
    lanes = lax.broadcasted_iota(jnp.int32, (width, width), 1)
    return (lanes <= rows).astype(F32).astype(BF16)


def ranked(pairs, first, width, below):
    atoms = lax.broadcasted_iota(jnp.int32, (width, 128), 0) + first
    hit = jnp.zeros((width, 128), F32)
    for block in pairs:
        for r in range(2):
            for l in range(0, block.shape[1], 128):
                hit = jnp.where(block[r : r + 1, l : l + 128] == atoms, 1.0, hit)
    used = jnp.broadcast_to(jnp.max(hit, axis=1, keepdims=True), (width, 128))
    order = jnp.dot(below, used.astype(BF16), preferred_element_type=F32)
    return jnp.where(used > 0.0, order - 1.0, -1.0), order[width - 1 : width, :]


def signs_kernel(groups, width, cap, place_ref, after_ref, *refs):
    pairs, (signs_out, most_out) = refs[:-2], refs[-2:]
    sides = len(pairs)
    below = upto(width)
    number = lax.broadcasted_iota(jnp.int32, (width, 128), 0) + 1
    high = (number // 8).astype(F32).astype(BF16)
    low = (number % 8).astype(F32).astype(BF16)
    slots = lax.broadcasted_iota(jnp.int32, (cap, width), 0).astype(F32)
    most = jnp.zeros((1, 128), F32)
    for s in range(groups):
        first = lax.rem(place_ref[0] + groups - s, groups) * width
        rank, count = ranked(pairs, first, width, below)
        most = jnp.maximum(most, count)
        chosen = (rank.T[0:1, :] == slots).astype(F32).astype(BF16)
        listed = 8.0 * jnp.dot(chosen, high, preferred_element_type=F32)
        listed += jnp.dot(chosen, low, preferred_element_type=F32)
        listed = listed.astype(jnp.int32) - 1
        listed = jnp.where(listed < 0, -1, listed + first)
        for b, block in enumerate(pairs):
            cols = block.shape[1]
            there = lax.rem(place_ref[1] + sides - b, sides) * cols
            for l in range(0, cols, 128):
                one = (block[0:1, l : l + 128] == listed).astype(F32)
                two = (block[1:2, l : l + 128] == listed).astype(F32)
                at = pl.ds(pl.multiple_of(there + l, 128), 128)
                signs_out[s * cap : (s + 1) * cap, at] = (one - two).astype(BF16)
    most_out[...] = most


def pair_signs(pairs, after, place, groups, width, cap):
    feats = len(pairs) * pairs[0].shape[1]
    vmem = pl.BlockSpec(memory_space=pltpu.VMEM)
    return pl.pallas_call(
        functools.partial(signs_kernel, groups, width, cap),
        in_specs=[pl.BlockSpec(memory_space=pltpu.SMEM), pl.BlockSpec(memory_space=pl.ANY)]
        + [vmem] * len(pairs),
        out_specs=[vmem] * 2,
        out_shape=[
            jax.ShapeDtypeStruct((groups * cap, feats), BF16),
            jax.ShapeDtypeStruct((1, 128), F32),
        ],
        compiler_params=params(),
        cost_estimate=LARGE,
        name="pair_signs",
    )(place, after, *pairs)


def chunk_sizes(frames):
    last = frames // 8 * 3
    return frames - last, last


def with_cap(cap, coords, pairs, traj_ids, place):
    groups, sides = lax.axis_size("atoms"), lax.axis_size("feat")
    atom_index, feat_index = place[0], place[1]
    width = coords.shape[2]
    frames = coords.shape[1] // groups
    cols = pairs[0].shape[1]
    feats = cols * sides
    sizes = chunk_sizes(frames // sides)

    chosen, traj_ids, pairs, later, picked = first_pick(
        coords, traj_ids, pairs, cap, place, sizes, groups
    )
    arrived = [sent_around(picked)]
    signs, most_used = pair_signs(pairs, picked[0], place, groups, width, cap)
    picked = pick(later, chosen, most_used)
    arrived.append(sent_around(picked))

    ids = jnp.concatenate([traj_ids[0], jnp.full((LAG,), -1, jnp.int32)])
    offset = atom_index * frames
    ids_now = lax.dynamic_slice_in_dim(ids, offset, frames)
    ids_later = lax.dynamic_slice_in_dim(ids, offset + LAG, frames)
    valid = (ids_now == ids_later).astype(F32)[:, None]

    own_pieces, codes, after = [], [], arrived[-1][0]
    for j, blocks in enumerate(arrived):
        block, code = distances(blocks, signs, after)
        after = block
        own_pieces.append(block)
        codes.append([rotated(code, "feat", s) for s in range(1, sides)])
        if j == 0:
            opening = passed_down(block[:HALO], "atoms")
    halo = lax.dynamic_slice_in_dim(opening, feat_index * cols, cols, 1)
    for s in range(1, sides):
        there = lax.rem(feat_index + s, sides)
        sent = rotated(lax.dynamic_slice_in_dim(opening, there * cols, cols, 1), "feat", s)
        halo = jnp.where(feat_index == s, sent, halo)

    reps = lax.axis_size("rep")
    shifts = shifts_of("atoms") + [0]
    shifts = tuple(shifts[: groups // 2]), tuple(shifts[groups // 2 :])
    before, own, shift, sums, tail = early_moments(own_pieces, valid, place, sides)
    parts, own, factors = late_moments(
        codes, before, shift, sums, tail, own, halo, valid, place, sides, groups, reps, shifts[0]
    )
    parts = [parts[0]] + [rotated(parts[r], "rep", r) for r in range(1, reps)]
    rest = rest_moments(before, factors, place, groups, reps, shifts[1])
    rest = [rest[0]] + [rotated(rest[r], "rep", r) for r in range(1, reps)]
    blocks, stats, norms = first_share(parts, place, groups, shifts[0], feats)
    blocks = [rotated(block, "atoms", s) for s, block in zip(shifts[0], blocks)]
    *more, kept = rest_share(rest, norms, stats, place, groups, shifts[1])
    blocks += [rotated(block, "atoms", s) for s, block in zip(shifts[1], more)]
    corr_inst, corr_lag, projections = finish(kept, stats, blocks, shift, own, place, reps)
    return (corr_inst, corr_lag, projections[None]), most_used[0, 0]


def shards(atom_coords, atom_pairs, traj_ids):
    place = [lax.axis_index(axis) for axis in ("atoms", "feat", "rep")]
    place = jnp.stack(place).astype(jnp.int32)
    width = atom_coords.shape[3]
    coords = jnp.transpose(atom_coords[0], (1, 0, 2))
    pairs = [atom_pairs] + [rotated(atom_pairs, "feat", s) for s in range(1, lax.axis_size("feat"))]
    cap = min(width, packed(width * 5 // 9) // 3)
    outs, most_used = with_cap(cap, coords, pairs, traj_ids, place)

    def again(carry):
        same = [block + (carry[0] - 1) for block in pairs]
        return carry[0] - 1, with_cap(width, coords, same, traj_ids, place)[0]

    overflow = (most_used > cap).astype(jnp.int32)
    return lax.while_loop(lambda carry: carry[0] > 0, again, (overflow, outs))[1]


def solution(mesh):
    placed = (P(("grp", "rep"), None, None, "atoms"), P(None, "feat"), P(("grp", "rep"), None))
    return jax.shard_map(
        shards,
        mesh=mesh,
        in_specs=placed,
        out_specs=(
            P(("grp", "atoms", "rep"), "feat"),
            P(("grp", "atoms", "rep"), "feat"),
            P(("grp", "rep"), "atoms", "feat"),
        ),
        check_vma=False,
    )
```

```python
import functools

import jax
import jax.numpy as jnp
from jax import lax
from jax.experimental import pallas as pl
from jax.experimental.pallas import tpu as pltpu
from jax.sharding import PartitionSpec as P

LAG = 10
HALO = 16
CHUNK = 64
CODE = 32700.0
FINE = 60000.0
MEAN_STEP = 0.001
ROOT_STEP = 0.02
TINY = 1e-30
REACH = 1e-6
VMEM_LIMIT = 20 * 1024 * 1024
F32 = jnp.float32
BF16 = jnp.bfloat16
LARGE = pl.CostEstimate(flops=10**11, bytes_accessed=1024, transcendentals=0)
SMALL = pl.CostEstimate(flops=1024, bytes_accessed=1024, transcendentals=0)


def rotated(block, axis, shift):
    size = lax.axis_size(axis)
    return lax.ppermute(block, axis, [(i, (i + shift) % size) for i in range(size)])


def shifts_of(axis):
    size = lax.axis_size(axis)
    return sorted(range(1, size), key=lambda s: -min(s, size - s))


def passed_down(block, axis):
    return lax.ppermute(block, axis, [(i + 1, i) for i in range(lax.axis_size(axis) - 1)])


def params():
    return pltpu.CompilerParams(vmem_limit_bytes=VMEM_LIMIT)


def start_rows(shifts, start, place_ref, coords_ref, rows_ref, sems):
    groups, sides = lax.axis_size("atoms"), lax.axis_size("feat")
    frames = coords_ref.shape[1] // groups
    copies = []
    for i, s in enumerate(shifts):
        there = lax.rem(place_ref[0] + s, groups)
        row = there * frames + place_ref[1] * (frames // sides) + start
        rows = pl.ds(pl.multiple_of(row, HALO), rows_ref.shape[2])
        copies.append(
            pltpu.make_async_copy(coords_ref.at[:, rows, :], rows_ref.at[i], sems.at[i])
        )
        copies[-1].start()
    return copies


def packed(cap):
    return -(-3 * cap // 128) * 128


def slot_rows(cap):
    return -(-cap // HALO) * HALO


def pick_rows(rows, chosen, out):
    _, size, width = rows.shape
    cap = chosen.shape[1]
    picked = jnp.dot(
        rows[...].reshape(3 * size, width), chosen, preferred_element_type=F32
    ).astype(BF16)
    for k in range(3):
        out[:, k * cap : (k + 1) * cap] = picked[k * size : (k + 1) * size, :]
    if out.shape[1] > 3 * cap:
        out[:, 3 * cap :] = jnp.zeros((size, out.shape[1] - 3 * cap), BF16)


def first_pick_kernel(sides, near, far, place_ref, coords_ref, ids_ref, *refs):
    pairs, refs = refs[:sides], refs[sides:]
    chosen_ref, ids_out, pairs_out, refs = refs[0], refs[1], refs[2 : 2 + sides], refs[2 + sides :]
    near_out, later_out, out, rows_ref, sems = refs
    width, cap = chosen_ref.shape
    size = rows_ref.shape[2]
    first = start_rows([far], 0, place_ref, coords_ref, rows_ref, sems.at[0])
    others = start_rows(near + [0], 0, place_ref, coords_ref, near_out, sems.at[1])
    others += start_rows([far] + near + [0], size, place_ref, coords_ref, later_out, sems.at[2])
    ids_out[...] = ids_ref[...]
    for block, copy in zip(pairs, pairs_out):
        copy[...] = block[...]
    rank, _ = ranked(pairs, place_ref[0] * width, width, upto(width))
    lanes = lax.broadcasted_iota(jnp.int32, (width, 128), 1)
    for l in range(0, cap, 128):
        some = min(128, cap - l)
        here = (rank == (lanes + l).astype(F32)).astype(F32).astype(BF16)
        chosen_ref[:, l : l + some] = here[:, :some]
    first[0].wait()
    pick_rows(rows_ref.at[0], chosen_ref[...], out)
    for copy in others:
        copy.wait()


def first_pick(coords, ids, pairs, cap, place, sizes, near, far):
    width = coords.shape[2]
    size, later = sizes
    vmem = pl.BlockSpec(memory_space=pltpu.VMEM)
    outs = pl.pallas_call(
        functools.partial(first_pick_kernel, len(pairs), near, far),
        in_specs=[
            pl.BlockSpec(memory_space=pltpu.SMEM),
            pl.BlockSpec(memory_space=pltpu.HBM),
        ]
        + [vmem] * (len(pairs) + 1),
        out_specs=[vmem] * (5 + len(pairs)),
        out_shape=[
            jax.ShapeDtypeStruct((width, cap), BF16),
            jax.ShapeDtypeStruct(ids.shape, ids.dtype),
        ]
        + [jax.ShapeDtypeStruct(block.shape, block.dtype) for block in pairs]
        + [
            jax.ShapeDtypeStruct((len(near) + 1, 3, size, width), BF16),
            jax.ShapeDtypeStruct((len(near) + 2, 3, later, width), BF16),
            jax.ShapeDtypeStruct((size, packed(cap)), BF16),
        ],
        scratch_shapes=[
            pltpu.VMEM((1, 3, size, width), BF16),
            pltpu.SemaphoreType.DMA((3, len(near) + 2)),
        ],
        compiler_params=params(),
        cost_estimate=SMALL,
        name="first_pick",
    )(place, coords, ids, *pairs)
    last = 2 + len(pairs)
    return outs[0], outs[1], outs[2:last], outs[last], outs[last + 1], outs[last + 2]


def pick_kernel(counts, chosen_ref, after_ref, *refs):
    rows_refs, outs = refs[: len(counts)], list(refs[len(counts) :])
    for rows_ref, count in zip(rows_refs, counts):
        for i in range(count):
            pick_rows(rows_ref.at[i], chosen_ref[...], outs.pop(0))


def pick(rows, chosen, after):
    cap = chosen.shape[1]
    counts = [some.shape[0] for some in rows]
    vmem = pl.BlockSpec(memory_space=pltpu.VMEM)
    return pl.pallas_call(
        functools.partial(pick_kernel, counts),
        in_specs=[vmem, pl.BlockSpec(memory_space=pl.ANY)] + [vmem] * len(rows),
        out_specs=[vmem] * sum(counts),
        out_shape=[
            jax.ShapeDtypeStruct((some.shape[2], packed(cap)), BF16)
            for some in rows
            for _ in range(some.shape[0])
        ],
        compiler_params=params(),
        cost_estimate=SMALL,
        name="pick",
    )(chosen, after, *rows)


def coded(value, step):
    first = jnp.round(value / step)
    second = jnp.round((value - first * step) * (FINE / step))
    return [first, second]


def decoded(first, second, step):
    return first * step + second * (step / FINE)


def decoded_piece(codes, rows):
    size = codes.shape[0] - HALO
    ends = codes[size:, :].astype(jnp.int32).astype(F32)
    middle = decoded(ends[0:1], ends[1:2], MEAN_STEP)
    reach = decoded(ends[2:3], ends[3:4], MEAN_STEP)
    return middle + codes[0:rows, :].astype(jnp.int32).astype(F32) * (reach * (1.0 / CODE))


def distance_kernel(cap, *refs):
    blocks, (signs_ref, after_ref, out, codes_out, joined) = refs[:-5], refs[-5:]
    size = blocks[0].shape[0]
    slots = signs_ref.shape[0] // len(blocks)
    for s, block in enumerate(blocks):
        for k in range(3):
            rows = slice(k * size, (k + 1) * size)
            joined[rows, s * slots : s * slots + cap] = block[:, k * cap : (k + 1) * cap]
        if slots > cap:
            joined[:, s * slots + cap : (s + 1) * slots] = jnp.zeros((3 * size, slots - cap), BF16)
    delta = jnp.dot(joined[...], signs_ref[...], preferred_element_type=F32)
    square = delta * delta
    total = square[:size] + square[size : 2 * size] + square[2 * size :]
    value = jnp.sqrt(total + 0.01)
    out[...] = value
    least, most = jnp.min(value, 0, keepdims=True), jnp.max(value, 0, keepdims=True)
    ends = coded(0.5 * (most + least), MEAN_STEP) + coded(0.5 * (most - least), MEAN_STEP)
    middle = decoded(ends[0], ends[1], MEAN_STEP)
    reach = decoded(ends[2], ends[3], MEAN_STEP)
    ratio = (value - middle) * (CODE / jnp.maximum(reach, REACH))
    ratio = jnp.round(jnp.clip(ratio, -32767.0, 32767.0))
    codes_out[0:size, :] = ratio.astype(jnp.int32).astype(jnp.int16)
    ends = jnp.concatenate(ends + [jnp.zeros((HALO - 4, out.shape[1]), F32)], 0)
    codes_out[size:, :] = ends.astype(jnp.int32).astype(jnp.int16)


def distances(blocks, signs, after, cap):
    size = blocks[0].shape[0]
    vmem = pl.BlockSpec(memory_space=pltpu.VMEM)
    return pl.pallas_call(
        functools.partial(distance_kernel, cap),
        in_specs=[vmem] * (len(blocks) + 1) + [pl.BlockSpec(memory_space=pl.ANY)],
        out_specs=[vmem] * 2,
        out_shape=[
            jax.ShapeDtypeStruct((size, signs.shape[1]), F32),
            jax.ShapeDtypeStruct((size + HALO, signs.shape[1]), jnp.int16),
        ],
        scratch_shapes=[pltpu.VMEM((3 * size, signs.shape[0]), BF16)],
        compiler_params=params(),
        cost_estimate=LARGE,
        name="distances",
    )(*blocks, signs, after)


def split_in_two(value):
    high = value.astype(BF16)
    return high, (value - high.astype(F32)).astype(BF16)


def product(left, right):
    left_high, left_low = split_in_two(left)
    right_high, right_low = split_in_two(right)
    left_high, left_low = left_high.T, left_low.T
    total = jnp.dot(left_high, right_high, preferred_element_type=F32)
    total += jnp.dot(left_high, right_low, preferred_element_type=F32)
    return total + jnp.dot(left_low, right_high, preferred_element_type=F32)


def row_sum(value):
    return jnp.sum(value, 0, keepdims=True)


def side_columns(side, sides, cols, write):
    for s in range(sides):

        @pl.when(side == s)
        def _():
            write(slice(s * cols, (s + 1) * cols))


def early_kernel(chunks, sides, place_ref, *refs):
    pieces = refs[:chunks]
    valid_ref, out, own_out, shift_out, sums_out, tail_out, every = refs[chunks:]
    frames = every.shape[0]
    cols = own_out.shape[1]
    row = 0
    for piece in pieces:
        every[row : row + piece.shape[0], :] = piece[...]
        row += piece.shape[0]
    side = place_ref[1]
    valid = valid_ref[pl.ds(pl.multiple_of(side * frames, HALO), frames), :]
    count = jnp.maximum(jnp.sum(valid), 1.0)
    shift = row_sum(valid * every[...]) / count
    shift_out[...] = shift
    every[...] = every[...] - shift
    tail_out[...] = every[frames - HALO : frames, :]

    def keep_own(part):
        own_out[...] = every[:, part]

    side_columns(side, sides, cols, keep_own)
    now = every[...]
    own = own_out[...]
    weighed = valid * now
    later = own[LAG:frames, :]
    weighed_later = valid[: frames - LAG] * later
    sums_out[0:1, :] = row_sum(weighed)
    sums_out[1:2, :] = row_sum(weighed * now)
    sums_out[2:3, 0:cols] = row_sum(weighed_later)
    sums_out[3:4, 0:cols] = row_sum(weighed_later * later)
    weighed_later = jnp.concatenate([weighed_later, jnp.zeros((LAG, cols), F32)], 0)
    out[...] = product(now, jnp.concatenate([valid * own, weighed_later], 1))


def early_moments(pieces, valid, place, sides):
    frames, feats = sum(piece.shape[0] for piece in pieces), pieces[0].shape[1]
    cols = feats // sides
    vmem = pl.BlockSpec(memory_space=pltpu.VMEM)
    return pl.pallas_call(
        functools.partial(early_kernel, len(pieces), sides),
        in_specs=[pl.BlockSpec(memory_space=pltpu.SMEM)] + [vmem] * (len(pieces) + 1),
        out_specs=[vmem] * 5,
        out_shape=[
            jax.ShapeDtypeStruct((feats, 2 * cols), F32),
            jax.ShapeDtypeStruct((frames, cols), F32),
            jax.ShapeDtypeStruct((1, feats), F32),
            jax.ShapeDtypeStruct((4, feats), F32),
            jax.ShapeDtypeStruct((HALO, feats), F32),
        ],
        scratch_shapes=[pltpu.VMEM((frames, feats), F32)],
        compiler_params=params(),
        cost_estimate=SMALL,
        name="early_moments",
    )(place, *pieces, valid)


def add_blocks(place_ref, shifts, groups, before_ref, left_refs, right_refs, outs):
    reps = len(outs)
    rows = before_ref.shape[0] // (groups * reps)
    left_high, left_low = left_refs
    right_high, right_low = right_refs[0][...], right_refs[1][...]
    for r in reversed(range(reps)):
        rep = lax.rem(place_ref[2] + r, reps)
        for i, s in enumerate(shifts):
            there = lax.rem(place_ref[0] + s, groups)
            at = pl.ds(pl.multiple_of((there * reps + rep) * rows, rows), rows)
            part = before_ref[at, :]
            part += jnp.dot(left_high[at, :], right_high, preferred_element_type=F32)
            part += jnp.dot(left_high[at, :], right_low, preferred_element_type=F32)
            part += jnp.dot(left_low[at, :], right_high, preferred_element_type=F32)
            outs[r][i * rows : (i + 1) * rows, :] = part


def late_kernel(sizes, sides, groups, reps, shifts, place_ref, *refs):
    chunks = len(sizes)
    codes = refs[: chunks * (sides - 1)]
    refs = refs[chunks * (sides - 1) :]
    before_ref, shift_ref, sums_ref, tail_ref, own_ref, halo_ref, valid_ref = refs[:7]
    outs = refs[7 : 7 + reps]
    own_out, left_high, left_low, right_high, right_low, left, right, own = refs[7 + reps :]
    here, cols = own_ref.shape
    frames, feats = here * sides, shift_ref.shape[1]
    side = place_ref[1]
    shift = shift_ref[...]
    bases = [pl.multiple_of(lax.rem(side + sides - s, sides) * here, HALO) for s in range(sides)]
    left[0:HALO, :] = tail_ref[...]
    row = HALO
    for s in range(1, sides):
        for j, size in enumerate(sizes):
            left[row : row + size, :] = decoded_piece(codes[j * (sides - 1) + s - 1], size) - shift
            row += size
    own[pl.ds(bases[0], here), :] = own_ref[...]

    def keep_own(part):
        own[frames:, :] = halo_ref[...] - shift[:, part]
        for s in range(1, sides):
            rows = slice(HALO + (s - 1) * here, HALO + s * here)
            own[pl.ds(bases[s], here), :] = left[rows, part]

    side_columns(side, sides, cols, keep_own)
    own_out[...] = own[0:frames, :]
    valid_all = valid_ref[...]
    total = jnp.sum(valid_all)
    count = jnp.maximum(total, 1.0)
    sums, squares = sums_ref[0:1, :], sums_ref[1:2, :]
    sums_next, squares_next = sums_ref[2:3, 0:cols], sums_ref[3:4, 0:cols]
    end = bases[0] + here - HALO
    later = own[pl.ds(pl.multiple_of(end, HALO), 2 * HALO), :][LAG : LAG + HALO]
    crossing = lax.broadcasted_iota(jnp.int32, (HALO, 1), 0) >= HALO - LAG
    valid = valid_ref[pl.ds(pl.multiple_of(end, HALO), HALO), :]
    weighed_later = jnp.where(crossing, valid * later, 0.0)
    sums_next += row_sum(weighed_later)
    squares_next += row_sum(weighed_later * later)
    right[0:HALO, 0:cols] = jnp.zeros((HALO, cols), F32)
    right[0:HALO, cols : 2 * cols] = weighed_later
    for s in range(1, sides):
        rows = slice(HALO + (s - 1) * here, HALO + s * here)
        valid = valid_ref[pl.ds(bases[s], here), :]
        weighed = valid * left[rows, :]
        sums += row_sum(weighed)
        squares += row_sum(weighed * left[rows, :])
        around = own[pl.ds(bases[s], here + HALO), :]
        right[rows, 0:cols] = valid * around[0:here]
        later = around[LAG : LAG + here]
        weighed_later = valid * later
        right[rows, cols : 2 * cols] = weighed_later
        sums_next += row_sum(weighed_later)
        squares_next += row_sum(weighed_later * later)
    own_sums = jnp.zeros((1, cols), F32)
    own_shift = jnp.zeros((1, cols), F32)
    for s in range(sides):
        mine = (side == s).astype(F32)
        own_sums += mine * sums[:, s * cols : (s + 1) * cols]
        own_shift += mine * shift[:, s * cols : (s + 1) * cols]
    first = lax.broadcasted_iota(jnp.int32, (HALO, 1), 0) == 0
    last = left.shape[0] - HALO
    left[last:, :] = jnp.where(first, sums, 0.0)
    right[last:, 0:cols] = jnp.where(first, -own_sums / count, 0.0)
    right[last:, cols : 2 * cols] = jnp.where(first, -sums_next / count, 0.0)
    high, low = split_in_two(left[...])
    left_high[...] = high.T
    left_low[...] = low.T
    right_high[...], right_low[...] = split_in_two(right[...])
    add_blocks(
        place_ref, shifts, groups, before_ref, (left_high, left_low), (right_high, right_low), outs
    )
    fold = feats // (2 * cols)
    mean, square = shift + sums / count, squares - sums * sums / count
    for out in outs:
        end = out.shape[0] - 8
        for f in range(fold):
            part = slice(2 * cols * f, 2 * cols * (f + 1))
            out[end + f : end + f + 1, :] = mean[:, part]
            out[end + fold + f : end + fold + f + 1, :] = square[:, part]
        end += 2 * fold
        out[end : end + 1, 0:cols] = own_shift + sums_next / count
        out[end : end + 1, cols : 2 * cols] = squares_next - sums_next * sums_next / count
        out[end + 1 : end + 2, :] = jnp.zeros((1, 2 * cols), F32) + total
        spare = out.shape[0] - end - 2
        if spare:
            out[end + 2 :, :] = jnp.zeros((spare, 2 * cols), F32)


def late_moments(codes, before, shift, sums, tail, own, halo, valid, place, sides, groups, reps, shifts):
    sizes = tuple(chunk[0].shape[0] - HALO for chunk in codes)
    codes = [code for chunk in codes for code in chunk]
    here, cols = own.shape
    feats = shift.shape[1]
    depth = here * (sides - 1) + 2 * HALO
    rows = feats // (groups * reps)
    vmem = pl.BlockSpec(memory_space=pltpu.VMEM)
    outs = pl.pallas_call(
        functools.partial(late_kernel, sizes, sides, groups, reps, shifts),
        in_specs=[pl.BlockSpec(memory_space=pltpu.SMEM)] + [vmem] * (len(codes) + 7),
        out_specs=[vmem] * (reps + 5),
        out_shape=[jax.ShapeDtypeStruct((len(shifts) * rows + 8, 2 * cols), F32)] * reps
        + [
            jax.ShapeDtypeStruct((here * sides, cols), F32),
            jax.ShapeDtypeStruct((feats, depth), BF16),
            jax.ShapeDtypeStruct((feats, depth), BF16),
            jax.ShapeDtypeStruct((depth, 2 * cols), BF16),
            jax.ShapeDtypeStruct((depth, 2 * cols), BF16),
        ],
        scratch_shapes=[
            pltpu.VMEM((depth, feats), F32),
            pltpu.VMEM((depth, 2 * cols), F32),
            pltpu.VMEM((here * sides + HALO, cols), F32),
        ],
        compiler_params=params(),
        cost_estimate=SMALL,
        name="late_moments",
    )(place, *codes, before, shift, sums, tail, own, halo, valid)
    return outs[:reps], outs[reps], outs[reps + 1 :]


def rest_kernel(groups, shifts, place_ref, before_ref, left_high, left_low, right_high, right_low, *outs):
    add_blocks(
        place_ref, shifts, groups, before_ref, (left_high, left_low), (right_high, right_low), outs
    )


def rest_moments(before, factors, place, groups, reps, shifts):
    rows = before.shape[0] // (groups * reps)
    vmem = pl.BlockSpec(memory_space=pltpu.VMEM)
    return pl.pallas_call(
        functools.partial(rest_kernel, groups, shifts),
        in_specs=[pl.BlockSpec(memory_space=pltpu.SMEM)] + [vmem] * 5,
        out_specs=[vmem] * reps,
        out_shape=[jax.ShapeDtypeStruct((len(shifts) * rows, before.shape[1]), F32)] * reps,
        compiler_params=params(),
        cost_estimate=SMALL,
        name="rest_moments",
    )(place, before, *factors)


def rolled(value, first):
    rows, width = value.shape
    wide = jnp.broadcast_to(value, (8, width)) if rows == 1 else value
    return pltpu.roll(wide, lax.rem(width - first, width), 1)[:rows]


def as_column(row):
    return jnp.broadcast_to(row, (8, row.shape[1])).T[:, 0:1]


def code_block(place_ref, groups, reps, s, i, parts, norms, out):
    width = parts[0].shape[1]
    cols = width // 2
    feats = norms.shape[1]
    rows = feats // (groups * reps)
    at = slice(i * rows, (i + 1) * rows)
    total = parts[0][at, :]
    for part in parts[1:]:
        total += part[at, :]
    if s == 0:
        out[...] = total
        return
    there = lax.rem(place_ref[0] + s, groups)
    first = (there * reps + place_ref[2]) * rows
    inverse_cols = jnp.concatenate(
        [rolled(norms[0:1, :], place_ref[1] * cols)[:, :cols], norms[1:2, :cols]], 1
    )
    ratio = total * as_column(rolled(norms[0:1, :], first)[:, :rows]) * inverse_cols
    root = jnp.sqrt(jnp.minimum(jnp.abs(ratio), 1.001)) * CODE
    root = jnp.where(ratio < 0.0, -root, root)
    out[0:rows, :] = jnp.round(root).astype(jnp.int32).astype(jnp.int16)


def first_share_kernel(groups, shifts, place_ref, *refs):
    count = len(shifts)
    parts, outs, codes_out, norms_out = refs[: -count - 2], refs[-count - 2 : -2], refs[-2], refs[-1]
    reps, width = len(parts), parts[0].shape[1]
    cols, feats = width // 2, norms_out.shape[1]
    fold = feats // width
    end = parts[0].shape[0] - 8
    square = jnp.zeros((1, feats), F32)
    square_next = jnp.zeros((1, cols), F32)
    codes = []
    for part in parts:
        own = part[end : end + 8, :]
        squares = [own[fold + f : fold + f + 1] for f in range(fold)]
        final = own[2 * fold : 2 * fold + 1]
        square += jnp.concatenate(squares, 1)
        square_next += final[:, cols:]
        for f in range(fold):
            codes += coded(own[f : f + 1], MEAN_STEP)
        for line in squares:
            codes += coded(jnp.sqrt(jnp.maximum(line, 0.0)), ROOT_STEP)
        pair = coded(final[:, :cols], MEAN_STEP)
        pair_next = coded(jnp.sqrt(jnp.maximum(final[:, cols:], 0.0)), ROOT_STEP)
        codes += [jnp.concatenate(both, 1) for both in zip(pair, pair_next)]
        codes.append(own[2 * fold + 1 : 2 * fold + 2])
    spare = codes_out.shape[0] - len(codes)
    if spare:
        codes.append(jnp.zeros((spare, width), F32))
    codes = jnp.concatenate(codes, 0).astype(jnp.int32).astype(jnp.int16)
    codes_out[...] = codes
    norms_out[...] = jnp.zeros(norms_out.shape, F32)
    norms_out[0:1, :] = lax.rsqrt(jnp.maximum(square, TINY))
    norms_out[1:2, :cols] = lax.rsqrt(jnp.maximum(square_next, TINY))
    for i, (s, out) in enumerate(zip(shifts, outs)):
        code_block(place_ref, groups, reps, s, i, parts, norms_out, out)
        out[out.shape[0] - codes.shape[0] :, :] = codes


def rest_share_kernel(groups, shifts, place_ref, norms_ref, codes_ref, *refs):
    count = len(shifts)
    parts, outs = refs[:-count], refs[-count:]
    for i, (s, out) in enumerate(zip(shifts, outs)):
        code_block(place_ref, groups, len(parts), s, i, parts, norms_ref, out)
        if s:
            out[out.shape[0] - codes_ref.shape[0] :, :] = codes_ref[...]


def first_share(parts, place, groups, shifts, feats):
    width, reps = parts[0].shape[1], len(parts)
    rows = feats // (groups * reps)
    lines = -(-reps * (4 * (feats // width) + 3) // 16) * 16
    vmem = pl.BlockSpec(memory_space=pltpu.VMEM)
    outs = pl.pallas_call(
        functools.partial(first_share_kernel, groups, shifts),
        in_specs=[pl.BlockSpec(memory_space=pltpu.SMEM)] + [vmem] * reps,
        out_specs=[vmem] * (len(shifts) + 2),
        out_shape=[jax.ShapeDtypeStruct((rows + lines, width), jnp.int16)] * len(shifts)
        + [
            jax.ShapeDtypeStruct((lines, width), jnp.int16),
            jax.ShapeDtypeStruct((8, feats), F32),
        ],
        compiler_params=params(),
        cost_estimate=SMALL,
        name="first_share",
    )(place, *parts)
    return outs[:-2], outs[-2], outs[-1]


def rest_share(parts, norms, codes, place, groups, shifts):
    width = parts[0].shape[1]
    rows = parts[0].shape[0] // len(shifts)
    coded_shape = jax.ShapeDtypeStruct((rows + codes.shape[0], width), jnp.int16)
    vmem = pl.BlockSpec(memory_space=pltpu.VMEM)
    return pl.pallas_call(
        functools.partial(rest_share_kernel, groups, shifts),
        in_specs=[pl.BlockSpec(memory_space=pltpu.SMEM)] + [vmem] * (len(parts) + 2),
        out_specs=[vmem] * len(shifts),
        out_shape=[coded_shape if s else jax.ShapeDtypeStruct((rows, width), F32) for s in shifts],
        compiler_params=params(),
        cost_estimate=SMALL,
        name="rest_share",
    )(place, norms, codes, *parts)


def finish_kernel(reps, place_ref, kept_ref, codes_ref, *refs):
    blocks = refs[:-5]
    shift_ref, own_ref, inst_out, lag_out, projections_out = refs[-5:]
    rows, cols = inst_out.shape
    feats = shift_ref.shape[1]
    width = 2 * cols
    fold = feats // width
    count = jnp.zeros((1, 1), F32)
    mean = jnp.zeros((1, feats), F32)
    mean_next = jnp.zeros((1, cols), F32)
    stats = []
    for block in (codes_ref,) + tuple(blocks):
        start = 0 if block is codes_ref else rows
        codes = block[start:, :].astype(jnp.int32).astype(F32)
        at = 0
        for r in range(reps):
            lines = [codes[at + i : at + i + 1] for i in range(4 * fold + 3)]
            at += 4 * fold + 3
            pairs = [(lines[2 * i], lines[2 * i + 1]) for i in range(2 * fold + 1)]
            means = [decoded(*pair, MEAN_STEP) for pair in pairs[:fold]]
            roots = [decoded(*pair, ROOT_STEP) for pair in pairs[fold : 2 * fold]]
            one, two = pairs[2 * fold]
            roots_next = decoded(one[:, cols:], two[:, cols:], ROOT_STEP)
            here = [
                jnp.concatenate(means, 1),
                jnp.concatenate([root * root for root in roots], 1),
                decoded(one[:, :cols], two[:, :cols], MEAN_STEP),
                roots_next * roots_next,
                lines[-1][:, 0:1],
            ]
            stats.append(here)
            count += here[4]
            mean += here[4] * here[0]
            mean_next += here[4] * here[2]
    mean, mean_next = mean / count, mean_next / count
    spread = jnp.zeros((1, feats), F32)
    spread_next = jnp.zeros((1, cols), F32)
    away, away_next = [], []
    for here in stats:
        away.append(here[0] - mean)
        away_next.append(here[2] - mean_next)
        spread += here[1] + here[4] * away[-1] * away[-1]
        spread_next += here[3] + here[4] * away_next[-1] * away_next[-1]
    numbers = jnp.concatenate([here[4] for here in stats], 0)
    scale = 1.0 / jnp.sqrt(spread / count + 1e-05)
    scale_next = 1.0 / jnp.sqrt(spread_next / count + 1e-05)
    away = jnp.concatenate(away, 0)

    first_row = (place_ref[0] * reps + place_ref[2]) * rows
    first_col = place_ref[1] * cols
    right = numbers * jnp.concatenate(
        [rolled(away, first_col)[:, :cols], jnp.concatenate(away_next, 0)], 1
    )
    moment = kept_ref[...] + jnp.dot(
        rolled(away, first_row)[:, :rows].T,
        right,
        precision=lax.Precision.HIGHEST,
        preferred_element_type=F32,
    )
    for g, block in enumerate(blocks):
        here = stats[(g + 1) * reps : (g + 2) * reps]
        root = jnp.sqrt(sum(one[1] for one in here))
        root_next = jnp.sqrt(sum(one[3] for one in here))
        root_rows = as_column(rolled(root, first_row)[:, :rows])
        root_cols = jnp.concatenate([rolled(root, first_col)[:, :cols], root_next], 1)
        code = block[0:rows, :].astype(jnp.int32).astype(F32) * (1.0 / CODE)
        moment += code * jnp.abs(code) * root_rows * root_cols
    scale_cols = rolled(scale, first_col)[:, :cols]
    moment = moment / count * as_column(rolled(scale, first_row)[:, :rows])
    inst_out[...] = moment[:, 0:cols] * scale_cols
    lag_out[...] = moment[:, cols : 2 * cols] * scale_next
    offset = rolled(shift_ref[...] - mean, first_col)[:, :cols]
    projections_out[...] = (own_ref[...] + offset) * scale_cols


def finish(kept, codes, blocks, shift, own, place, reps):
    rows = kept.shape[0]
    frames, cols = own.shape
    vmem = pl.BlockSpec(memory_space=pltpu.VMEM)
    return pl.pallas_call(
        functools.partial(finish_kernel, reps),
        in_specs=[pl.BlockSpec(memory_space=pltpu.SMEM)] + [vmem] * (len(blocks) + 4),
        out_specs=[vmem] * 3,
        out_shape=[
            jax.ShapeDtypeStruct((rows, cols), F32),
            jax.ShapeDtypeStruct((rows, cols), F32),
            jax.ShapeDtypeStruct((frames, cols), F32),
        ],
        compiler_params=params(),
        cost_estimate=SMALL,
        name="finish",
    )(place, kept, codes, *blocks, shift, own)


def upto(width):
    rows = lax.broadcasted_iota(jnp.int32, (width, width), 0)
    lanes = lax.broadcasted_iota(jnp.int32, (width, width), 1)
    return (lanes <= rows).astype(F32).astype(BF16)


def ranked(pairs, first, width, below):
    atoms = lax.broadcasted_iota(jnp.int32, (width, 128), 0) + first
    hit = jnp.zeros((width, 128), F32)
    for block in pairs:
        for r in range(2):
            for l in range(0, block.shape[1], 128):
                hit = jnp.where(block[r : r + 1, l : l + 128] == atoms, 1.0, hit)
    used = jnp.broadcast_to(jnp.max(hit, axis=1, keepdims=True), (width, 128))
    order = jnp.dot(below, used.astype(BF16), preferred_element_type=F32)
    return jnp.where(used > 0.0, order - 1.0, -1.0), order[width - 1 : width, :]


def signs_kernel(groups, width, slot_count, place_ref, after_ref, *refs):
    pairs, (signs_out, most_out) = refs[:-2], refs[-2:]
    sides = len(pairs)
    below = upto(width)
    number = lax.broadcasted_iota(jnp.int32, (width, 128), 0) + 1
    high = (number // 8).astype(F32).astype(BF16)
    low = (number % 8).astype(F32).astype(BF16)
    slots = lax.broadcasted_iota(jnp.int32, (slot_count, width), 0).astype(F32)
    most = jnp.zeros((1, 128), F32)
    for s in range(groups):
        first = lax.rem(place_ref[0] + groups - s, groups) * width
        rank, count = ranked(pairs, first, width, below)
        most = jnp.maximum(most, count)
        chosen = (rank.T[0:1, :] == slots).astype(F32).astype(BF16)
        listed = 8.0 * jnp.dot(chosen, high, preferred_element_type=F32)
        listed += jnp.dot(chosen, low, preferred_element_type=F32)
        listed = listed.astype(jnp.int32) - 1
        listed = jnp.where(listed < 0, -1, listed + first)
        for b, block in enumerate(pairs):
            cols = block.shape[1]
            there = lax.rem(place_ref[1] + sides - b, sides) * cols
            for l in range(0, cols, 128):
                one = (block[0:1, l : l + 128] == listed).astype(F32)
                two = (block[1:2, l : l + 128] == listed).astype(F32)
                at = pl.ds(pl.multiple_of(there + l, 128), 128)
                rows = slice(s * slot_count, (s + 1) * slot_count)
                signs_out[rows, at] = (one - two).astype(BF16)
    most_out[...] = most


def pair_signs(pairs, after, place, groups, width, cap):
    feats = len(pairs) * pairs[0].shape[1]
    vmem = pl.BlockSpec(memory_space=pltpu.VMEM)
    return pl.pallas_call(
        functools.partial(signs_kernel, groups, width, slot_rows(cap)),
        in_specs=[pl.BlockSpec(memory_space=pltpu.SMEM), pl.BlockSpec(memory_space=pl.ANY)]
        + [vmem] * len(pairs),
        out_specs=[vmem] * 2,
        out_shape=[
            jax.ShapeDtypeStruct((groups * slot_rows(cap), feats), BF16),
            jax.ShapeDtypeStruct((1, 128), F32),
        ],
        compiler_params=params(),
        cost_estimate=LARGE,
        name="pair_signs",
    )(place, after, *pairs)


def chunk_sizes(frames):
    last = frames // 8 * 3
    return frames - last, last


def with_cap(cap, coords, pairs, traj_ids, place):
    groups, sides = lax.axis_size("atoms"), lax.axis_size("feat")
    atom_index, feat_index = place[0], place[1]
    width = coords.shape[2]
    frames = coords.shape[1] // groups
    cols = pairs[0].shape[1]
    feats = cols * sides
    sizes = chunk_sizes(frames // sides)

    far, near = shifts_of("atoms")[0], shifts_of("atoms")[1:]
    chosen, traj_ids, pairs, rows, later, block = first_pick(
        coords, traj_ids, pairs, cap, place, sizes, near, far
    )
    order = near + [0]
    picked = {far: block} | dict(zip(order, pick([rows], chosen, block)))
    signs, most_used = pair_signs(pairs, block, place, groups, width, cap)
    order = [far] + order
    arrived = []
    for j in range(2):
        if j:
            picked = dict(zip(order, pick([later], chosen, most_used)))
        moved = {s: rotated(picked[s], "atoms", s) if s else picked[s] for s in order}
        arrived.append([moved[s] for s in range(groups)])

    ids = jnp.concatenate([traj_ids[0], jnp.full((LAG,), -1, jnp.int32)])
    offset = atom_index * frames
    ids_now = lax.dynamic_slice_in_dim(ids, offset, frames)
    ids_later = lax.dynamic_slice_in_dim(ids, offset + LAG, frames)
    valid = (ids_now == ids_later).astype(F32)[:, None]

    own_pieces, codes, after = [], [], arrived[-1][0]
    for j, blocks in enumerate(arrived):
        block, code = distances(blocks, signs, after, cap)
        after = block
        own_pieces.append(block)
        codes.append([rotated(code, "feat", s) for s in range(1, sides)])
        if j == 0:
            opening = passed_down(block[:HALO], "atoms")
    halo = lax.dynamic_slice_in_dim(opening, feat_index * cols, cols, 1)
    opening = opening + 0.0 * own_pieces[-1][:HALO]
    for s in range(1, sides):
        there = lax.rem(feat_index + s, sides)
        sent = rotated(lax.dynamic_slice_in_dim(opening, there * cols, cols, 1), "feat", s)
        halo = jnp.where(feat_index == s, sent, halo)

    reps = lax.axis_size("rep")
    shifts = shifts_of("atoms") + [0]
    shifts = tuple(shifts[: groups // 2]), tuple(shifts[groups // 2 :])
    before, own, shift, sums, tail = early_moments(own_pieces, valid, place, sides)
    parts, own, factors = late_moments(
        codes, before, shift, sums, tail, own, halo, valid, place, sides, groups, reps, shifts[0]
    )
    parts = [parts[0]] + [rotated(parts[r], "rep", r) for r in range(1, reps)]
    rest = rest_moments(before, factors, place, groups, reps, shifts[1])
    rest = [rest[0]] + [rotated(rest[r], "rep", r) for r in range(1, reps)]
    blocks, stats, norms = first_share(parts, place, groups, shifts[0], feats)
    blocks = [rotated(block, "atoms", s) for s, block in zip(shifts[0], blocks)]
    *more, kept = rest_share(rest, norms, stats, place, groups, shifts[1])
    blocks += [rotated(block, "atoms", s) for s, block in zip(shifts[1], more)]
    corr_inst, corr_lag, projections = finish(kept, stats, blocks, shift, own, place, reps)
    return (corr_inst, corr_lag, projections[None]), most_used[0, 0]


def shards(atom_coords, atom_pairs, traj_ids):
    place = [lax.axis_index(axis) for axis in ("atoms", "feat", "rep")]
    place = jnp.stack(place).astype(jnp.int32)
    width = atom_coords.shape[3]
    coords = jnp.transpose(atom_coords[0], (1, 0, 2))
    pairs = [atom_pairs] + [rotated(atom_pairs, "feat", s) for s in range(1, lax.axis_size("feat"))]
    cap = min(width, packed(width * 5 // 9) // 3)
    outs, most_used = with_cap(cap, coords, pairs, traj_ids, place)

    def again(carry):
        same = [block + (carry[0] - 1) for block in pairs]
        return carry[0] - 1, with_cap(width, coords, same, traj_ids, place)[0]

    overflow = (most_used > cap).astype(jnp.int32)
    return lax.while_loop(lambda carry: carry[0] > 0, again, (overflow, outs))[1]


def solution(mesh):
    placed = (P(("grp", "rep"), None, None, "atoms"), P(None, "feat"), P(("grp", "rep"), None))
    return jax.shard_map(
        shards,
        mesh=mesh,
        in_specs=placed,
        out_specs=(
            P(("grp", "atoms", "rep"), "feat"),
            P(("grp", "atoms", "rep"), "feat"),
            P(("grp", "rep"), "atoms", "feat"),
        ),
        check_vma=False,
    )
```

```python
import functools

import jax
import jax.numpy as jnp
from jax import lax
from jax.experimental import pallas as pl
from jax.experimental.pallas import tpu as pltpu
from jax.sharding import PartitionSpec as P

LAG = 10
HALO = 16
CHUNK = 64
CODE = 32700.0
FINE = 60000.0
MEAN_STEP = 0.001
ROOT_STEP = 0.02
TINY = 1e-30
REACH = 1e-6
VMEM_LIMIT = 16 * 1024 * 1024
F32 = jnp.float32
BF16 = jnp.bfloat16
LARGE = pl.CostEstimate(flops=3*10**10, bytes_accessed=1024, transcendentals=0)
SMALL = pl.CostEstimate(flops=1024, bytes_accessed=1024, transcendentals=0)


def rotated(block, axis, shift):
    size = lax.axis_size(axis)
    return lax.ppermute(block, axis, [(i, (i + shift) % size) for i in range(size)])


def shifts_of(axis):
    size = lax.axis_size(axis)
    return sorted(range(1, size), key=lambda s: -min(s, size - s))


def passed_down(block, axis):
    return lax.ppermute(block, axis, [(i + 1, i) for i in range(lax.axis_size(axis) - 1)])


def params():
    return pltpu.CompilerParams(vmem_limit_bytes=VMEM_LIMIT)


def start_rows(shifts, start, place_ref, coords_ref, rows_ref, sems):
    groups, sides = lax.axis_size("atoms"), lax.axis_size("feat")
    frames = coords_ref.shape[1] // groups
    copies = []
    for i, s in enumerate(shifts):
        there = lax.rem(place_ref[0] + s, groups)
        row = there * frames + place_ref[1] * (frames // sides) + start
        rows = pl.ds(pl.multiple_of(row, HALO), rows_ref.shape[2])
        copies.append(
            pltpu.make_async_copy(coords_ref.at[:, rows, :], rows_ref.at[i], sems.at[i])
        )
        copies[-1].start()
    return copies


def packed(cap):
    return -(-3 * cap // 128) * 128


def slot_rows(cap):
    return -(-cap // HALO) * HALO


def pick_rows(rows, chosen, out):
    _, size, width = rows.shape
    cap = chosen.shape[1]
    picked = jnp.dot(
        rows[...].reshape(3 * size, width), chosen, preferred_element_type=F32
    ).astype(BF16)
    for k in range(3):
        out[:, k * cap : (k + 1) * cap] = picked[k * size : (k + 1) * size, :]
    if out.shape[1] > 3 * cap:
        out[:, 3 * cap :] = jnp.zeros((size, out.shape[1] - 3 * cap), BF16)


def first_pick_kernel(sides, near, far, place_ref, coords_ref, ids_ref, *refs):
    pairs, refs = refs[:sides], refs[sides:]
    chosen_ref, ids_out, pairs_out, refs = refs[0], refs[1], refs[2 : 2 + sides], refs[2 + sides :]
    near_out, later_out, out, rows_ref, sems = refs
    width, cap = chosen_ref.shape
    size = rows_ref.shape[2]
    first = start_rows([far], 0, place_ref, coords_ref, rows_ref, sems.at[0])
    others = start_rows(near + [0], 0, place_ref, coords_ref, near_out, sems.at[1])
    others += start_rows([far] + near + [0], size, place_ref, coords_ref, later_out, sems.at[2])
    ids_out[...] = ids_ref[...]
    for block, copy in zip(pairs, pairs_out):
        copy[...] = block[...]
    rank, _ = ranked(pairs, place_ref[0] * width, width, upto(width))
    lanes = lax.broadcasted_iota(jnp.int32, (width, 128), 1)
    for l in range(0, cap, 128):
        some = min(128, cap - l)
        here = (rank == (lanes + l).astype(F32)).astype(F32).astype(BF16)
        chosen_ref[:, l : l + some] = here[:, :some]
    first[0].wait()
    pick_rows(rows_ref.at[0], chosen_ref[...], out)
    for copy in others:
        copy.wait()


def first_pick(coords, ids, pairs, cap, place, sizes, near, far):
    width = coords.shape[2]
    size, later = sizes
    vmem = pl.BlockSpec(memory_space=pltpu.VMEM)
    outs = pl.pallas_call(
        functools.partial(first_pick_kernel, len(pairs), near, far),
        in_specs=[
            pl.BlockSpec(memory_space=pltpu.SMEM),
            pl.BlockSpec(memory_space=pltpu.HBM),
        ]
        + [vmem] * (len(pairs) + 1),
        out_specs=[vmem] * (5 + len(pairs)),
        out_shape=[
            jax.ShapeDtypeStruct((width, cap), BF16),
            jax.ShapeDtypeStruct(ids.shape, ids.dtype),
        ]
        + [jax.ShapeDtypeStruct(block.shape, block.dtype) for block in pairs]
        + [
            jax.ShapeDtypeStruct((len(near) + 1, 3, size, width), BF16),
            jax.ShapeDtypeStruct((len(near) + 2, 3, later, width), BF16),
            jax.ShapeDtypeStruct((size, packed(cap)), BF16),
        ],
        scratch_shapes=[
            pltpu.VMEM((1, 3, size, width), BF16),
            pltpu.SemaphoreType.DMA((3, len(near) + 2)),
        ],
        compiler_params=params(),
        cost_estimate=SMALL,
        name="first_pick",
    )(place, coords, ids, *pairs)
    last = 2 + len(pairs)
    return outs[0], outs[1], outs[2:last], outs[last], outs[last + 1], outs[last + 2]


def pick_kernel(counts, chosen_ref, after_ref, *refs):
    rows_refs, outs = refs[: len(counts)], list(refs[len(counts) :])
    for rows_ref, count in zip(rows_refs, counts):
        for i in range(count):
            pick_rows(rows_ref.at[i], chosen_ref[...], outs.pop(0))


def pick(rows, chosen, after):
    cap = chosen.shape[1]
    counts = [some.shape[0] for some in rows]
    vmem = pl.BlockSpec(memory_space=pltpu.VMEM)
    return pl.pallas_call(
        functools.partial(pick_kernel, counts),
        in_specs=[vmem, pl.BlockSpec(memory_space=pl.ANY)] + [vmem] * len(rows),
        out_specs=[vmem] * sum(counts),
        out_shape=[
            jax.ShapeDtypeStruct((some.shape[2], packed(cap)), BF16)
            for some in rows
            for _ in range(some.shape[0])
        ],
        compiler_params=params(),
        cost_estimate=SMALL,
        name="pick",
    )(chosen, after, *rows)


def coded(value, step):
    first = jnp.round(value / step)
    second = jnp.round((value - first * step) * (FINE / step))
    return [first, second]


def decoded(first, second, step):
    return first * step + second * (step / FINE)


def decoded_piece(codes, rows):
    size = codes.shape[0] - HALO
    ends = codes[size:, :].astype(jnp.int32).astype(F32)
    middle = decoded(ends[0:1], ends[1:2], MEAN_STEP)
    reach = decoded(ends[2:3], ends[3:4], MEAN_STEP)
    return middle + codes[0:rows, :].astype(jnp.int32).astype(F32) * (reach * (1.0 / CODE))


def distance_kernel(cap, *refs):
    blocks, (signs_ref, after_ref, out, codes_out, joined) = refs[:-5], refs[-5:]
    size = blocks[0].shape[0]
    slots = signs_ref.shape[0] // len(blocks)
    for s, block in enumerate(blocks):
        for k in range(3):
            rows = slice(k * size, (k + 1) * size)
            joined[rows, s * slots : s * slots + cap] = block[:, k * cap : (k + 1) * cap]
        if slots > cap:
            joined[:, s * slots + cap : (s + 1) * slots] = jnp.zeros((3 * size, slots - cap), BF16)
    delta = jnp.dot(joined[...], signs_ref[...], preferred_element_type=F32)
    square = delta * delta
    total = square[:size] + square[size : 2 * size] + square[2 * size :]
    value = jnp.sqrt(total + 0.01)
    out[...] = value
    least, most = jnp.min(value, 0, keepdims=True), jnp.max(value, 0, keepdims=True)
    ends = coded(0.5 * (most + least), MEAN_STEP) + coded(0.5 * (most - least), MEAN_STEP)
    middle = decoded(ends[0], ends[1], MEAN_STEP)
    reach = decoded(ends[2], ends[3], MEAN_STEP)
    ratio = (value - middle) * (CODE / jnp.maximum(reach, REACH))
    ratio = jnp.round(jnp.clip(ratio, -32767.0, 32767.0))
    codes_out[0:size, :] = ratio.astype(jnp.int32).astype(jnp.int16)
    ends = jnp.concatenate(ends + [jnp.zeros((HALO - 4, out.shape[1]), F32)], 0)
    codes_out[size:, :] = ends.astype(jnp.int32).astype(jnp.int16)


def distances(blocks, signs, after, cap):
    size = blocks[0].shape[0]
    vmem = pl.BlockSpec(memory_space=pltpu.VMEM)
    return pl.pallas_call(
        functools.partial(distance_kernel, cap),
        in_specs=[vmem] * (len(blocks) + 1) + [pl.BlockSpec(memory_space=pl.ANY)],
        out_specs=[vmem] * 2,
        out_shape=[
            jax.ShapeDtypeStruct((size, signs.shape[1]), F32),
            jax.ShapeDtypeStruct((size + HALO, signs.shape[1]), jnp.int16),
        ],
        scratch_shapes=[pltpu.VMEM((3 * size, signs.shape[0]), BF16)],
        compiler_params=params(),
        cost_estimate=LARGE,
        name="distances",
    )(*blocks, signs, after)


def split_in_two(value):
    high = value.astype(BF16)
    return high, (value - high.astype(F32)).astype(BF16)


def product(left, right):
    left_high, left_low = split_in_two(left)
    right_high, right_low = split_in_two(right)
    left_high, left_low = left_high.T, left_low.T
    total = jnp.dot(left_high, right_high, preferred_element_type=F32)
    total += jnp.dot(left_high, right_low, preferred_element_type=F32)
    return total + jnp.dot(left_low, right_high, preferred_element_type=F32)


def row_sum(value):
    return jnp.sum(value, 0, keepdims=True)


def side_columns(side, sides, cols, write):
    for s in range(sides):

        @pl.when(side == s)
        def _():
            write(slice(s * cols, (s + 1) * cols))


def early_kernel(chunks, sides, place_ref, *refs):
    pieces = refs[:chunks]
    valid_ref, out, own_out, shift_out, sums_out, tail_out, every = refs[chunks:]
    frames = every.shape[0]
    cols = own_out.shape[1]
    row = 0
    for piece in pieces:
        every[row : row + piece.shape[0], :] = piece[...]
        row += piece.shape[0]
    side = place_ref[1]
    valid = valid_ref[pl.ds(pl.multiple_of(side * frames, HALO), frames), :]
    count = jnp.maximum(jnp.sum(valid), 1.0)
    shift = row_sum(valid * every[...]) / count
    shift_out[...] = shift
    every[...] = every[...] - shift
    tail_out[...] = every[frames - HALO : frames, :]

    def keep_own(part):
        own_out[...] = every[:, part]

    side_columns(side, sides, cols, keep_own)
    now = every[...]
    own = own_out[...]
    weighed = valid * now
    later = own[LAG:frames, :]
    weighed_later = valid[: frames - LAG] * later
    sums_out[0:1, :] = row_sum(weighed)
    sums_out[1:2, :] = row_sum(weighed * now)
    sums_out[2:3, 0:cols] = row_sum(weighed_later)
    sums_out[3:4, 0:cols] = row_sum(weighed_later * later)
    weighed_later = jnp.concatenate([weighed_later, jnp.zeros((LAG, cols), F32)], 0)
    out[...] = product(now, jnp.concatenate([valid * own, weighed_later], 1))


def early_moments(pieces, valid, place, sides):
    frames, feats = sum(piece.shape[0] for piece in pieces), pieces[0].shape[1]
    cols = feats // sides
    vmem = pl.BlockSpec(memory_space=pltpu.VMEM)
    return pl.pallas_call(
        functools.partial(early_kernel, len(pieces), sides),
        in_specs=[pl.BlockSpec(memory_space=pltpu.SMEM)] + [vmem] * (len(pieces) + 1),
        out_specs=[vmem] * 5,
        out_shape=[
            jax.ShapeDtypeStruct((feats, 2 * cols), F32),
            jax.ShapeDtypeStruct((frames, cols), F32),
            jax.ShapeDtypeStruct((1, feats), F32),
            jax.ShapeDtypeStruct((4, feats), F32),
            jax.ShapeDtypeStruct((HALO, feats), F32),
        ],
        scratch_shapes=[pltpu.VMEM((frames, feats), F32)],
        compiler_params=params(),
        cost_estimate=SMALL,
        name="early_moments",
    )(place, *pieces, valid)


def add_blocks(place_ref, shifts, groups, before_ref, left_refs, right_refs, outs):
    reps = len(outs)
    rows = before_ref.shape[0] // (groups * reps)
    left_high, left_low = left_refs
    right_high, right_low = right_refs[0][...], right_refs[1][...]
    for r in reversed(range(reps)):
        rep = lax.rem(place_ref[2] + r, reps)
        for i, s in enumerate(shifts):
            there = lax.rem(place_ref[0] + s, groups)
            at = pl.ds(pl.multiple_of((there * reps + rep) * rows, rows), rows)
            part = before_ref[at, :]
            part += jnp.dot(left_high[at, :], right_high, preferred_element_type=F32)
            part += jnp.dot(left_high[at, :], right_low, preferred_element_type=F32)
            part += jnp.dot(left_low[at, :], right_high, preferred_element_type=F32)
            outs[r][i * rows : (i + 1) * rows, :] = part


def late_kernel(sizes, sides, groups, reps, shifts, place_ref, *refs):
    chunks = len(sizes)
    codes = refs[: chunks * (sides - 1)]
    refs = refs[chunks * (sides - 1) :]
    before_ref, shift_ref, sums_ref, tail_ref, own_ref, halo_ref, valid_ref = refs[:7]
    outs = refs[7 : 7 + reps]
    own_out, left_high, left_low, right_high, right_low, left, right, own = refs[7 + reps :]
    here, cols = own_ref.shape
    frames, feats = here * sides, shift_ref.shape[1]
    side = place_ref[1]
    shift = shift_ref[...]
    bases = [pl.multiple_of(lax.rem(side + sides - s, sides) * here, HALO) for s in range(sides)]
    left[0:HALO, :] = tail_ref[...]
    row = HALO
    for s in range(1, sides):
        for j, size in enumerate(sizes):
            left[row : row + size, :] = decoded_piece(codes[j * (sides - 1) + s - 1], size) - shift
            row += size
    own[pl.ds(bases[0], here), :] = own_ref[...]

    def keep_own(part):
        own[frames:, :] = halo_ref[...] - shift[:, part]
        for s in range(1, sides):
            rows = slice(HALO + (s - 1) * here, HALO + s * here)
            own[pl.ds(bases[s], here), :] = left[rows, part]

    side_columns(side, sides, cols, keep_own)
    own_out[...] = own[0:frames, :]
    valid_all = valid_ref[...]
    total = jnp.sum(valid_all)
    count = jnp.maximum(total, 1.0)
    sums, squares = sums_ref[0:1, :], sums_ref[1:2, :]
    sums_next, squares_next = sums_ref[2:3, 0:cols], sums_ref[3:4, 0:cols]
    end = bases[0] + here - HALO
    later = own[pl.ds(pl.multiple_of(end, HALO), 2 * HALO), :][LAG : LAG + HALO]
    crossing = lax.broadcasted_iota(jnp.int32, (HALO, 1), 0) >= HALO - LAG
    valid = valid_ref[pl.ds(pl.multiple_of(end, HALO), HALO), :]
    weighed_later = jnp.where(crossing, valid * later, 0.0)
    sums_next += row_sum(weighed_later)
    squares_next += row_sum(weighed_later * later)
    right[0:HALO, 0:cols] = jnp.zeros((HALO, cols), F32)
    right[0:HALO, cols : 2 * cols] = weighed_later
    for s in range(1, sides):
        rows = slice(HALO + (s - 1) * here, HALO + s * here)
        valid = valid_ref[pl.ds(bases[s], here), :]
        weighed = valid * left[rows, :]
        sums += row_sum(weighed)
        squares += row_sum(weighed * left[rows, :])
        around = own[pl.ds(bases[s], here + HALO), :]
        right[rows, 0:cols] = valid * around[0:here]
        later = around[LAG : LAG + here]
        weighed_later = valid * later
        right[rows, cols : 2 * cols] = weighed_later
        sums_next += row_sum(weighed_later)
        squares_next += row_sum(weighed_later * later)
    own_sums = jnp.zeros((1, cols), F32)
    own_shift = jnp.zeros((1, cols), F32)
    for s in range(sides):
        mine = (side == s).astype(F32)
        own_sums += mine * sums[:, s * cols : (s + 1) * cols]
        own_shift += mine * shift[:, s * cols : (s + 1) * cols]
    first = lax.broadcasted_iota(jnp.int32, (HALO, 1), 0) == 0
    last = left.shape[0] - HALO
    left[last:, :] = jnp.where(first, sums, 0.0)
    right[last:, 0:cols] = jnp.where(first, -own_sums / count, 0.0)
    right[last:, cols : 2 * cols] = jnp.where(first, -sums_next / count, 0.0)
    high, low = split_in_two(left[...])
    left_high[...] = high.T
    left_low[...] = low.T
    right_high[...], right_low[...] = split_in_two(right[...])
    add_blocks(
        place_ref, shifts, groups, before_ref, (left_high, left_low), (right_high, right_low), outs
    )
    fold = feats // (2 * cols)
    mean, square = shift + sums / count, squares - sums * sums / count
    for out in outs:
        end = out.shape[0] - 8
        for f in range(fold):
            part = slice(2 * cols * f, 2 * cols * (f + 1))
            out[end + f : end + f + 1, :] = mean[:, part]
            out[end + fold + f : end + fold + f + 1, :] = square[:, part]
        end += 2 * fold
        out[end : end + 1, 0:cols] = own_shift + sums_next / count
        out[end : end + 1, cols : 2 * cols] = squares_next - sums_next * sums_next / count
        out[end + 1 : end + 2, :] = jnp.zeros((1, 2 * cols), F32) + total
        spare = out.shape[0] - end - 2
        if spare:
            out[end + 2 :, :] = jnp.zeros((spare, 2 * cols), F32)


def late_moments(codes, before, shift, sums, tail, own, halo, valid, place, sides, groups, reps, shifts):
    sizes = tuple(chunk[0].shape[0] - HALO for chunk in codes)
    codes = [code for chunk in codes for code in chunk]
    here, cols = own.shape
    feats = shift.shape[1]
    depth = here * (sides - 1) + 2 * HALO
    rows = feats // (groups * reps)
    vmem = pl.BlockSpec(memory_space=pltpu.VMEM)
    outs = pl.pallas_call(
        functools.partial(late_kernel, sizes, sides, groups, reps, shifts),
        in_specs=[pl.BlockSpec(memory_space=pltpu.SMEM)] + [vmem] * (len(codes) + 7),
        out_specs=[vmem] * (reps + 5),
        out_shape=[jax.ShapeDtypeStruct((len(shifts) * rows + 8, 2 * cols), F32)] * reps
        + [
            jax.ShapeDtypeStruct((here * sides, cols), F32),
            jax.ShapeDtypeStruct((feats, depth), BF16),
            jax.ShapeDtypeStruct((feats, depth), BF16),
            jax.ShapeDtypeStruct((depth, 2 * cols), BF16),
            jax.ShapeDtypeStruct((depth, 2 * cols), BF16),
        ],
        scratch_shapes=[
            pltpu.VMEM((depth, feats), F32),
            pltpu.VMEM((depth, 2 * cols), F32),
            pltpu.VMEM((here * sides + HALO, cols), F32),
        ],
        compiler_params=params(),
        cost_estimate=SMALL,
        name="late_moments",
    )(place, *codes, before, shift, sums, tail, own, halo, valid)
    return outs[:reps], outs[reps], outs[reps + 1 :]


def rest_kernel(groups, shifts, place_ref, before_ref, left_high, left_low, right_high, right_low, *outs):
    add_blocks(
        place_ref, shifts, groups, before_ref, (left_high, left_low), (right_high, right_low), outs
    )


def rest_moments(before, factors, place, groups, reps, shifts):
    rows = before.shape[0] // (groups * reps)
    vmem = pl.BlockSpec(memory_space=pltpu.VMEM)
    return pl.pallas_call(
        functools.partial(rest_kernel, groups, shifts),
        in_specs=[pl.BlockSpec(memory_space=pltpu.SMEM)] + [vmem] * 5,
        out_specs=[vmem] * reps,
        out_shape=[jax.ShapeDtypeStruct((len(shifts) * rows, before.shape[1]), F32)] * reps,
        compiler_params=params(),
        cost_estimate=SMALL,
        name="rest_moments",
    )(place, before, *factors)


def rolled(value, first):
    rows, width = value.shape
    wide = jnp.broadcast_to(value, (8, width)) if rows == 1 else value
    return pltpu.roll(wide, lax.rem(width - first, width), 1)[:rows]


def as_column(row):
    return jnp.broadcast_to(row, (8, row.shape[1])).T[:, 0:1]


def code_block(place_ref, groups, reps, s, i, parts, norms, out):
    width = parts[0].shape[1]
    cols = width // 2
    feats = norms.shape[1]
    rows = feats // (groups * reps)
    at = slice(i * rows, (i + 1) * rows)
    total = parts[0][at, :]
    for part in parts[1:]:
        total += part[at, :]
    if s == 0:
        out[...] = total
        return
    there = lax.rem(place_ref[0] + s, groups)
    first = (there * reps + place_ref[2]) * rows
    inverse_cols = jnp.concatenate(
        [rolled(norms[0:1, :], place_ref[1] * cols)[:, :cols], norms[1:2, :cols]], 1
    )
    ratio = total * as_column(rolled(norms[0:1, :], first)[:, :rows]) * inverse_cols
    root = jnp.sqrt(jnp.minimum(jnp.abs(ratio), 1.001)) * CODE
    root = jnp.where(ratio < 0.0, -root, root)
    out[0:rows, :] = jnp.round(root).astype(jnp.int32).astype(jnp.int16)


def first_share_kernel(groups, shifts, place_ref, *refs):
    count = len(shifts)
    parts, outs, codes_out, norms_out = refs[: -count - 2], refs[-count - 2 : -2], refs[-2], refs[-1]
    reps, width = len(parts), parts[0].shape[1]
    cols, feats = width // 2, norms_out.shape[1]
    fold = feats // width
    end = parts[0].shape[0] - 8
    square = jnp.zeros((1, feats), F32)
    square_next = jnp.zeros((1, cols), F32)
    codes = []
    for part in parts:
        own = part[end : end + 8, :]
        squares = [own[fold + f : fold + f + 1] for f in range(fold)]
        final = own[2 * fold : 2 * fold + 1]
        square += jnp.concatenate(squares, 1)
        square_next += final[:, cols:]
        for f in range(fold):
            codes += coded(own[f : f + 1], MEAN_STEP)
        for line in squares:
            codes += coded(jnp.sqrt(jnp.maximum(line, 0.0)), ROOT_STEP)
        pair = coded(final[:, :cols], MEAN_STEP)
        pair_next = coded(jnp.sqrt(jnp.maximum(final[:, cols:], 0.0)), ROOT_STEP)
        codes += [jnp.concatenate(both, 1) for both in zip(pair, pair_next)]
        codes.append(own[2 * fold + 1 : 2 * fold + 2])
    spare = codes_out.shape[0] - len(codes)
    if spare:
        codes.append(jnp.zeros((spare, width), F32))
    codes = jnp.concatenate(codes, 0).astype(jnp.int32).astype(jnp.int16)
    codes_out[...] = codes
    norms_out[...] = jnp.zeros(norms_out.shape, F32)
    norms_out[0:1, :] = lax.rsqrt(jnp.maximum(square, TINY))
    norms_out[1:2, :cols] = lax.rsqrt(jnp.maximum(square_next, TINY))
    for i, (s, out) in enumerate(zip(shifts, outs)):
        code_block(place_ref, groups, reps, s, i, parts, norms_out, out)
        out[out.shape[0] - codes.shape[0] :, :] = codes


def rest_share_kernel(groups, shifts, place_ref, norms_ref, codes_ref, *refs):
    count = len(shifts)
    parts, outs = refs[:-count], refs[-count:]
    for i, (s, out) in enumerate(zip(shifts, outs)):
        code_block(place_ref, groups, len(parts), s, i, parts, norms_ref, out)
        if s:
            out[out.shape[0] - codes_ref.shape[0] :, :] = codes_ref[...]


def first_share(parts, place, groups, shifts, feats):
    width, reps = parts[0].shape[1], len(parts)
    rows = feats // (groups * reps)
    lines = -(-reps * (4 * (feats // width) + 3) // 16) * 16
    vmem = pl.BlockSpec(memory_space=pltpu.VMEM)
    outs = pl.pallas_call(
        functools.partial(first_share_kernel, groups, shifts),
        in_specs=[pl.BlockSpec(memory_space=pltpu.SMEM)] + [vmem] * reps,
        out_specs=[vmem] * (len(shifts) + 2),
        out_shape=[jax.ShapeDtypeStruct((rows + lines, width), jnp.int16)] * len(shifts)
        + [
            jax.ShapeDtypeStruct((lines, width), jnp.int16),
            jax.ShapeDtypeStruct((8, feats), F32),
        ],
        compiler_params=params(),
        cost_estimate=SMALL,
        name="first_share",
    )(place, *parts)
    return outs[:-2], outs[-2], outs[-1]


def rest_share(parts, norms, codes, place, groups, shifts):
    width = parts[0].shape[1]
    rows = parts[0].shape[0] // len(shifts)
    coded_shape = jax.ShapeDtypeStruct((rows + codes.shape[0], width), jnp.int16)
    vmem = pl.BlockSpec(memory_space=pltpu.VMEM)
    return pl.pallas_call(
        functools.partial(rest_share_kernel, groups, shifts),
        in_specs=[pl.BlockSpec(memory_space=pltpu.SMEM)] + [vmem] * (len(parts) + 2),
        out_specs=[vmem] * len(shifts),
        out_shape=[coded_shape if s else jax.ShapeDtypeStruct((rows, width), F32) for s in shifts],
        compiler_params=params(),
        cost_estimate=SMALL,
        name="rest_share",
    )(place, norms, codes, *parts)


def finish_kernel(reps, place_ref, kept_ref, codes_ref, *refs):
    blocks = refs[:-5]
    shift_ref, own_ref, inst_out, lag_out, projections_out = refs[-5:]
    rows, cols = inst_out.shape
    feats = shift_ref.shape[1]
    width = 2 * cols
    fold = feats // width
    count = jnp.zeros((1, 1), F32)
    mean = jnp.zeros((1, feats), F32)
    mean_next = jnp.zeros((1, cols), F32)
    stats = []
    for block in (codes_ref,) + tuple(blocks):
        start = 0 if block is codes_ref else rows
        codes = block[start:, :].astype(jnp.int32).astype(F32)
        at = 0
        for r in range(reps):
            lines = [codes[at + i : at + i + 1] for i in range(4 * fold + 3)]
            at += 4 * fold + 3
            pairs = [(lines[2 * i], lines[2 * i + 1]) for i in range(2 * fold + 1)]
            means = [decoded(*pair, MEAN_STEP) for pair in pairs[:fold]]
            roots = [decoded(*pair, ROOT_STEP) for pair in pairs[fold : 2 * fold]]
            one, two = pairs[2 * fold]
            roots_next = decoded(one[:, cols:], two[:, cols:], ROOT_STEP)
            here = [
                jnp.concatenate(means, 1),
                jnp.concatenate([root * root for root in roots], 1),
                decoded(one[:, :cols], two[:, :cols], MEAN_STEP),
                roots_next * roots_next,
                lines[-1][:, 0:1],
            ]
            stats.append(here)
            count += here[4]
            mean += here[4] * here[0]
            mean_next += here[4] * here[2]
    mean, mean_next = mean / count, mean_next / count
    spread = jnp.zeros((1, feats), F32)
    spread_next = jnp.zeros((1, cols), F32)
    away, away_next = [], []
    for here in stats:
        away.append(here[0] - mean)
        away_next.append(here[2] - mean_next)
        spread += here[1] + here[4] * away[-1] * away[-1]
        spread_next += here[3] + here[4] * away_next[-1] * away_next[-1]
    numbers = jnp.concatenate([here[4] for here in stats], 0)
    scale = 1.0 / jnp.sqrt(spread / count + 1e-05)
    scale_next = 1.0 / jnp.sqrt(spread_next / count + 1e-05)
    away = jnp.concatenate(away, 0)

    first_row = (place_ref[0] * reps + place_ref[2]) * rows
    first_col = place_ref[1] * cols
    right = numbers * jnp.concatenate(
        [rolled(away, first_col)[:, :cols], jnp.concatenate(away_next, 0)], 1
    )
    moment = kept_ref[...] + jnp.dot(
        rolled(away, first_row)[:, :rows].T,
        right,
        precision=lax.Precision.HIGHEST,
        preferred_element_type=F32,
    )
    for g, block in enumerate(blocks):
        here = stats[(g + 1) * reps : (g + 2) * reps]
        root = jnp.sqrt(sum(one[1] for one in here))
        root_next = jnp.sqrt(sum(one[3] for one in here))
        root_rows = as_column(rolled(root, first_row)[:, :rows])
        root_cols = jnp.concatenate([rolled(root, first_col)[:, :cols], root_next], 1)
        code = block[0:rows, :].astype(jnp.int32).astype(F32) * (1.0 / CODE)
        moment += code * jnp.abs(code) * root_rows * root_cols
    scale_cols = rolled(scale, first_col)[:, :cols]
    moment = moment / count * as_column(rolled(scale, first_row)[:, :rows])
    inst_out[...] = moment[:, 0:cols] * scale_cols
    lag_out[...] = moment[:, cols : 2 * cols] * scale_next
    offset = rolled(shift_ref[...] - mean, first_col)[:, :cols]
    projections_out[...] = (own_ref[...] + offset) * scale_cols


def finish(kept, codes, blocks, shift, own, place, reps):
    rows = kept.shape[0]
    frames, cols = own.shape
    vmem = pl.BlockSpec(memory_space=pltpu.VMEM)
    return pl.pallas_call(
        functools.partial(finish_kernel, reps),
        in_specs=[pl.BlockSpec(memory_space=pltpu.SMEM)] + [vmem] * (len(blocks) + 4),
        out_specs=[vmem] * 3,
        out_shape=[
            jax.ShapeDtypeStruct((rows, cols), F32),
            jax.ShapeDtypeStruct((rows, cols), F32),
            jax.ShapeDtypeStruct((frames, cols), F32),
        ],
        compiler_params=params(),
        cost_estimate=SMALL,
        name="finish",
    )(place, kept, codes, *blocks, shift, own)


def upto(width):
    rows = lax.broadcasted_iota(jnp.int32, (width, width), 0)
    lanes = lax.broadcasted_iota(jnp.int32, (width, width), 1)
    return (lanes <= rows).astype(F32).astype(BF16)


def ranked(pairs, first, width, below):
    atoms = lax.broadcasted_iota(jnp.int32, (width, 128), 0) + first
    hit = jnp.zeros((width, 128), F32)
    for block in pairs:
        for r in range(2):
            for l in range(0, block.shape[1], 128):
                hit = jnp.where(block[r : r + 1, l : l + 128] == atoms, 1.0, hit)
    used = jnp.broadcast_to(jnp.max(hit, axis=1, keepdims=True), (width, 128))
    order = jnp.dot(below, used.astype(BF16), preferred_element_type=F32)
    return jnp.where(used > 0.0, order - 1.0, -1.0), order[width - 1 : width, :]


def signs_kernel(groups, width, slot_count, place_ref, after_ref, *refs):
    pairs, (signs_out, most_out) = refs[:-2], refs[-2:]
    sides = len(pairs)
    below = upto(width)
    number = lax.broadcasted_iota(jnp.int32, (width, 128), 0) + 1
    high = (number // 8).astype(F32).astype(BF16)
    low = (number % 8).astype(F32).astype(BF16)
    slots = lax.broadcasted_iota(jnp.int32, (slot_count, width), 0).astype(F32)
    most = jnp.zeros((1, 128), F32)
    for s in range(groups):
        first = lax.rem(place_ref[0] + groups - s, groups) * width
        rank, count = ranked(pairs, first, width, below)
        most = jnp.maximum(most, count)
        chosen = (rank.T[0:1, :] == slots).astype(F32).astype(BF16)
        listed = 8.0 * jnp.dot(chosen, high, preferred_element_type=F32)
        listed += jnp.dot(chosen, low, preferred_element_type=F32)
        listed = listed.astype(jnp.int32) - 1
        listed = jnp.where(listed < 0, -1, listed + first)
        for b, block in enumerate(pairs):
            cols = block.shape[1]
            there = lax.rem(place_ref[1] + sides - b, sides) * cols
            for l in range(0, cols, 128):
                one = (block[0:1, l : l + 128] == listed).astype(F32)
                two = (block[1:2, l : l + 128] == listed).astype(F32)
                at = pl.ds(pl.multiple_of(there + l, 128), 128)
                rows = slice(s * slot_count, (s + 1) * slot_count)
                signs_out[rows, at] = (one - two).astype(BF16)
    most_out[...] = most


def pair_signs(pairs, after, place, groups, width, cap):
    feats = len(pairs) * pairs[0].shape[1]
    vmem = pl.BlockSpec(memory_space=pltpu.VMEM)
    return pl.pallas_call(
        functools.partial(signs_kernel, groups, width, slot_rows(cap)),
        in_specs=[pl.BlockSpec(memory_space=pltpu.SMEM), pl.BlockSpec(memory_space=pl.ANY)]
        + [vmem] * len(pairs),
        out_specs=[vmem] * 2,
        out_shape=[
            jax.ShapeDtypeStruct((groups * slot_rows(cap), feats), BF16),
            jax.ShapeDtypeStruct((1, 128), F32),
        ],
        compiler_params=params(),
        cost_estimate=LARGE,
        name="pair_signs",
    )(place, after, *pairs)


def chunk_sizes(frames):
    last = frames // 8 * 3
    return frames - last, last


def with_cap(cap, coords, pairs, traj_ids, place):
    groups, sides = lax.axis_size("atoms"), lax.axis_size("feat")
    atom_index, feat_index = place[0], place[1]
    width = coords.shape[2]
    frames = coords.shape[1] // groups
    cols = pairs[0].shape[1]
    feats = cols * sides
    sizes = chunk_sizes(frames // sides)

    far, near = shifts_of("atoms")[0], shifts_of("atoms")[1:]
    chosen, traj_ids, pairs, rows, later, block = first_pick(
        coords, traj_ids, pairs, cap, place, sizes, near, far
    )
    order = near + [0]
    picked = {far: block} | dict(zip(order, pick([rows], chosen, block)))
    signs, most_used = pair_signs(pairs, block, place, groups, width, cap)
    order = [far] + order
    arrived = []
    for j in range(2):
        if j:
            picked = dict(zip(order, pick([later], chosen, most_used)))
        moved = {s: rotated(picked[s], "atoms", s) if s else picked[s] for s in order}
        arrived.append([moved[s] for s in range(groups)])

    ids = jnp.concatenate([traj_ids[0], jnp.full((LAG,), -1, jnp.int32)])
    offset = atom_index * frames
    ids_now = lax.dynamic_slice_in_dim(ids, offset, frames)
    ids_later = lax.dynamic_slice_in_dim(ids, offset + LAG, frames)
    valid = (ids_now == ids_later).astype(F32)[:, None]

    own_pieces, codes, after = [], [], arrived[-1][0]
    for j, blocks in enumerate(arrived):
        block, code = distances(blocks, signs, after, cap)
        after = block
        own_pieces.append(block)
        codes.append([rotated(code, "feat", s) for s in range(1, sides)])
        if j == 0:
            opening = passed_down(block[:HALO], "atoms")
    halo = lax.dynamic_slice_in_dim(opening, feat_index * cols, cols, 1)
    opening = opening + 0.0 * own_pieces[-1][:HALO]
    for s in range(1, sides):
        there = lax.rem(feat_index + s, sides)
        sent = rotated(lax.dynamic_slice_in_dim(opening, there * cols, cols, 1), "feat", s)
        halo = jnp.where(feat_index == s, sent, halo)

    reps = lax.axis_size("rep")
    shifts = shifts_of("atoms") + [0]
    shifts = tuple(shifts[: groups // 2]), tuple(shifts[groups // 2 :])
    before, own, shift, sums, tail = early_moments(own_pieces, valid, place, sides)
    parts, own, factors = late_moments(
        codes, before, shift, sums, tail, own, halo, valid, place, sides, groups, reps, shifts[0]
    )
    parts = [parts[0]] + [rotated(parts[r], "rep", r) for r in range(1, reps)]
    rest = rest_moments(before, factors, place, groups, reps, shifts[1])
    rest = [rest[0]] + [rotated(rest[r], "rep", r) for r in range(1, reps)]
    blocks, stats, norms = first_share(parts, place, groups, shifts[0], feats)
    blocks = [rotated(block, "atoms", s) for s, block in zip(shifts[0], blocks)]
    *more, kept = rest_share(rest, norms, stats, place, groups, shifts[1])
    blocks += [rotated(block, "atoms", s) for s, block in zip(shifts[1], more)]
    corr_inst, corr_lag, projections = finish(kept, stats, blocks, shift, own, place, reps)
    return (corr_inst, corr_lag, projections[None]), most_used[0, 0]


def shards(atom_coords, atom_pairs, traj_ids):
    place = [lax.axis_index(axis) for axis in ("atoms", "feat", "rep")]
    place = jnp.stack(place).astype(jnp.int32)
    width = atom_coords.shape[3]
    coords = jnp.transpose(atom_coords[0], (1, 0, 2))
    pairs = [atom_pairs] + [rotated(atom_pairs, "feat", s) for s in range(1, lax.axis_size("feat"))]
    cap = min(width, packed(width * 5 // 9) // 3)
    outs, most_used = with_cap(cap, coords, pairs, traj_ids, place)

    def again(carry):
        same = [block + (carry[0] - 1) for block in pairs]
        return carry[0] - 1, with_cap(width, coords, same, traj_ids, place)[0]

    overflow = (most_used > cap).astype(jnp.int32)
    return lax.while_loop(lambda carry: carry[0] > 0, again, (overflow, outs))[1]


def solution(mesh):
    placed = (P(("grp", "rep"), None, None, "atoms"), P(None, "feat"), P(("grp", "rep"), None))
    return jax.shard_map(
        shards,
        mesh=mesh,
        in_specs=placed,
        out_specs=(
            P(("grp", "atoms", "rep"), "feat"),
            P(("grp", "atoms", "rep"), "feat"),
            P(("grp", "rep"), "atoms", "feat"),
        ),
        check_vma=False,
    )
```

```python
import functools

import jax
import jax.numpy as jnp
from jax import lax
from jax.experimental import pallas as pl
from jax.experimental.pallas import tpu as pltpu
from jax.sharding import PartitionSpec as P

LAG = 10
HALO = 16
CHUNK = 64
CODE = 32700.0
FINE = 60000.0
MEAN_STEP = 0.001
ROOT_STEP = 0.02
TINY = 1e-30
REACH = 1e-6
VMEM_LIMIT = 16 * 1024 * 1024
F32 = jnp.float32
BF16 = jnp.bfloat16
LARGE = pl.CostEstimate(flops=3*10**10, bytes_accessed=1024, transcendentals=0)
SMALL = pl.CostEstimate(flops=1024, bytes_accessed=1024, transcendentals=0)


def rotated(block, axis, shift):
    size = lax.axis_size(axis)
    return lax.ppermute(block, axis, [(i, (i + shift) % size) for i in range(size)])


def shifts_of(axis):
    size = lax.axis_size(axis)
    return sorted(range(1, size), key=lambda s: (-min(s, size - s), -s))


def passed_down(block, axis):
    return lax.ppermute(block, axis, [(i + 1, i) for i in range(lax.axis_size(axis) - 1)])


def params():
    return pltpu.CompilerParams(vmem_limit_bytes=VMEM_LIMIT)


def start_rows(shifts, start, place_ref, coords_ref, rows_ref, sems):
    groups, sides = lax.axis_size("atoms"), lax.axis_size("feat")
    frames = coords_ref.shape[1] // groups
    copies = []
    for i, s in enumerate(shifts):
        there = lax.rem(place_ref[0] + s, groups)
        row = there * frames + place_ref[1] * (frames // sides) + start
        rows = pl.ds(pl.multiple_of(row, HALO), rows_ref.shape[2])
        copies.append(
            pltpu.make_async_copy(coords_ref.at[:, rows, :], rows_ref.at[i], sems.at[i])
        )
        copies[-1].start()
    return copies


def packed(cap):
    return -(-3 * cap // 128) * 128


def slot_rows(cap):
    return -(-cap // HALO) * HALO


def pick_rows(rows, chosen, out):
    _, size, width = rows.shape
    cap = chosen.shape[1]
    picked = jnp.dot(
        rows[...].reshape(3 * size, width), chosen, preferred_element_type=F32
    ).astype(BF16)
    for k in range(3):
        out[:, k * cap : (k + 1) * cap] = picked[k * size : (k + 1) * size, :]
    if out.shape[1] > 3 * cap:
        out[:, 3 * cap :] = jnp.zeros((size, out.shape[1] - 3 * cap), BF16)


def first_pick_kernel(sides, near, far, place_ref, coords_ref, ids_ref, *refs):
    pairs, refs = refs[:sides], refs[sides:]
    chosen_ref, ids_out, pairs_out, refs = refs[0], refs[1], refs[2 : 2 + sides], refs[2 + sides :]
    near_out, later_out, out, rows_ref, sems = refs
    width, cap = chosen_ref.shape
    size = rows_ref.shape[2]
    first = start_rows([far], 0, place_ref, coords_ref, rows_ref, sems.at[0])
    others = start_rows(near + [0], 0, place_ref, coords_ref, near_out, sems.at[1])
    others += start_rows([far] + near + [0], size, place_ref, coords_ref, later_out, sems.at[2])
    ids_out[...] = ids_ref[...]
    for block, copy in zip(pairs, pairs_out):
        copy[...] = block[...]
    rank, _ = ranked(pairs, place_ref[0] * width, width, upto(width))
    lanes = lax.broadcasted_iota(jnp.int32, (width, 128), 1)
    for l in range(0, cap, 128):
        some = min(128, cap - l)
        here = (rank == (lanes + l).astype(F32)).astype(F32).astype(BF16)
        chosen_ref[:, l : l + some] = here[:, :some]
    first[0].wait()
    pick_rows(rows_ref.at[0], chosen_ref[...], out)
    for copy in others:
        copy.wait()


def first_pick(coords, ids, pairs, cap, place, sizes, near, far):
    width = coords.shape[2]
    size, later = sizes
    vmem = pl.BlockSpec(memory_space=pltpu.VMEM)
    outs = pl.pallas_call(
        functools.partial(first_pick_kernel, len(pairs), near, far),
        in_specs=[
            pl.BlockSpec(memory_space=pltpu.SMEM),
            pl.BlockSpec(memory_space=pltpu.HBM),
        ]
        + [vmem] * (len(pairs) + 1),
        out_specs=[vmem] * (5 + len(pairs)),
        out_shape=[
            jax.ShapeDtypeStruct((width, cap), BF16),
            jax.ShapeDtypeStruct(ids.shape, ids.dtype),
        ]
        + [jax.ShapeDtypeStruct(block.shape, block.dtype) for block in pairs]
        + [
            jax.ShapeDtypeStruct((len(near) + 1, 3, size, width), BF16),
            jax.ShapeDtypeStruct((len(near) + 2, 3, later, width), BF16),
            jax.ShapeDtypeStruct((size, packed(cap)), BF16),
        ],
        scratch_shapes=[
            pltpu.VMEM((1, 3, size, width), BF16),
            pltpu.SemaphoreType.DMA((3, len(near) + 2)),
        ],
        compiler_params=params(),
        cost_estimate=SMALL,
        name="first_pick",
    )(place, coords, ids, *pairs)
    last = 2 + len(pairs)
    return outs[0], outs[1], outs[2:last], outs[last], outs[last + 1], outs[last + 2]


def pick_kernel(counts, chosen_ref, after_ref, *refs):
    rows_refs, outs = refs[: len(counts)], list(refs[len(counts) :])
    for rows_ref, count in zip(rows_refs, counts):
        for i in range(count):
            pick_rows(rows_ref.at[i], chosen_ref[...], outs.pop(0))


def pick(rows, chosen, after):
    cap = chosen.shape[1]
    counts = [some.shape[0] for some in rows]
    vmem = pl.BlockSpec(memory_space=pltpu.VMEM)
    return pl.pallas_call(
        functools.partial(pick_kernel, counts),
        in_specs=[vmem, pl.BlockSpec(memory_space=pl.ANY)] + [vmem] * len(rows),
        out_specs=[vmem] * sum(counts),
        out_shape=[
            jax.ShapeDtypeStruct((some.shape[2], packed(cap)), BF16)
            for some in rows
            for _ in range(some.shape[0])
        ],
        compiler_params=params(),
        cost_estimate=SMALL,
        name="pick",
    )(chosen, after, *rows)


def coded(value, step):
    first = jnp.round(value / step)
    second = jnp.round((value - first * step) * (FINE / step))
    return [first, second]


def decoded(first, second, step):
    return first * step + second * (step / FINE)


def decoded_piece(codes, rows):
    size = codes.shape[0] - HALO
    ends = codes[size:, :].astype(jnp.int32).astype(F32)
    middle = decoded(ends[0:1], ends[1:2], MEAN_STEP)
    reach = decoded(ends[2:3], ends[3:4], MEAN_STEP)
    return middle + codes[0:rows, :].astype(jnp.int32).astype(F32) * (reach * (1.0 / CODE))


def distance_kernel(cap, *refs):
    blocks, (signs_ref, after_ref, out, codes_out, joined) = refs[:-5], refs[-5:]
    size = blocks[0].shape[0]
    slots = signs_ref.shape[0] // len(blocks)
    for s, block in enumerate(blocks):
        for k in range(3):
            rows = slice(k * size, (k + 1) * size)
            joined[rows, s * slots : s * slots + cap] = block[:, k * cap : (k + 1) * cap]
        if slots > cap:
            joined[:, s * slots + cap : (s + 1) * slots] = jnp.zeros((3 * size, slots - cap), BF16)
    delta = jnp.dot(joined[...], signs_ref[...], preferred_element_type=F32)
    square = delta * delta
    total = square[:size] + square[size : 2 * size] + square[2 * size :]
    value = jnp.sqrt(total + 0.01)
    out[...] = value
    least, most = jnp.min(value, 0, keepdims=True), jnp.max(value, 0, keepdims=True)
    ends = coded(0.5 * (most + least), MEAN_STEP) + coded(0.5 * (most - least), MEAN_STEP)
    middle = decoded(ends[0], ends[1], MEAN_STEP)
    reach = decoded(ends[2], ends[3], MEAN_STEP)
    ratio = (value - middle) * (CODE / jnp.maximum(reach, REACH))
    ratio = jnp.round(jnp.clip(ratio, -32767.0, 32767.0))
    codes_out[0:size, :] = ratio.astype(jnp.int32).astype(jnp.int16)
    ends = jnp.concatenate(ends + [jnp.zeros((HALO - 4, out.shape[1]), F32)], 0)
    codes_out[size:, :] = ends.astype(jnp.int32).astype(jnp.int16)


def distances(blocks, signs, after, cap):
    size = blocks[0].shape[0]
    vmem = pl.BlockSpec(memory_space=pltpu.VMEM)
    return pl.pallas_call(
        functools.partial(distance_kernel, cap),
        in_specs=[vmem] * (len(blocks) + 1) + [pl.BlockSpec(memory_space=pl.ANY)],
        out_specs=[vmem] * 2,
        out_shape=[
            jax.ShapeDtypeStruct((size, signs.shape[1]), F32),
            jax.ShapeDtypeStruct((size + HALO, signs.shape[1]), jnp.int16),
        ],
        scratch_shapes=[pltpu.VMEM((3 * size, signs.shape[0]), BF16)],
        compiler_params=params(),
        cost_estimate=LARGE,
        name="distances",
    )(*blocks, signs, after)


def split_in_two(value):
    high = value.astype(BF16)
    return high, (value - high.astype(F32)).astype(BF16)


def product(left, right):
    left_high, left_low = split_in_two(left)
    right_high, right_low = split_in_two(right)
    left_high, left_low = left_high.T, left_low.T
    total = jnp.dot(left_high, right_high, preferred_element_type=F32)
    total += jnp.dot(left_high, right_low, preferred_element_type=F32)
    return total + jnp.dot(left_low, right_high, preferred_element_type=F32)


def row_sum(value):
    return jnp.sum(value, 0, keepdims=True)


def side_columns(side, sides, cols, write):
    for s in range(sides):

        @pl.when(side == s)
        def _():
            write(slice(s * cols, (s + 1) * cols))


def early_kernel(chunks, sides, place_ref, *refs):
    pieces = refs[:chunks]
    valid_ref, out, own_out, shift_out, sums_out, tail_out, every = refs[chunks:]
    frames = every.shape[0]
    cols = own_out.shape[1]
    row = 0
    for piece in pieces:
        every[row : row + piece.shape[0], :] = piece[...]
        row += piece.shape[0]
    side = place_ref[1]
    valid = valid_ref[pl.ds(pl.multiple_of(side * frames, HALO), frames), :]
    count = jnp.maximum(jnp.sum(valid), 1.0)
    shift = row_sum(valid * every[...]) / count
    shift_out[...] = shift
    every[...] = every[...] - shift
    tail_out[...] = every[frames - HALO : frames, :]

    def keep_own(part):
        own_out[...] = every[:, part]

    side_columns(side, sides, cols, keep_own)
    now = every[...]
    own = own_out[...]
    weighed = valid * now
    later = own[LAG:frames, :]
    weighed_later = valid[: frames - LAG] * later
    sums_out[0:1, :] = row_sum(weighed)
    sums_out[1:2, :] = row_sum(weighed * now)
    sums_out[2:3, 0:cols] = row_sum(weighed_later)
    sums_out[3:4, 0:cols] = row_sum(weighed_later * later)
    weighed_later = jnp.concatenate([weighed_later, jnp.zeros((LAG, cols), F32)], 0)
    out[...] = product(now, jnp.concatenate([valid * own, weighed_later], 1))


def early_moments(pieces, valid, place, sides):
    frames, feats = sum(piece.shape[0] for piece in pieces), pieces[0].shape[1]
    cols = feats // sides
    vmem = pl.BlockSpec(memory_space=pltpu.VMEM)
    return pl.pallas_call(
        functools.partial(early_kernel, len(pieces), sides),
        in_specs=[pl.BlockSpec(memory_space=pltpu.SMEM)] + [vmem] * (len(pieces) + 1),
        out_specs=[vmem] * 5,
        out_shape=[
            jax.ShapeDtypeStruct((feats, 2 * cols), F32),
            jax.ShapeDtypeStruct((frames, cols), F32),
            jax.ShapeDtypeStruct((1, feats), F32),
            jax.ShapeDtypeStruct((4, feats), F32),
            jax.ShapeDtypeStruct((HALO, feats), F32),
        ],
        scratch_shapes=[pltpu.VMEM((frames, feats), F32)],
        compiler_params=params(),
        cost_estimate=SMALL,
        name="early_moments",
    )(place, *pieces, valid)


def add_blocks(place_ref, shifts, groups, before_ref, left_refs, right_refs, outs):
    reps = len(outs)
    rows = before_ref.shape[0] // (groups * reps)
    left_high, left_low = left_refs
    right_high, right_low = right_refs[0][...], right_refs[1][...]
    for r in reversed(range(reps)):
        rep = lax.rem(place_ref[2] + r, reps)
        for i, s in enumerate(shifts):
            there = lax.rem(place_ref[0] + s, groups)
            at = pl.ds(pl.multiple_of((there * reps + rep) * rows, rows), rows)
            part = before_ref[at, :]
            part += jnp.dot(left_high[at, :], right_high, preferred_element_type=F32)
            part += jnp.dot(left_high[at, :], right_low, preferred_element_type=F32)
            part += jnp.dot(left_low[at, :], right_high, preferred_element_type=F32)
            outs[r][i * rows : (i + 1) * rows, :] = part


def late_kernel(sizes, sides, groups, reps, shifts, place_ref, *refs):
    chunks = len(sizes)
    codes = refs[: chunks * (sides - 1)]
    refs = refs[chunks * (sides - 1) :]
    before_ref, shift_ref, sums_ref, tail_ref, own_ref, halo_ref, valid_ref = refs[:7]
    outs = refs[7 : 7 + reps]
    own_out, left_high, left_low, right_high, right_low, left, right, own = refs[7 + reps :]
    here, cols = own_ref.shape
    frames, feats = here * sides, shift_ref.shape[1]
    side = place_ref[1]
    shift = shift_ref[...]
    bases = [pl.multiple_of(lax.rem(side + sides - s, sides) * here, HALO) for s in range(sides)]
    left[0:HALO, :] = tail_ref[...]
    row = HALO
    for s in range(1, sides):
        for j, size in enumerate(sizes):
            left[row : row + size, :] = decoded_piece(codes[j * (sides - 1) + s - 1], size) - shift
            row += size
    own[pl.ds(bases[0], here), :] = own_ref[...]

    def keep_own(part):
        own[frames:, :] = halo_ref[...] - shift[:, part]
        for s in range(1, sides):
            rows = slice(HALO + (s - 1) * here, HALO + s * here)
            own[pl.ds(bases[s], here), :] = left[rows, part]

    side_columns(side, sides, cols, keep_own)
    own_out[...] = own[0:frames, :]
    valid_all = valid_ref[...]
    total = jnp.sum(valid_all)
    count = jnp.maximum(total, 1.0)
    sums, squares = sums_ref[0:1, :], sums_ref[1:2, :]
    sums_next, squares_next = sums_ref[2:3, 0:cols], sums_ref[3:4, 0:cols]
    end = bases[0] + here - HALO
    later = own[pl.ds(pl.multiple_of(end, HALO), 2 * HALO), :][LAG : LAG + HALO]
    crossing = lax.broadcasted_iota(jnp.int32, (HALO, 1), 0) >= HALO - LAG
    valid = valid_ref[pl.ds(pl.multiple_of(end, HALO), HALO), :]
    weighed_later = jnp.where(crossing, valid * later, 0.0)
    sums_next += row_sum(weighed_later)
    squares_next += row_sum(weighed_later * later)
    right[0:HALO, 0:cols] = jnp.zeros((HALO, cols), F32)
    right[0:HALO, cols : 2 * cols] = weighed_later
    for s in range(1, sides):
        rows = slice(HALO + (s - 1) * here, HALO + s * here)
        valid = valid_ref[pl.ds(bases[s], here), :]
        weighed = valid * left[rows, :]
        sums += row_sum(weighed)
        squares += row_sum(weighed * left[rows, :])
        around = own[pl.ds(bases[s], here + HALO), :]
        right[rows, 0:cols] = valid * around[0:here]
        later = around[LAG : LAG + here]
        weighed_later = valid * later
        right[rows, cols : 2 * cols] = weighed_later
        sums_next += row_sum(weighed_later)
        squares_next += row_sum(weighed_later * later)
    own_sums = jnp.zeros((1, cols), F32)
    own_shift = jnp.zeros((1, cols), F32)
    for s in range(sides):
        mine = (side == s).astype(F32)
        own_sums += mine * sums[:, s * cols : (s + 1) * cols]
        own_shift += mine * shift[:, s * cols : (s + 1) * cols]
    first = lax.broadcasted_iota(jnp.int32, (HALO, 1), 0) == 0
    last = left.shape[0] - HALO
    left[last:, :] = jnp.where(first, sums, 0.0)
    right[last:, 0:cols] = jnp.where(first, -own_sums / count, 0.0)
    right[last:, cols : 2 * cols] = jnp.where(first, -sums_next / count, 0.0)
    high, low = split_in_two(left[...])
    left_high[...] = high.T
    left_low[...] = low.T
    right_high[...], right_low[...] = split_in_two(right[...])
    add_blocks(
        place_ref, shifts, groups, before_ref, (left_high, left_low), (right_high, right_low), outs
    )
    fold = feats // (2 * cols)
    mean, square = shift + sums / count, squares - sums * sums / count
    for out in outs:
        end = out.shape[0] - 8
        for f in range(fold):
            part = slice(2 * cols * f, 2 * cols * (f + 1))
            out[end + f : end + f + 1, :] = mean[:, part]
            out[end + fold + f : end + fold + f + 1, :] = square[:, part]
        end += 2 * fold
        out[end : end + 1, 0:cols] = own_shift + sums_next / count
        out[end : end + 1, cols : 2 * cols] = squares_next - sums_next * sums_next / count
        out[end + 1 : end + 2, :] = jnp.zeros((1, 2 * cols), F32) + total
        spare = out.shape[0] - end - 2
        if spare:
            out[end + 2 :, :] = jnp.zeros((spare, 2 * cols), F32)


def late_moments(codes, before, shift, sums, tail, own, halo, valid, place, sides, groups, reps, shifts):
    sizes = tuple(chunk[0].shape[0] - HALO for chunk in codes)
    codes = [code for chunk in codes for code in chunk]
    here, cols = own.shape
    feats = shift.shape[1]
    depth = here * (sides - 1) + 2 * HALO
    rows = feats // (groups * reps)
    vmem = pl.BlockSpec(memory_space=pltpu.VMEM)
    outs = pl.pallas_call(
        functools.partial(late_kernel, sizes, sides, groups, reps, shifts),
        in_specs=[pl.BlockSpec(memory_space=pltpu.SMEM)] + [vmem] * (len(codes) + 7),
        out_specs=[vmem] * (reps + 5),
        out_shape=[jax.ShapeDtypeStruct((len(shifts) * rows + 8, 2 * cols), F32)] * reps
        + [
            jax.ShapeDtypeStruct((here * sides, cols), F32),
            jax.ShapeDtypeStruct((feats, depth), BF16),
            jax.ShapeDtypeStruct((feats, depth), BF16),
            jax.ShapeDtypeStruct((depth, 2 * cols), BF16),
            jax.ShapeDtypeStruct((depth, 2 * cols), BF16),
        ],
        scratch_shapes=[
            pltpu.VMEM((depth, feats), F32),
            pltpu.VMEM((depth, 2 * cols), F32),
            pltpu.VMEM((here * sides + HALO, cols), F32),
        ],
        compiler_params=params(),
        cost_estimate=SMALL,
        name="late_moments",
    )(place, *codes, before, shift, sums, tail, own, halo, valid)
    return outs[:reps], outs[reps], outs[reps + 1 :]


def rest_kernel(groups, shifts, place_ref, before_ref, left_high, left_low, right_high, right_low, *outs):
    add_blocks(
        place_ref, shifts, groups, before_ref, (left_high, left_low), (right_high, right_low), outs
    )


def rest_moments(before, factors, place, groups, reps, shifts):
    rows = before.shape[0] // (groups * reps)
    vmem = pl.BlockSpec(memory_space=pltpu.VMEM)
    return pl.pallas_call(
        functools.partial(rest_kernel, groups, shifts),
        in_specs=[pl.BlockSpec(memory_space=pltpu.SMEM)] + [vmem] * 5,
        out_specs=[vmem] * reps,
        out_shape=[jax.ShapeDtypeStruct((len(shifts) * rows, before.shape[1]), F32)] * reps,
        compiler_params=params(),
        cost_estimate=SMALL,
        name="rest_moments",
    )(place, before, *factors)


def rolled(value, first):
    rows, width = value.shape
    wide = jnp.broadcast_to(value, (8, width)) if rows == 1 else value
    return pltpu.roll(wide, lax.rem(width - first, width), 1)[:rows]


def as_column(row):
    return jnp.broadcast_to(row, (8, row.shape[1])).T[:, 0:1]


def code_block(place_ref, groups, reps, s, i, parts, norms, out):
    width = parts[0].shape[1]
    cols = width // 2
    feats = norms.shape[1]
    rows = feats // (groups * reps)
    at = slice(i * rows, (i + 1) * rows)
    total = parts[0][at, :]
    for part in parts[1:]:
        total += part[at, :]
    if s == 0:
        out[...] = total
        return
    there = lax.rem(place_ref[0] + s, groups)
    first = (there * reps + place_ref[2]) * rows
    inverse_cols = jnp.concatenate(
        [rolled(norms[0:1, :], place_ref[1] * cols)[:, :cols], norms[1:2, :cols]], 1
    )
    ratio = total * as_column(rolled(norms[0:1, :], first)[:, :rows]) * inverse_cols
    root = jnp.sqrt(jnp.minimum(jnp.abs(ratio), 1.001)) * CODE
    root = jnp.where(ratio < 0.0, -root, root)
    out[0:rows, :] = jnp.round(root).astype(jnp.int32).astype(jnp.int16)


def first_share_kernel(groups, shifts, place_ref, *refs):
    count = len(shifts)
    parts, outs, codes_out, norms_out = refs[: -count - 2], refs[-count - 2 : -2], refs[-2], refs[-1]
    reps, width = len(parts), parts[0].shape[1]
    cols, feats = width // 2, norms_out.shape[1]
    fold = feats // width
    end = parts[0].shape[0] - 8
    square = jnp.zeros((1, feats), F32)
    square_next = jnp.zeros((1, cols), F32)
    codes = []
    for part in parts:
        own = part[end : end + 8, :]
        squares = [own[fold + f : fold + f + 1] for f in range(fold)]
        final = own[2 * fold : 2 * fold + 1]
        square += jnp.concatenate(squares, 1)
        square_next += final[:, cols:]
        for f in range(fold):
            codes += coded(own[f : f + 1], MEAN_STEP)
        for line in squares:
            codes += coded(jnp.sqrt(jnp.maximum(line, 0.0)), ROOT_STEP)
        pair = coded(final[:, :cols], MEAN_STEP)
        pair_next = coded(jnp.sqrt(jnp.maximum(final[:, cols:], 0.0)), ROOT_STEP)
        codes += [jnp.concatenate(both, 1) for both in zip(pair, pair_next)]
        codes.append(own[2 * fold + 1 : 2 * fold + 2])
    spare = codes_out.shape[0] - len(codes)
    if spare:
        codes.append(jnp.zeros((spare, width), F32))
    codes = jnp.concatenate(codes, 0).astype(jnp.int32).astype(jnp.int16)
    codes_out[...] = codes
    norms_out[...] = jnp.zeros(norms_out.shape, F32)
    norms_out[0:1, :] = lax.rsqrt(jnp.maximum(square, TINY))
    norms_out[1:2, :cols] = lax.rsqrt(jnp.maximum(square_next, TINY))
    for i, (s, out) in enumerate(zip(shifts, outs)):
        code_block(place_ref, groups, reps, s, i, parts, norms_out, out)
        out[out.shape[0] - codes.shape[0] :, :] = codes


def rest_share_kernel(groups, shifts, place_ref, norms_ref, codes_ref, *refs):
    count = len(shifts)
    parts, outs = refs[:-count], refs[-count:]
    for i, (s, out) in enumerate(zip(shifts, outs)):
        code_block(place_ref, groups, len(parts), s, i, parts, norms_ref, out)
        if s:
            out[out.shape[0] - codes_ref.shape[0] :, :] = codes_ref[...]


def first_share(parts, place, groups, shifts, feats):
    width, reps = parts[0].shape[1], len(parts)
    rows = feats // (groups * reps)
    lines = -(-reps * (4 * (feats // width) + 3) // 16) * 16
    vmem = pl.BlockSpec(memory_space=pltpu.VMEM)
    outs = pl.pallas_call(
        functools.partial(first_share_kernel, groups, shifts),
        in_specs=[pl.BlockSpec(memory_space=pltpu.SMEM)] + [vmem] * reps,
        out_specs=[vmem] * (len(shifts) + 2),
        out_shape=[jax.ShapeDtypeStruct((rows + lines, width), jnp.int16)] * len(shifts)
        + [
            jax.ShapeDtypeStruct((lines, width), jnp.int16),
            jax.ShapeDtypeStruct((8, feats), F32),
        ],
        compiler_params=params(),
        cost_estimate=SMALL,
        name="first_share",
    )(place, *parts)
    return outs[:-2], outs[-2], outs[-1]


def rest_share(parts, norms, codes, place, groups, shifts):
    width = parts[0].shape[1]
    rows = parts[0].shape[0] // len(shifts)
    coded_shape = jax.ShapeDtypeStruct((rows + codes.shape[0], width), jnp.int16)
    vmem = pl.BlockSpec(memory_space=pltpu.VMEM)
    return pl.pallas_call(
        functools.partial(rest_share_kernel, groups, shifts),
        in_specs=[pl.BlockSpec(memory_space=pltpu.SMEM)] + [vmem] * (len(parts) + 2),
        out_specs=[vmem] * len(shifts),
        out_shape=[coded_shape if s else jax.ShapeDtypeStruct((rows, width), F32) for s in shifts],
        compiler_params=params(),
        cost_estimate=SMALL,
        name="rest_share",
    )(place, norms, codes, *parts)


def finish_kernel(reps, place_ref, kept_ref, codes_ref, *refs):
    blocks = refs[:-5]
    shift_ref, own_ref, inst_out, lag_out, projections_out = refs[-5:]
    rows, cols = inst_out.shape
    feats = shift_ref.shape[1]
    width = 2 * cols
    fold = feats // width
    count = jnp.zeros((1, 1), F32)
    mean = jnp.zeros((1, feats), F32)
    mean_next = jnp.zeros((1, cols), F32)
    stats = []
    for block in (codes_ref,) + tuple(blocks):
        start = 0 if block is codes_ref else rows
        codes = block[start:, :].astype(jnp.int32).astype(F32)
        at = 0
        for r in range(reps):
            lines = [codes[at + i : at + i + 1] for i in range(4 * fold + 3)]
            at += 4 * fold + 3
            pairs = [(lines[2 * i], lines[2 * i + 1]) for i in range(2 * fold + 1)]
            means = [decoded(*pair, MEAN_STEP) for pair in pairs[:fold]]
            roots = [decoded(*pair, ROOT_STEP) for pair in pairs[fold : 2 * fold]]
            one, two = pairs[2 * fold]
            roots_next = decoded(one[:, cols:], two[:, cols:], ROOT_STEP)
            here = [
                jnp.concatenate(means, 1),
                jnp.concatenate([root * root for root in roots], 1),
                decoded(one[:, :cols], two[:, :cols], MEAN_STEP),
                roots_next * roots_next,
                lines[-1][:, 0:1],
            ]
            stats.append(here)
            count += here[4]
            mean += here[4] * here[0]
            mean_next += here[4] * here[2]
    mean, mean_next = mean / count, mean_next / count
    spread = jnp.zeros((1, feats), F32)
    spread_next = jnp.zeros((1, cols), F32)
    away, away_next = [], []
    for here in stats:
        away.append(here[0] - mean)
        away_next.append(here[2] - mean_next)
        spread += here[1] + here[4] * away[-1] * away[-1]
        spread_next += here[3] + here[4] * away_next[-1] * away_next[-1]
    numbers = jnp.concatenate([here[4] for here in stats], 0)
    scale = 1.0 / jnp.sqrt(spread / count + 1e-05)
    scale_next = 1.0 / jnp.sqrt(spread_next / count + 1e-05)
    away = jnp.concatenate(away, 0)

    first_row = (place_ref[0] * reps + place_ref[2]) * rows
    first_col = place_ref[1] * cols
    right = numbers * jnp.concatenate(
        [rolled(away, first_col)[:, :cols], jnp.concatenate(away_next, 0)], 1
    )
    moment = kept_ref[...] + jnp.dot(
        rolled(away, first_row)[:, :rows].T,
        right,
        precision=lax.Precision.HIGHEST,
        preferred_element_type=F32,
    )
    for g, block in enumerate(blocks):
        here = stats[(g + 1) * reps : (g + 2) * reps]
        root = jnp.sqrt(sum(one[1] for one in here))
        root_next = jnp.sqrt(sum(one[3] for one in here))
        root_rows = as_column(rolled(root, first_row)[:, :rows])
        root_cols = jnp.concatenate([rolled(root, first_col)[:, :cols], root_next], 1)
        code = block[0:rows, :].astype(jnp.int32).astype(F32) * (1.0 / CODE)
        moment += code * jnp.abs(code) * root_rows * root_cols
    scale_cols = rolled(scale, first_col)[:, :cols]
    moment = moment / count * as_column(rolled(scale, first_row)[:, :rows])
    inst_out[...] = moment[:, 0:cols] * scale_cols
    lag_out[...] = moment[:, cols : 2 * cols] * scale_next
    offset = rolled(shift_ref[...] - mean, first_col)[:, :cols]
    projections_out[...] = (own_ref[...] + offset) * scale_cols


def finish(kept, codes, blocks, shift, own, place, reps):
    rows = kept.shape[0]
    frames, cols = own.shape
    vmem = pl.BlockSpec(memory_space=pltpu.VMEM)
    return pl.pallas_call(
        functools.partial(finish_kernel, reps),
        in_specs=[pl.BlockSpec(memory_space=pltpu.SMEM)] + [vmem] * (len(blocks) + 4),
        out_specs=[vmem] * 3,
        out_shape=[
            jax.ShapeDtypeStruct((rows, cols), F32),
            jax.ShapeDtypeStruct((rows, cols), F32),
            jax.ShapeDtypeStruct((frames, cols), F32),
        ],
        compiler_params=params(),
        cost_estimate=SMALL,
        name="finish",
    )(place, kept, codes, *blocks, shift, own)


def upto(width):
    rows = lax.broadcasted_iota(jnp.int32, (width, width), 0)
    lanes = lax.broadcasted_iota(jnp.int32, (width, width), 1)
    return (lanes <= rows).astype(F32).astype(BF16)


def ranked(pairs, first, width, below):
    atoms = lax.broadcasted_iota(jnp.int32, (width, 128), 0) + first
    hit = jnp.zeros((width, 128), F32)
    for block in pairs:
        for r in range(2):
            for l in range(0, block.shape[1], 128):
                hit = jnp.where(block[r : r + 1, l : l + 128] == atoms, 1.0, hit)
    used = jnp.broadcast_to(jnp.max(hit, axis=1, keepdims=True), (width, 128))
    order = jnp.dot(below, used.astype(BF16), preferred_element_type=F32)
    return jnp.where(used > 0.0, order - 1.0, -1.0), order[width - 1 : width, :]


def signs_kernel(groups, width, slot_count, place_ref, after_ref, *refs):
    pairs, (signs_out, most_out) = refs[:-2], refs[-2:]
    sides = len(pairs)
    below = upto(width)
    number = lax.broadcasted_iota(jnp.int32, (width, 128), 0) + 1
    high = (number // 8).astype(F32).astype(BF16)
    low = (number % 8).astype(F32).astype(BF16)
    slots = lax.broadcasted_iota(jnp.int32, (slot_count, width), 0).astype(F32)
    most = jnp.zeros((1, 128), F32)
    for s in range(groups):
        first = lax.rem(place_ref[0] + groups - s, groups) * width
        rank, count = ranked(pairs, first, width, below)
        most = jnp.maximum(most, count)
        chosen = (rank.T[0:1, :] == slots).astype(F32).astype(BF16)
        listed = 8.0 * jnp.dot(chosen, high, preferred_element_type=F32)
        listed += jnp.dot(chosen, low, preferred_element_type=F32)
        listed = listed.astype(jnp.int32) - 1
        listed = jnp.where(listed < 0, -1, listed + first)
        for b, block in enumerate(pairs):
            cols = block.shape[1]
            there = lax.rem(place_ref[1] + sides - b, sides) * cols
            for l in range(0, cols, 128):
                one = (block[0:1, l : l + 128] == listed).astype(F32)
                two = (block[1:2, l : l + 128] == listed).astype(F32)
                at = pl.ds(pl.multiple_of(there + l, 128), 128)
                rows = slice(s * slot_count, (s + 1) * slot_count)
                signs_out[rows, at] = (one - two).astype(BF16)
    most_out[...] = most


def pair_signs(pairs, after, place, groups, width, cap):
    feats = len(pairs) * pairs[0].shape[1]
    vmem = pl.BlockSpec(memory_space=pltpu.VMEM)
    return pl.pallas_call(
        functools.partial(signs_kernel, groups, width, slot_rows(cap)),
        in_specs=[pl.BlockSpec(memory_space=pltpu.SMEM), pl.BlockSpec(memory_space=pl.ANY)]
        + [vmem] * len(pairs),
        out_specs=[vmem] * 2,
        out_shape=[
            jax.ShapeDtypeStruct((groups * slot_rows(cap), feats), BF16),
            jax.ShapeDtypeStruct((1, 128), F32),
        ],
        compiler_params=params(),
        cost_estimate=LARGE,
        name="pair_signs",
    )(place, after, *pairs)


def chunk_sizes(frames):
    last = frames // 8 * 3
    return frames - last, last


def with_cap(cap, coords, pairs, traj_ids, place):
    groups, sides = lax.axis_size("atoms"), lax.axis_size("feat")
    atom_index, feat_index = place[0], place[1]
    width = coords.shape[2]
    frames = coords.shape[1] // groups
    cols = pairs[0].shape[1]
    feats = cols * sides
    sizes = chunk_sizes(frames // sides)

    far, near = shifts_of("atoms")[0], shifts_of("atoms")[1:]
    chosen, traj_ids, pairs, rows, later, block = first_pick(
        coords, traj_ids, pairs, cap, place, sizes, near, far
    )
    order = near + [0]
    picked = {far: block} | dict(zip(order, pick([rows], chosen, block)))
    signs, most_used = pair_signs(pairs, block, place, groups, width, cap)
    order = [far] + order
    arrived = []
    for j in range(2):
        if j:
            picked = dict(zip(order, pick([later], chosen, most_used)))
        moved = {s: rotated(picked[s], "atoms", s) if s else picked[s] for s in order}
        arrived.append([moved[s] for s in range(groups)])

    ids = jnp.concatenate([traj_ids[0], jnp.full((LAG,), -1, jnp.int32)])
    offset = atom_index * frames
    ids_now = lax.dynamic_slice_in_dim(ids, offset, frames)
    ids_later = lax.dynamic_slice_in_dim(ids, offset + LAG, frames)
    valid = (ids_now == ids_later).astype(F32)[:, None]

    own_pieces, codes, after = [], [], arrived[-1][0]
    for j, blocks in enumerate(arrived):
        block, code = distances(blocks, signs, after, cap)
        after = block
        own_pieces.append(block)
        codes.append([rotated(code, "feat", s) for s in range(1, sides)])
        if j == 0:
            opening = passed_down(block[:HALO], "atoms")
    halo = lax.dynamic_slice_in_dim(opening, feat_index * cols, cols, 1)
    opening = opening + 0.0 * own_pieces[-1][:HALO]
    for s in range(1, sides):
        there = lax.rem(feat_index + s, sides)
        sent = rotated(lax.dynamic_slice_in_dim(opening, there * cols, cols, 1), "feat", s)
        halo = jnp.where(feat_index == s, sent, halo)

    reps = lax.axis_size("rep")
    shifts = shifts_of("atoms") + [0]
    shifts = tuple(shifts[: groups // 2]), tuple(shifts[groups // 2 :])
    before, own, shift, sums, tail = early_moments(own_pieces, valid, place, sides)
    parts, own, factors = late_moments(
        codes, before, shift, sums, tail, own, halo, valid, place, sides, groups, reps, shifts[0]
    )
    parts = [parts[0]] + [rotated(parts[r], "rep", r) for r in range(1, reps)]
    rest = rest_moments(before, factors, place, groups, reps, shifts[1])
    rest = [rest[0]] + [rotated(rest[r], "rep", r) for r in range(1, reps)]
    blocks, stats, norms = first_share(parts, place, groups, shifts[0], feats)
    blocks = [rotated(block, "atoms", s) for s, block in zip(shifts[0], blocks)]
    *more, kept = rest_share(rest, norms, stats, place, groups, shifts[1])
    blocks += [rotated(block, "atoms", s) for s, block in zip(shifts[1], more)]
    corr_inst, corr_lag, projections = finish(kept, stats, blocks, shift, own, place, reps)
    return (corr_inst, corr_lag, projections[None]), most_used[0, 0]


def shards(atom_coords, atom_pairs, traj_ids):
    place = [lax.axis_index(axis) for axis in ("atoms", "feat", "rep")]
    place = jnp.stack(place).astype(jnp.int32)
    width = atom_coords.shape[3]
    coords = jnp.transpose(atom_coords[0], (1, 0, 2))
    pairs = [atom_pairs] + [rotated(atom_pairs, "feat", s) for s in range(1, lax.axis_size("feat"))]
    cap = min(width, packed(width * 5 // 9) // 3)
    outs, most_used = with_cap(cap, coords, pairs, traj_ids, place)

    def again(carry):
        same = [block + (carry[0] - 1) for block in pairs]
        return carry[0] - 1, with_cap(width, coords, same, traj_ids, place)[0]

    overflow = (most_used > cap).astype(jnp.int32)
    return lax.while_loop(lambda carry: carry[0] > 0, again, (overflow, outs))[1]


def solution(mesh):
    placed = (P(("grp", "rep"), None, None, "atoms"), P(None, "feat"), P(("grp", "rep"), None))
    return jax.shard_map(
        shards,
        mesh=mesh,
        in_specs=placed,
        out_specs=(
            P(("grp", "atoms", "rep"), "feat"),
            P(("grp", "atoms", "rep"), "feat"),
            P(("grp", "rep"), "atoms", "feat"),
        ),
        check_vma=False,
    )
```
